128 devices in a mesh: seq: 16 (over z_hi, x, core), batch: 8 (over y, z_lo).
Axes of the slice: x: 4, y: 4, z: 4 (z_hi: 2, z_lo: 2; z = z_hi * 2 + z_lo), core: 2. Of those that a mesh axis runs over, the one named last changes fastest.
Arguments:
- tokens: bfloat16 [8, 2048, 1024], P('batch', 'seq')
- doc_lengths: int32 [8, 4], P('batch'), may hold values from 0 to 2048, as said below
- block_order: int32 [32], replicated, may hold values from 0 to 31, each once
- small_params: bfloat16 [13312], P(('seq', 'batch'))
- w_qkv: bfloat16 [1024, 3072], P(('seq', 'batch')), may hold values from -0.1875 to 0.1875
- w_out: bfloat16 [1024, 1024], P(('seq', 'batch')), may hold values from -0.75 to 0.75
- w_up: bfloat16 [1024, 4096], P(('seq', 'batch')), may hold values from -0.1875 to 0.1875
- w_down: bfloat16 [4096, 1024], P(('seq', 'batch')), may hold values from -0.09375 to 0.09375
- cotangent: bfloat16 [8, 2048, 1024], P('batch', 'seq'), may hold values from -6 to 6
Outputs:
- mixed: bfloat16 [8, 2048, 1024], P('batch', 'seq')
- grad_tokens: bfloat16 [8, 2048, 1024], P('batch', 'seq')
- grad_small: float32 [13312], P(('seq', 'batch'))
- grad_qkv: float32 [1024, 3072], P(('seq', 'batch'))
- grad_out: float32 [1024, 1024], P(('seq', 'batch'))
- grad_up: float32 [1024, 4096], P(('seq', 'batch'))
- grad_down: float32 [4096, 1024], P(('seq', 'batch'))
The draws below stay inside these ranges and needn't reach their ends.
Inputs may be any that keep to these rules, and one draw needn't show every extreme that they name: `doc_lengths`: each row's entries sum to 2048; some rows are one document (2048 then zeros), the others are cut into 4 documents, some possibly empty.
All inputs are finite; a program needn't handle non-finite values.
Results may differ from the reference program's by a relative error of at most 0.018.
Values may be sent and summed in bfloat16 or wider, within the bound.
A program may use at most 192 MiB of HBM per device.

```python
import math
import jax
import jax.numpy as jnp
from jax import lax

D = 1024
H = 16
HD = 64
ROT = 16
FF = 4096
DOCS = 4
BLK = 64
ROW_TOK = 2048
ROWS = 8
SMALL = 13312
N_SEQ = 16


def draw_tokens(key, part):
    key = jax.random.fold_in(key, 11)
    row_key, column_key, base_key = jax.random.split(key, 3)
    row_scale = jnp.exp(jax.random.uniform(row_key, (ROWS, ROW_TOK, 1), jnp.float32, math.log(0.3), math.log(3.0)))
    column_scale = jnp.exp(jax.random.uniform(column_key, (1, 1, D), jnp.float32, math.log(0.5), math.log(2.0)))
    base = jax.random.truncated_normal(base_key, -4.0, 4.0, (ROWS, ROW_TOK, D), jnp.float32)
    return (base * row_scale * column_scale).astype(jnp.bfloat16)


def draw_small_params(key, part):
    key = jax.random.fold_in(key, 23)
    gain_key, shift_key = jax.random.split(key, 2)
    index = jnp.arange(SMALL)
    gains = 1.0 + 0.3 * jax.random.uniform(gain_key, (SMALL,), jnp.float32, -1.0, 1.0)
    shifts = 0.3 * jax.random.truncated_normal(shift_key, -3.0, 3.0, (SMALL,), jnp.float32)
    is_gain = (index < D) | (index >= 2 * D) & (index < 3 * D)
    return jnp.where(is_gain, gains, shifts).astype(jnp.bfloat16)


def draw_doc_lengths(key, part):
    key = jax.random.fold_in(key, 37)
    cut_key, pick_key = jax.random.split(key, 2)
    cuts = jnp.sort(jax.random.randint(cut_key, (ROWS, DOCS - 1), 1, ROW_TOK), axis=1).astype(jnp.int32)
    edges = jnp.concatenate([jnp.zeros((ROWS, 1), jnp.int32), cuts, jnp.full((ROWS, 1), ROW_TOK, jnp.int32)], axis=1)
    ragged = edges[:, 1:] - edges[:, :-1]
    single = jnp.where(jnp.arange(DOCS) == 0, ROW_TOK, 0).astype(jnp.int32)
    order = jax.random.permutation(pick_key, ROWS)
    return jnp.where((order < ROWS // 2)[:, None], single[None, :], ragged).astype(jnp.int32)


def shard_levels(stream_key, extent, cuts, least, high):
    factor_of, own = 1.0, jax.random.fold_in(stream_key, 6)
    for dim, blocks in cuts:
        steps = jnp.exp(jax.random.uniform(jax.random.fold_in(own, dim), (blocks,), jnp.float32, least / len(cuts), high / len(cuts)))
        factor_of = factor_of * jnp.repeat(steps, extent[dim] // blocks).reshape([-1 if axis == dim else 1 for axis in range(len(extent))])
    return factor_of


def gaussian(stream_key, dims, scale, reach, cuts=(), held_as=jnp.bfloat16):
    level = shard_levels(stream_key, dims, cuts, -0.22, 0.18) if cuts else 1.0
    values = jax.random.normal(stream_key, dims, jnp.float32) * scale * level
    return jnp.minimum(jnp.maximum(values, -reach), reach).astype(held_as)


def setup_inputs(seed: int = 0) -> dict:
    streams_of = jax.random.split(jax.random.key(seed), 10)
    return {
        "tokens": draw_tokens(jax.random.fold_in(streams_of[9], 71), 0),
        "doc_lengths": draw_doc_lengths(jax.random.fold_in(streams_of[9], 71), 0),
        "block_order": jax.random.permutation(streams_of[2], 2 * N_SEQ).astype(jnp.int32),
        "small_params": draw_small_params(jax.random.fold_in(streams_of[9], 71), 0),
        "w_qkv": gaussian(streams_of[4], (D, 3 * D), D ** -0.5, 0.1875, ((0, 128),)),
        "w_out": gaussian(streams_of[5], (D, D), (D // 16) ** -0.5, 0.75, ((0, 128),)),
        "w_up": gaussian(streams_of[6], (D, FF), D ** -0.5, 0.1875, ((0, 128),)),
        "w_down": gaussian(streams_of[7], (FF, D), FF ** -0.5, 0.09375, ((0, 128),)),
        "cotangent": gaussian(streams_of[8], (ROWS, ROW_TOK, D), 1.0, 6.0, ((0, 8), (1, 16))),
    }


@jax.custom_vjp
def low(v):
    return lax.optimization_barrier(v.astype(jnp.bfloat16)).astype(jnp.float32)

@jax.custom_vjp
def low_back(v):
    return v

def low_keep(v):
    return (low(v), None)

def low_pass(kept, grad):
    return (grad,)

def back_keep(v):
    return (v, None)

def back_low(kept, grad):
    return (low(grad),)
low.defvjp(low_keep, low_pass)
low_back.defvjp(back_keep, back_low)
EPS = 1e-05
NEG = -1e+30
PRECISE = lax.Precision.HIGHEST

def positions_of(block_order, lengths, count, block):
    index = jnp.arange(count, dtype=jnp.int32)
    slots = jnp.arange(block_order.shape[0], dtype=jnp.int32)
    placed = lax.optimization_barrier(jnp.sum(jnp.where((index // block)[:, None] == slots[None, :], block_order[None, :], 0), axis=1)).astype(jnp.int32)
    where = placed * block + index % block
    ends = jnp.cumsum(lengths).astype(jnp.int32)
    docs = lax.optimization_barrier(jnp.sum((where[:, None] >= ends[None, :]).astype(jnp.int32), axis=1)).astype(jnp.int32)
    firsts = ends - lengths
    number = jnp.arange(lengths.shape[0], dtype=jnp.int32)
    begin = lax.optimization_barrier(jnp.sum(jnp.where(docs[:, None] == number[None, :], firsts[None, :], 0), axis=1)).astype(jnp.int32)
    return (where, docs, where - begin)

def rotate(part, relpos):
    half = ROT // 2
    rates = 10000.0 ** (-2.0 * jnp.arange(half, dtype=jnp.float32) / ROT)
    angle = relpos.astype(jnp.float32)[:, None] * rates[None, :]
    cosine = jnp.cos(angle)[:, None, :]
    sine = jnp.sin(angle)[:, None, :]
    front = part[..., :half]
    latter = part[..., half:ROT]
    return jnp.concatenate([front * cosine - latter * sine, latter * cosine + front * sine, part[..., ROT:]], axis=-1)

def layer_norm(values, gain, shift):
    centred = values - lax.optimization_barrier(jnp.mean(values, axis=-1, keepdims=True))
    spread = lax.optimization_barrier(jnp.mean(centred * centred, axis=-1, keepdims=True))
    return centred * lax.rsqrt(spread + EPS) * gain + shift

def split_small(small):
    return (small[:D], small[D:2 * D], small[2 * D:3 * D], small[3 * D:4 * D], small[4 * D:7 * D], small[7 * D:8 * D], small[8 * D:8 * D + FF], small[8 * D + FF:])

def row_forward(inputs, small, w_qkv, w_out, w_up, w_down, where, docs, relpos):
    count = inputs.shape[0]
    gain_one, shift_one, gain_two, shift_two, bias_qkv, bias_out, bias_up, bias_down = split_small(small)
    first = low(layer_norm(inputs, gain_one, shift_one))
    second = low(layer_norm(inputs, gain_two, shift_two))
    projected = low_back(jnp.dot(first, w_qkv, precision=PRECISE) + bias_qkv).reshape(count, 3, H, HD)
    query = low(rotate(projected[:, 0], relpos))
    keyrot = low(rotate(projected[:, 1], relpos))
    value = low(projected[:, 2])
    span = min(512, count)

    def attend(item):
        block_query, block_where, block_docs = item
        raw = jnp.einsum('qhd,khd->hqk', block_query, keyrot, precision=PRECISE) * HD ** (-0.5)
        allowed = (block_docs[:, None] == docs[None, :]) & (where[None, :] <= block_where[:, None])
        scores = jnp.where(allowed[None], low_back(raw), NEG)
        probs = jax.nn.softmax(scores, axis=-1)
        return jnp.einsum('hqk,khd->qhd', low(probs), value, precision=PRECISE)
    blocks = count // span
    heads = lax.map(jax.checkpoint(attend), (query.reshape(blocks, span, H, HD), where.reshape(blocks, span), docs.reshape(blocks, span)))
    attn_heads = low(low_back(heads.reshape(count, D)))
    attention = jnp.dot(attn_heads, w_out, precision=PRECISE) + bias_out
    hidden = low_back(jnp.dot(second, w_up, precision=PRECISE) + bias_up)
    active = low(jax.nn.gelu(hidden, approximate=False))
    feed = jnp.dot(active, w_down, precision=PRECISE) + bias_down
    return inputs + attention + feed

def reference(tokens, doc_lengths, block_order, small_params, w_qkv, w_out, w_up, w_down, cotangent):
    count = tokens.shape[1]

    def forward(inputs, small, matrix_qkv, matrix_out, matrix_up, matrix_down):

        def one(item):
            row, lengths = item
            where, docs, relpos = positions_of(block_order, lengths, count, BLK)
            return row_forward(row, small, matrix_qkv, matrix_out, matrix_up, matrix_down, where, docs, relpos)
        return lax.map(jax.checkpoint(one), (inputs, doc_lengths))
    floats = tuple((a.astype(jnp.float32) for a in (tokens, small_params, w_qkv, w_out, w_up, w_down)))
    result, pull = jax.vjp(forward, *floats)
    grads = pull(cotangent.astype(jnp.float32))
    return (result.astype(jnp.bfloat16), grads[0].astype(jnp.bfloat16), grads[1], grads[2], grads[3], grads[4], grads[5])
```

```python
import jax
import jax.numpy as jnp
import numpy as np
from jax import lax
from jax.experimental import pallas as pl
from jax.experimental.pallas import tpu as pltpu
from jax.sharding import PartitionSpec as P

HD = 64
ROT = 16
EPS = 1e-05
NEG = -1e30
MESH = pl.DeviceIdType.MESH
BF = jnp.bfloat16
F32 = jnp.float32

SEQ = 16
BATCH = 8
TOK = 128
ROW = SEQ * TOK
D = 1024
HID = 256
PER = 104
QB = 256


def dot(a, b):
    return lax.dot_general(a, b, (((1,), (0,)), ((), ())), preferred_element_type=F32)


def dot_nt(a, b):
    return lax.dot_general(a, b, (((1,), (1,)), ((), ())), preferred_element_type=F32)


def dot_tn(a, b):
    return lax.dot_general(a, b, (((0,), (0,)), ((), ())), preferred_element_type=F32)


def iota(shape, dim):
    return lax.broadcasted_iota(jnp.int32, shape, dim)


def slot(z, x, c):
    return z * 8 + x * 2 + c


def rows_at(index, count):
    return pl.ds(pl.multiple_of(index * count, count), count)


def kernel(
    x_ref, dy_ref, ws_ref, wd_ref, wo_ref, rate_ref, inv_ref, order_ref, len_ref,
    mixed_ref, gtok_ref, gw_ref, gd_ref, go_ref, small_ref,
    nrm, dya, wst, wbuf, wd2, wo2, wob, rawq, rawu, cols, wcat, brow, drow,
    prj, act, dge, tabc, tabs, qs, ks, vs, qst, dos, dost, osort, ost,
    sbuf, dcat, dkt, dvt, dsort, stat,
    part_m, part_d, sib_m, half_m, full_m, zed_m, sib_d, half_d, full_d, zed_d,
    gdacc, gtu, gdsend, gosend, gdrecv, gorecv, gsend, grecv, gsum, gfin, smv, smr, smt, sma,
    ag_ss, ag_rs, rs_ss, rs_rs, sq_ss, sq_rs, bt_ss, bt_rs,
):
    s = lax.axis_index("seq")
    b = lax.axis_index("batch")
    z, x, c = s // 8, lax.rem(s // 2, 4), lax.rem(s, 2)
    xr, xl, xo = lax.rem(x + 1, 4), lax.rem(x + 3, 4), lax.rem(x + 2, 4)
    zo, co = 1 - z, 1 - c
    right, left = (slot(z, xr, c), b), (slot(z, xl, c), b)
    across, sibling = (slot(zo, x, c), b), (slot(z, x, co), b)

    def remote(src, dst, send, recv, device):
        return pltpu.make_async_remote_copy(
            src_ref=src, dst_ref=dst, send_sem=send, recv_sem=recv,
            device_id=device, device_id_type=MESH,
        )

    barrier = pltpu.get_barrier_semaphore()

    @pl.loop(1, SEQ)
    def _(j):
        pl.semaphore_signal(barrier, inc=1, device_id=(lax.rem(s + j, SEQ), b), device_id_type=MESH)

    @pl.loop(1, BATCH)
    def _(j):
        pl.semaphore_signal(barrier, inc=1, device_id=(s, lax.rem(b + j, BATCH)), device_id_type=MESH)

    def normed_of():
        inputs = x_ref[...].astype(F32)
        centred = inputs - jnp.mean(inputs, axis=-1, keepdims=True)
        inverse = lax.rsqrt(jnp.mean(centred * centred, axis=-1, keepdims=True) + EPS)
        return inputs, centred * inverse, inverse

    nrm[rows_at(s, TOK), :] = normed_of()[1].astype(BF)
    dya[rows_at(s, TOK), :] = dy_ref[...]
    wst[rows_at(s, 16), :] = ws_ref[rows_at(s, 16), :]
    wd2[rows_at(b, 32), :] = wd_ref[...]
    wo2[rows_at(b, 8), :] = wo_ref[...]
    pl.semaphore_wait(barrier, SEQ - 1 + BATCH - 1)

    def seq_copy(j, k, src, dst):
        return remote(src, dst, sq_ss.at[k, j], sq_rs.at[k, j], (lax.rem(s + j, SEQ), b))

    def batch_copy(j, k, src, dst):
        return remote(src, dst, bt_ss.at[k, j], bt_rs.at[k, j], (s, lax.rem(b + j, BATCH)))

    @pl.loop(1, SEQ)
    def _(j):
        peer = lax.rem(s + j, SEQ)
        seq_copy(j, 0, ws_ref.at[rows_at(peer, 16)], wst.at[rows_at(s, 16)]).start()

    class Gather:
        def __init__(self, buf, k):
            self.buf, self.k = buf, k

        def copy(self, e, index, device, low=0, count=TOK):
            at = self.buf.at[pl.ds(pl.multiple_of(index * TOK + low, 64), count)]
            return remote(at, at, ag_ss.at[self.k, e], ag_rs.at[self.k, e], device)

        def sends(self):
            own, far = s, slot(zo, x, c)
            return {
                0: (own, right, 0, TOK), 1: (own, left, 0, TOK),
                2: (own, across, 0, TOK), 3: (own, sibling, 0, TOK),
                4: (far, right, 0, TOK), 5: (far, left, 0, TOK), 6: (far, sibling, 0, TOK),
                7: (slot(z, xl, c), right, 0, 64), 8: (slot(z, xr, c), left, 64, 64),
                9: (slot(z, xl, c), sibling, 0, TOK), 10: (slot(z, xr, c), sibling, 0, TOK),
                11: (slot(zo, xl, c), right, 0, 64), 12: (slot(zo, xr, c), left, 64, 64),
                13: (slot(zo, xl, c), sibling, 0, TOK), 14: (slot(zo, xr, c), sibling, 0, TOK),
                15: (slot(z, xo, c), sibling, 0, TOK), 16: (slot(zo, xo, c), sibling, 0, TOK),
            }

        def receives(self):
            return {
                0: (slot(z, xl, c), 0, TOK), 1: (slot(z, xr, c), 0, TOK),
                2: (slot(zo, x, c), 0, TOK), 3: (slot(z, x, co), 0, TOK),
                4: (slot(zo, xl, c), 0, TOK), 5: (slot(zo, xr, c), 0, TOK), 6: (slot(zo, x, co), 0, TOK),
                7: (slot(z, xo, c), 0, 64), 8: (slot(z, xo, c), 64, 64),
                9: (slot(z, xl, co), 0, TOK), 10: (slot(z, xr, co), 0, TOK),
                11: (slot(zo, xo, c), 0, 64), 12: (slot(zo, xo, c), 64, 64),
                13: (slot(zo, xl, co), 0, TOK), 14: (slot(zo, xr, co), 0, TOK),
                15: (slot(z, xo, co), 0, TOK), 16: (slot(zo, xo, co), 0, TOK),
            }

        def start(self, *events):
            for e in events:
                index, device, low, count = self.sends()[e]
                self.copy(e, index, device, low, count).start()

        def wait(self, *events):
            for e in events:
                index, low, count = self.receives()[e]
                self.copy(e, index, right, low, count).wait_recv()

        def step(self, n):
            if n == 0:
                self.start(0, 1, 2, 3)
            elif n == 1:
                self.wait(2)
                self.start(4, 5, 6)
                self.wait(0)
                self.start(7, 9)
                self.wait(1)
                self.start(8, 10)
            elif n == 2:
                self.wait(4)
                self.start(11, 13)
                self.wait(5)
                self.start(12, 14)
            elif n == 3:
                self.wait(7, 8)
                self.start(15)
                self.wait(11, 12)
                self.start(16)
            else:
                self.wait(3, 6, 9, 10, 13, 14, 15, 16)

        def drain(self):
            for e, (index, device, low, count) in self.sends().items():
                self.copy(e, index, device, low, count).wait_send()

    normed_gather = Gather(nrm, 0)
    dy_gather = Gather(dya, 1)
    normed_gather.step(0)

    @pl.loop(1, SEQ)
    def _(j):
        giver = lax.rem(s + SEQ - j, SEQ)
        seq_copy(j, 0, wst.at[rows_at(giver, 16)], wst.at[rows_at(giver, 16)]).wait_recv()

    wbuf[rows_at(b, 256), :] = wst[...]

    @pl.loop(1, BATCH)
    def _(j):
        batch_copy(j, 0, wst, wbuf.at[rows_at(b, 256)]).start()
        batch_copy(j, 1, wd_ref, wd2.at[rows_at(b, 32)]).start()
        batch_copy(j, 2, wo_ref, wo2.at[rows_at(b, 8)]).start()

    normed_gather.step(1)

    ends = [len_ref[0]]
    for k in range(1, 4):
        ends.append(ends[-1] + len_ref[k])

    def begin_of(where):
        begin = jnp.zeros_like(where)
        for end in ends:
            begin = jnp.maximum(begin, jnp.where(where >= end, end, 0))
        return begin

    @pl.loop(0, 8)
    def _(i):
        where = i * QB + iota((QB, 128), 0)
        angle = (where - begin_of(where)).astype(F32) * rate_ref[0:1, :]
        lane = lax.rem(iota((QB, 128), 1), 64)
        sine = jnp.sin(angle)
        tabc[rows_at(i, QB), :] = jnp.where(lane < ROT, jnp.cos(angle), 1.0)
        sine = jnp.where(lane < ROT // 2, -sine, sine)
        tabs[rows_at(i, QB), :] = jnp.where(lane < ROT, sine, 0.0)

    def partner_of(part):
        lane = lax.rem(iota(part.shape, 1), 64)
        return jnp.where(lane < ROT // 2, pltpu.roll(part, 120, 1), pltpu.roll(part, 8, 1))

    normed_gather.step(2)
    normed_gather.step(3)
    dy_gather.step(0)

    @pl.loop(1, BATCH)
    def _(j):
        giver = lax.rem(b + BATCH - j, BATCH)
        batch_copy(j, 0, wbuf.at[rows_at(giver, 256)], wbuf.at[rows_at(giver, 256)]).wait_recv()
        batch_copy(j, 1, wd2.at[rows_at(giver, 32)], wd2.at[rows_at(giver, 32)]).wait_recv()
        batch_copy(j, 2, wo2.at[rows_at(giver, 8)], wo2.at[rows_at(giver, 8)]).wait_recv()

    wob[...] = wo2[...].astype(BF)

    @pl.loop(0, SEQ)
    def _(i):
        for j in range(BATCH):
            block = wbuf[pl.ds(pl.multiple_of(j * 256 + i * 16, 16), 16), :].astype(F32)
            at = pl.ds(pl.multiple_of(i * 64 + j * 8, 8), 8)
            rawu[at, :] = block[0:8, :]
            rawq[at, :] = block[8:16, :]

    def small_window(start, count):
        return rawq[start : start + count, 128:256].astype(BF)

    for k, start in enumerate((0, 72, 152, 232)):
        number = k * D + iota((D, 128), 0)
        line = (iota((D, 128), 1) + start) * 13
        hot = ((line <= number) & (number < line + 13)).astype(F32).astype(BF)
        found = dot(hot, small_window(start, 128))
        place = number - 13 * jnp.floor((number.astype(F32) + 0.5) * (1.0 / 13.0)).astype(jnp.int32)
        found = jnp.where(iota((D, 128), 1) == place + 64, found, 0.0)
        cols[:, k : k + 1] = jnp.sum(found, axis=1, keepdims=True)

    def small_row(number, start, count):
        width = number.shape[1]
        line = (iota((count, width), 0) + start) * 13
        hot = ((line <= number) & (number < line + 13)).astype(F32).astype(BF)
        found = dot_tn(small_window(start, count), hot)
        place = number - 13 * jnp.floor((number.astype(F32) + 0.5) * (1.0 / 13.0)).astype(jnp.int32)
        found = jnp.where(iota((128, width), 0) == place + 64, found, 0.0)
        return jnp.sum(found, axis=0, keepdims=True)

    lane = iota((1, 256), 1)
    number_q = 4 * D + (lane // 64) * D + s * 64 + lax.rem(lane, 64)
    bias_q = small_row(jnp.where(lane < 192, number_q, -100), 312, 448)
    bias_u = small_row(8 * D + s * HID + lane, 624, 328)
    keep = iota((128, 256), 1) < 192
    row_q, row_u = bias_q, bias_u
    for i in range(8):
        at = slice(i * 128, i * 128 + 128)
        wq = jnp.where(keep, rawq[at, :], 0.0)
        wu = rawu[at, :]
        wcat[at, 0:256] = (wq * cols[at, 0:1]).astype(BF)
        wcat[at, 256:512] = (wu * cols[at, 2:3]).astype(BF)
        row_q = row_q + jnp.sum(wq * cols[at, 1:2], axis=0, keepdims=True)
        row_u = row_u + jnp.sum(wu * cols[at, 3:4], axis=0, keepdims=True)
    brow[:, 0:256] = row_q
    brow[:, 256:512] = row_u
    wide = iota((1, D), 1)
    drow[...] = small_row(7 * D + wide, 544, 128) + small_row(12 * D + wide, 896, 128)

    normed_gather.step(4)

    @pl.loop(0, 8)
    def _(i):
        at = rows_at(i, QB)
        out = dot(nrm[at, :], wcat[...]) + brow[...]
        prj[pl.ds(i * 4, 4)] = out[:, 0:256].reshape(4, 64, 256)
        hidden = out[:, 256:512]
        share = 0.5 * (1.0 + lax.erf(hidden * (2.0**-0.5)))
        act[at, :] = (hidden * share).astype(BF)
        dge[at, :] = share + hidden * jnp.exp(-0.5 * hidden * hidden) * ((2.0 * np.pi) ** -0.5)

    dy_gather.step(1)

    @pl.loop(0, 32)
    def _(i):
        at = rows_at(i, 64)
        come = prj[inv_ref[i]]
        part = come[:, 0:128]
        part = part * tabc[at, :] + partner_of(part) * tabs[at, :]
        qs[at, :] = (part[:, 0:64].astype(BF) * 0.125).astype(BF)
        ks[at, :] = pltpu.roll(part, 64, 1)[:, 0:64].astype(BF)
        vs[at, :] = come[:, 128:192].astype(BF)

    def masked(scores, i, j):
        q_at = i * QB + iota((QB, 1), 0)
        k_at = j * QB + iota((1, QB), 1)
        allowed = (k_at >= begin_of(q_at)) & (k_at <= q_at)
        return jnp.where(allowed, scores, NEG)

    @pl.loop(0, 8)
    def _(i):
        at = rows_at(i, QB)

        def scores_step(j, top):
            scores = masked(dot_nt(qs[at, :], ks[rows_at(j, QB), :]), i, j)
            sbuf[:, rows_at(j, QB)] = scores
            return jnp.maximum(top, jnp.maximum(scores[:, 0:128], scores[:, 128:256]))

        top = lax.fori_loop(0, i + 1, scores_step, jnp.full((QB, 128), NEG, F32))
        top = jnp.max(top, axis=1, keepdims=True)

        def value_step(j, carry):
            total, summed = carry
            expos = jnp.exp(sbuf[:, rows_at(j, QB)] - top)
            summed = summed + dot(expos.astype(BF), vs[rows_at(j, QB), :])
            return total + (expos[:, 0:128] + expos[:, 128:256]), summed

        total, summed = lax.fori_loop(
            0, i + 1, value_step, (jnp.zeros((QB, 128), F32), jnp.zeros((QB, HD), F32))
        )
        total = jnp.sum(total, axis=1, keepdims=True)
        out = summed / total
        osort[pl.ds(i * 4, 4)] = out.reshape(4, 64, HD)
        stat[at, 64:65] = top + jnp.log(total)

    dy_gather.step(2)

    @pl.loop(0, 32)
    def _(j):
        ost[rows_at(j, 64), :] = osort[order_ref[j]].astype(BF)

    class Scatter:
        def __init__(self, part, sib, half, full, zed, k):
            self.part, self.sib, self.half, self.full, self.zed, self.k = part, sib, half, full, zed, k
            self.order = [(zo, xo), (zo, xr), (zo, xl), (zo, x), (z, xo), (z, xr), (z, xl), (z, x)]

        def copy(self, e, src, dst, device):
            return remote(src, dst, rs_ss.at[self.k, e], rs_rs.at[self.k, e], device)

        def chip(self, n):
            return pl.ds(pl.multiple_of((self.order[n][0] * 4 + self.order[n][1]) * 256, 256), 256)

        def at(self, n, core, low=0, count=TOK):
            zz, xx = self.order[n]
            return pl.ds(pl.multiple_of(slot(zz, xx, core) * TOK + low, 64), count)

        def out(self, e):
            part, sib, half, full = self.part, self.sib, self.half, self.full
            if e < 8:
                return part.at[self.at(e, co)], sib.at[rows_at(e, TOK)], sibling
            if e == 16:
                return part.at[self.at(3, c)], self.zed, across
            g, kind = (e - 8) // 4, (e - 8) % 4
            if kind == 0:
                return part.at[self.at(4 * g, c, 0, 64)], half.at[rows_at(2 * g, 64)], left
            if kind == 1:
                return part.at[self.at(4 * g, c, 64, 64)], half.at[rows_at(2 * g + 1, 64)], right
            if kind == 2:
                return part.at[self.at(4 * g + 1, c)], full.at[rows_at(2 * g, TOK)], right
            return part.at[self.at(4 * g + 2, c)], full.at[rows_at(2 * g + 1, TOK)], left

        def start(self, e):
            self.copy(e, *self.out(e)).start()

        def wait(self, e):
            src, dst, device = self.out(e)
            self.copy(e, dst, dst, device).wait_recv()

        def add_sibling(self, n):
            self.wait(n)
            at = self.at(n, c)
            self.part[at, :] = (
                self.part[at, :].astype(F32) + self.sib[n * TOK : n * TOK + TOK, :].astype(F32)
            ).astype(BF)

        def add_half(self, n, e, low, index):
            self.wait(e)
            at = self.at(n, c, low, 64)
            self.part[at, :] = (
                self.part[at, :].astype(F32) + self.half[index * 64 : index * 64 + 64, :].astype(F32)
            ).astype(BF)

        def full_sum(self, n, g):
            self.wait(8 + 4 * g + 2)
            self.wait(8 + 4 * g + 3)
            total = self.part[self.at(n, c), :].astype(F32)
            for index in (2 * g, 2 * g + 1):
                total = total + self.full[index * TOK : index * TOK + TOK, :].astype(F32)
            return total

        def step(self, n):
            if n == 0 or n == 3:
                g = n // 3
                self.add_sibling(4 * g)
                self.start(8 + 4 * g)
                self.start(8 + 4 * g + 1)
                self.add_sibling(4 * g + 1)
                self.add_sibling(4 * g + 2)
            elif n == 1 or n == 4:
                g = n // 4
                self.add_half(4 * g + 1, 8 + 4 * g + 1, 64, 2 * g + 1)
                self.start(8 + 4 * g + 2)
                self.add_half(4 * g + 2, 8 + 4 * g, 0, 2 * g)
                self.start(8 + 4 * g + 3)
                self.add_sibling(4 * g + 3)
            elif n == 2:
                self.part[self.at(3, c), :] = self.full_sum(3, 0).astype(BF)
                self.start(16)

        def result(self):
            total = self.full_sum(7, 1)
            self.wait(16)
            return total + self.zed[...].astype(F32)

        def drain(self):
            for e in range(17):
                self.copy(e, *self.out(e)).wait_send()

    mixed_sum = Scatter(part_m, sib_m, half_m, full_m, zed_m, 0)
    dn_sum = Scatter(part_d, sib_d, half_d, full_d, zed_d, 1)

    for n in range(8):
        at = mixed_sum.chip(n)
        part_m[at, :] = (dot(act[at, :], wd2[...]) + dot(ost[at, :], wob[...])).astype(BF)
        mixed_sum.start(n)

    dy_gather.step(3)
    mixed_sum.step(0)
    dy_gather.step(4)
    mixed_sum.step(1)

    @pl.loop(0, 8)
    def _(i):
        at = rows_at(i, QB)
        dy = dya[at, :]
        dcat[at, 256:512] = (dot_nt(dy, wd2[...]) * dge[at, :]).astype(BF)
        dost[pl.ds(i * 4, 4)] = dot_nt(dy, wob[...]).astype(BF).reshape(4, 64, HD)

    mixed_sum.step(2)
    mixed_sum.step(3)

    @pl.loop(0, 32)
    def _(i):
        dos[rows_at(i, 64), :] = dost[inv_ref[i]]

    gdacc[...] = jnp.zeros_like(gdacc)
    gtu[...] = jnp.zeros_like(gtu)

    @pl.loop(0, 4)
    def _(i):
        at = rows_at(i, 512)
        gdacc[0:256, :] += dot_tn(act[at, :], dya[at, :])
        gdacc[256:320, :] += dot_tn(ost[at, :], dya[at, :])

    gdsend[...] = gdacc[0:256, :].astype(BF)
    gosend[...] = gdacc[256:320, :]
    gdrecv[rows_at(b, 32), :] = gdsend[rows_at(b, 32), :]
    gorecv[rows_at(b, 8), :] = gosend[rows_at(b, 8), :]

    @pl.loop(1, BATCH)
    def _(j):
        peer = lax.rem(b + j, BATCH)
        batch_copy(j, 3, gdsend.at[rows_at(peer, 32)], gdrecv.at[rows_at(b, 32)]).start()
        batch_copy(j, 4, gosend.at[rows_at(peer, 8)], gorecv.at[rows_at(b, 8)]).start()

    mixed_sum.step(4)

    @pl.loop(0, 4)
    def _(i):
        at = rows_at(i, 512)
        gtu[...] += dot_tn(dcat[at, 256:512], nrm[at, :])

    mixed_ref[...] = (mixed_sum.result() + x_ref[...].astype(F32) + drow[...]).astype(BF)

    @pl.loop(0, 8)
    def _(i):
        at = rows_at(i, QB)
        stat[at, 65:66] = jnp.sum(
            dos[at, :].astype(F32) * osort[pl.ds(i * 4, 4)].reshape(QB, HD), axis=1, keepdims=True
        )
        qst[0:64, at] = qs[at, :].T
        qst[64:128, at] = dos[at, :].T

    dkt[...] = jnp.zeros_like(dkt)
    dvt[...] = jnp.zeros_like(dvt)

    @pl.loop(0, 8)
    def _(i):
        at = rows_at(i, QB)

        def step(j, dq):
            k_at = rows_at(j, QB)
            scores = masked(dot_nt(qs[at, :], ks[k_at, :]), i, j)
            probs = jnp.exp(scores - stat[at, 64:65])
            pulled = dot_nt(dos[at, :], vs[k_at, :])
            grads = (probs * (pulled - stat[at, 65:66])).astype(BF)
            dkt[:, k_at] += dot(qst[0:64, at], grads)
            dvt[:, k_at] += dot(qst[64:128, at], probs.astype(BF))
            return dq + dot(grads, ks[k_at, :])

        stat[at, 0:64] = lax.fori_loop(0, i + 1, step, jnp.zeros((QB, HD), F32)) * 0.125

    @pl.loop(0, 8)
    def _(i):
        at = rows_at(i, QB)
        both = jnp.concatenate([stat[at, 0:64], dkt[:, at].T], axis=1)
        both = both * tabc[at, :] - partner_of(both) * tabs[at, :]
        last = jnp.concatenate([dvt[:, at].T, jnp.zeros((QB, 64), F32)], axis=1)
        whole = jnp.concatenate([both, last], axis=1).astype(BF)
        dsort[pl.ds(i * 4, 4)] = whole.reshape(4, 64, 256)

    @pl.loop(0, 32)
    def _(j):
        dcat[rows_at(j, 64), 0:256] = dsort[order_ref[j]]

    for n in range(8):
        at = dn_sum.chip(n)
        part_d[at, :] = dot_nt(dcat[at, :], wcat[...]).astype(BF)
        dn_sum.start(n)
    dn_sum.step(0)

    gdacc[0:256, :] = jnp.zeros((256, D), F32)

    @pl.loop(0, 4)
    def _(i):
        at = rows_at(i, 512)
        gdacc[0:256, :] += dot_tn(dcat[at, 0:256], nrm[at, :])

    def total_step(i, total):
        return total + jnp.sum(dcat[rows_at(i, QB), :].astype(F32), axis=0, keepdims=True)

    sums = lax.fori_loop(0, 8, total_step, jnp.zeros((1, 512), F32))
    sum_q, sum_u = sums[:, 0:256], sums[:, 256:512]

    dn_sum.step(1)

    for i in range(4):
        at = slice(i * 256, i * 256 + 256)
        grad_q = gdacc[0:256, at].T
        grad_u = gtu[:, at].T
        pieces = [
            jnp.sum(grad_q * rawq[at, :], axis=1, keepdims=True),
            jnp.sum(sum_q * rawq[at, :], axis=1, keepdims=True),
            jnp.sum(grad_u * rawu[at, :], axis=1, keepdims=True),
            jnp.sum(sum_u * rawu[at, :], axis=1, keepdims=True),
        ]
        spread = jnp.zeros((256, 128), F32)
        for k in range(4):
            spread = jnp.where(iota((256, 128), 1) == k, pieces[k], spread)
        smv[:, at] = spread.T[0:8, :]
        grad_q = grad_q * cols[at, 0:1] + cols[at, 1:2] * sum_q
        grad_u = grad_u * cols[at, 2:3] + cols[at, 3:4] * sum_u
        for m in range(32):
            place = ((m % 8) * 16 + (i * 4 + m // 8)) * 16
            gsend[place : place + 16, :] = jnp.concatenate(
                [grad_u[m * 8 : m * 8 + 8, :], grad_q[m * 8 : m * 8 + 8, :]], axis=0
            ).astype(BF)

    smv[4:5, :] = jnp.sum(dy_ref[...].astype(F32), axis=0, keepdims=True)
    smv[5:6, 0:256] = sum_q
    smv[5:6, 256:512] = sum_u
    smv[5:6, 512:1024] = jnp.zeros((1, 512), F32)
    smr[rows_at(b, 8), :] = smv[...]
    grecv[rows_at(b, 256), :] = gsend[rows_at(b, 256), :]

    @pl.loop(1, BATCH)
    def _(j):
        peer = lax.rem(b + j, BATCH)
        batch_copy(j, 5, gsend.at[rows_at(peer, 256)], grecv.at[rows_at(b, 256)]).start()
        batch_copy(j, 6, smv, smr.at[rows_at(b, 8)]).start()

    dn_sum.step(2)
    dn_sum.step(3)

    @pl.loop(1, BATCH)
    def _(j):
        giver = lax.rem(b + BATCH - j, BATCH)
        batch_copy(j, 3, gdrecv.at[rows_at(giver, 32)], gdrecv.at[rows_at(giver, 32)]).wait_recv()
        batch_copy(j, 4, gorecv.at[rows_at(giver, 8)], gorecv.at[rows_at(giver, 8)]).wait_recv()

    total_d = gdrecv[0:32, :].astype(F32)
    total_o = gorecv[0:8, :]
    for k in range(1, BATCH):
        total_d = total_d + gdrecv[k * 32 : k * 32 + 32, :].astype(F32)
        total_o = total_o + gorecv[k * 8 : k * 8 + 8, :]
    gd_ref[...] = total_d
    go_ref[...] = total_o

    dn_sum.step(4)

    @pl.loop(1, BATCH)
    def _(j):
        giver = lax.rem(b + BATCH - j, BATCH)
        batch_copy(j, 5, grecv.at[rows_at(giver, 256)], grecv.at[rows_at(giver, 256)]).wait_recv()
        batch_copy(j, 6, smr.at[rows_at(giver, 8)], smr.at[rows_at(giver, 8)]).wait_recv()

    total_w = grecv[0:256, :].astype(F32)
    total_s = smr[0:8, :]
    for k in range(1, BATCH):
        total_w = total_w + grecv[k * 256 : k * 256 + 256, :].astype(F32)
        total_s = total_s + smr[k * 8 : k * 8 + 8, :]
    gsum[...] = total_w.astype(BF)
    gfin[rows_at(s, 16), :] = gsum[rows_at(s, 16), :]
    smt[...] = total_s
    sma[rows_at(s, 8), :] = total_s

    @pl.loop(1, SEQ)
    def _(j):
        peer = lax.rem(s + j, SEQ)
        seq_copy(j, 1, gsum.at[rows_at(peer, 16)], gfin.at[rows_at(s, 16)]).start()
        seq_copy(j, 2, smt, sma.at[rows_at(s, 8)]).start()

    merged = dn_sum.result()
    _, normed, inverse = normed_of()
    grad_norm = inverse * (
        merged
        - jnp.mean(merged, axis=-1, keepdims=True)
        - normed * jnp.mean(merged * normed, axis=-1, keepdims=True)
    )
    gtok_ref[...] = (dy_ref[...].astype(F32) + grad_norm).astype(BF)

    @pl.loop(1, SEQ)
    def _(j):
        giver = lax.rem(s + SEQ - j, SEQ)
        seq_copy(j, 1, gfin.at[rows_at(giver, 16)], gfin.at[rows_at(giver, 16)]).wait_recv()
        seq_copy(j, 2, sma.at[rows_at(giver, 8)], sma.at[rows_at(giver, 8)]).wait_recv()

    gw_ref[...] = gfin[...].astype(F32)
    small_ref[...] = sma[...]

    normed_gather.drain()
    dy_gather.drain()
    mixed_sum.drain()
    dn_sum.drain()

    @pl.loop(1, SEQ)
    def _(j):
        peer = lax.rem(s + j, SEQ)
        seq_copy(j, 0, ws_ref.at[rows_at(peer, 16)], wst.at[rows_at(s, 16)]).wait_send()
        seq_copy(j, 1, gsum.at[rows_at(peer, 16)], gfin.at[rows_at(s, 16)]).wait_send()
        seq_copy(j, 2, smt, sma.at[rows_at(s, 8)]).wait_send()

    @pl.loop(1, BATCH)
    def _(j):
        peer = lax.rem(b + j, BATCH)
        batch_copy(j, 0, wst, wbuf.at[rows_at(b, 256)]).wait_send()
        batch_copy(j, 1, wd_ref, wd2.at[rows_at(b, 32)]).wait_send()
        batch_copy(j, 2, wo_ref, wo2.at[rows_at(b, 8)]).wait_send()
        batch_copy(j, 3, gdsend.at[rows_at(peer, 32)], gdrecv.at[rows_at(b, 32)]).wait_send()
        batch_copy(j, 4, gosend.at[rows_at(peer, 8)], gorecv.at[rows_at(b, 8)]).wait_send()
        batch_copy(j, 5, gsend.at[rows_at(peer, 256)], grecv.at[rows_at(b, 256)]).wait_send()
        batch_copy(j, 6, smv, smr.at[rows_at(b, 8)]).wait_send()


def layer(x, dy, ws, wd, wo, rate, inv, order, lengths):
    vmem = pl.BlockSpec(memory_space=pltpu.VMEM)
    smem = pl.BlockSpec(memory_space=pltpu.SMEM)
    scratch = [
        ((ROW, D), BF), ((ROW, D), BF), ((256, 256), BF), ((2048, 256), BF),
        ((256, D), BF), ((64, D), F32), ((64, D), BF),
        ((D, 256), F32), ((D, 256), F32), ((D, 128), F32), ((D, 512), BF),
        ((1, 512), F32), ((1, D), F32),
        ((32, 64, 256), F32), ((ROW, HID), BF), ((ROW, HID), F32),
        ((ROW, 128), F32), ((ROW, 128), F32),
        ((ROW, HD), BF), ((ROW, HD), BF), ((ROW, HD), BF), ((128, ROW), BF),
        ((ROW, HD), BF), ((32, 64, HD), BF), ((32, 64, HD), F32), ((ROW, HD), BF),
        ((QB, ROW), F32), ((ROW, 512), BF), ((HD, ROW), F32), ((HD, ROW), F32),
        ((32, 64, 256), BF), ((ROW, 128), F32),
        ((ROW, D), BF), ((ROW, D), BF),
        ((8 * TOK, D), BF), ((4 * 64, D), BF), ((4 * TOK, D), BF), ((TOK, D), BF),
        ((8 * TOK, D), BF), ((4 * 64, D), BF), ((4 * TOK, D), BF), ((TOK, D), BF),
        ((320, D), F32), ((256, D), F32),
        ((256, D), BF), ((64, D), F32), ((256, D), BF), ((64, D), F32),
        ((2048, 256), BF), ((2048, 256), BF), ((256, 256), BF), ((256, 256), BF),
        ((8, D), F32), ((64, D), F32), ((8, D), F32), ((128, D), F32),
    ]
    shapes = [pltpu.VMEM(shape, dtype) for shape, dtype in scratch]
    shapes += [
        pltpu.SemaphoreType.DMA((2, 17)), pltpu.SemaphoreType.DMA((2, 17)),
        pltpu.SemaphoreType.DMA((2, 17)), pltpu.SemaphoreType.DMA((2, 17)),
        pltpu.SemaphoreType.DMA((3, SEQ)), pltpu.SemaphoreType.DMA((3, SEQ)),
        pltpu.SemaphoreType.DMA((7, BATCH)), pltpu.SemaphoreType.DMA((7, BATCH)),
    ]
    return pl.pallas_call(
        kernel,
        out_shape=(
            jax.ShapeDtypeStruct((TOK, D), BF),
            jax.ShapeDtypeStruct((TOK, D), BF),
            jax.ShapeDtypeStruct((256, 256), F32),
            jax.ShapeDtypeStruct((32, D), F32),
            jax.ShapeDtypeStruct((8, D), F32),
            jax.ShapeDtypeStruct((128, D), F32),
        ),
        in_specs=[vmem] * 6 + [smem] * 3,
        out_specs=(vmem,) * 6,
        scratch_shapes=shapes,
        compiler_params=pltpu.CompilerParams(
            collective_id=0, has_side_effects=True, vmem_limit_bytes=62 * 2**20
        ),
    )(x, dy, ws, wd, wo, rate, inv, order, lengths)


def local(tokens, doc_lengths, block_order, small_params, w_qkv, w_out, w_up, w_down, cotangent):
    place = lax.axis_index("seq") * BATCH + lax.axis_index("batch")
    up = w_up.reshape(8, SEQ, HID).transpose(1, 0, 2)
    qkv = w_qkv.reshape(8, 3, SEQ, HD).transpose(2, 0, 1, 3).reshape(SEQ, 8, 3 * HD)
    extra = jnp.pad(small_params.reshape(8, 13), ((0, 0), (0, 51)))
    extra = jnp.broadcast_to(extra[None], (SEQ, 8, 64))
    sent = jnp.concatenate([up, jnp.concatenate([qkv, extra], axis=2)], axis=1).reshape(SEQ * 16, 256)
    rates = np.float32(10000.0) ** (-2.0 * (np.arange(128) % 8).astype(np.float32) / ROT)
    rate = jnp.asarray(np.broadcast_to(rates.astype(np.float32), (8, 128)))
    index = jnp.arange(32, dtype=jnp.int32)
    inverse = jnp.sum(jnp.where(block_order[None, :] == index[:, None], index[None, :], 0), axis=1)
    mixed, grad_tokens, grad_w, grad_down, grad_out, small = layer(
        tokens[0], cotangent[0], sent, w_down, w_out.astype(F32), rate,
        inverse.astype(jnp.int32), block_order, doc_lengths[0],
    )
    grad_w = grad_w.reshape(SEQ, 2, 8, 256)
    grad_up = grad_w[:, 0].transpose(1, 0, 2).reshape(8, SEQ * HID)
    grad_qkv = grad_w[:, 1, :, : 3 * HD].reshape(SEQ, 8, 3, HD)
    grad_qkv = grad_qkv.transpose(1, 2, 0, 3).reshape(8, 3 * D)
    small = small.reshape(SEQ, 8, D)
    lines = jnp.sum(small[:, 0:5], axis=0)
    bias_qkv = small[:, 5, : 3 * HD].reshape(SEQ, 3, HD).transpose(1, 0, 2).reshape(-1)
    bias_up = small[:, 5, 256:512].reshape(-1)
    grad_small = jnp.concatenate(
        [lines[0], lines[1], lines[2], lines[3], bias_qkv, lines[4], bias_up, lines[4]]
    )
    grad_small = lax.dynamic_slice_in_dim(grad_small, place * PER, PER)
    return (mixed[None], grad_tokens[None], grad_small, grad_qkv, grad_out, grad_up, grad_down)


def solution(mesh):
    placed = (
        P("batch", "seq", None),
        P("batch", None),
        P(),
        P(("seq", "batch")),
        P(("seq", "batch"), None),
        P(("seq", "batch"), None),
        P(("seq", "batch"), None),
        P(("seq", "batch"), None),
        P("batch", "seq", None),
    )
    return jax.shard_map(
        local,
        mesh=mesh,
        in_specs=placed,
        out_specs=(
            P("batch", "seq", None),
            P("batch", "seq", None),
            P(("seq", "batch")),
            P(("seq", "batch"), None),
            P(("seq", "batch"), None),
            P(("seq", "batch"), None),
            P(("seq", "batch"), None),
        ),
        check_vma=False,
    )
```

```python
import jax
import jax.numpy as jnp
import numpy as np
from jax import lax
from jax.experimental import pallas as pl
from jax.experimental.pallas import tpu as pltpu
from jax.sharding import PartitionSpec as P

HD = 64
ROT = 16
EPS = 1e-05
NEG = -1e30
MESH = pl.DeviceIdType.MESH
BF = jnp.bfloat16
F32 = jnp.float32

SEQ = 16
BATCH = 8
TOK = 128
ROW = SEQ * TOK
D = 1024
HID = 256
PER = 104
QB = 256
AB = 512


def dot(a, b):
    return lax.dot_general(a, b, (((1,), (0,)), ((), ())), preferred_element_type=F32)


def dot_nt(a, b):
    return lax.dot_general(a, b, (((1,), (1,)), ((), ())), preferred_element_type=F32)


def dot_tn(a, b):
    return lax.dot_general(a, b, (((0,), (0,)), ((), ())), preferred_element_type=F32)


def iota(shape, dim):
    return lax.broadcasted_iota(jnp.int32, shape, dim)


def slot(z, x, c):
    return z * 8 + x * 2 + c


def rows_at(index, count):
    return pl.ds(pl.multiple_of(index * count, count), count)


def kernel(
    x_ref, dy_ref, wq_ref, wo_ref, wu_ref, wd_ref, sp_ref, order_ref, len_ref,
    mixed_ref, gtok_ref, gu_ref, gq_ref, gd_ref, go_ref, small_ref,
    nrm, dya, wsend, wst, wbuf, wd2, wos, wo2, wob, rawq, rawu, cols, wcat, brow, drow,
    prj, act, dge, tabc, tabs, qa, ka, va, kat, vat, qat, doa, doat, dost, osort, ost,
    dcat, dkt, dvt, dsort, dqs,
    part, sib_m, half_m, full_m, zed_m, sib_d, half_d, full_d, zed_d,
    gdacc, gtu, gdsend, gosend, gdrecv, gorecv,
    gusend, gurecv, gusum, gufin, gqsend, gqrecv, gqsum, gqfin,
    flat, fsend, frecv, fsum, fall,
    inv_ref, ag_ss, ag_rs, rs_ss, rs_rs, sq_ss, sq_rs, bt_ss, bt_rs,
):
    s = lax.axis_index("seq")
    b = lax.axis_index("batch")
    z, x, c = s // 8, lax.rem(s // 2, 4), lax.rem(s, 2)
    xr, xl, xo = lax.rem(x + 1, 4), lax.rem(x + 3, 4), lax.rem(x + 2, 4)
    zo, co = 1 - z, 1 - c
    right, left = (slot(z, xr, c), b), (slot(z, xl, c), b)
    across, sibling = (slot(zo, x, c), b), (slot(z, x, co), b)

    def remote(src, dst, send, recv, device):
        return pltpu.make_async_remote_copy(
            src_ref=src, dst_ref=dst, send_sem=send, recv_sem=recv,
            device_id=device, device_id_type=MESH,
        )

    barrier = pltpu.get_barrier_semaphore()

    @pl.loop(1, SEQ)
    def _(j):
        pl.semaphore_signal(barrier, inc=1, device_id=(lax.rem(s + j, SEQ), b), device_id_type=MESH)

    @pl.loop(1, BATCH)
    def _(j):
        pl.semaphore_signal(barrier, inc=1, device_id=(s, lax.rem(b + j, BATCH)), device_id_type=MESH)

    def normed_of():
        inputs = x_ref[...].astype(F32)
        centred = inputs - jnp.mean(inputs, axis=-1, keepdims=True)
        inverse = lax.rsqrt(jnp.mean(centred * centred, axis=-1, keepdims=True) + EPS)
        return inputs, centred * inverse, inverse

    nrm[rows_at(s, TOK), :] = normed_of()[1].astype(BF)
    dya[rows_at(s, TOK), :] = dy_ref[...]

    def pair(one, two):
        return jnp.where(iota((8, 128), 1) < 64, one, two)

    small = jnp.concatenate([sp_ref[...].astype(F32), jnp.zeros((1, 128 - PER), F32)], axis=1)
    extra = jnp.where(
        iota((8, 128), 0) == 0, pltpu.roll(small, 64, 1), jnp.where(iota((8, 128), 0) == 1, small, 0.0)
    )
    wide_q = wq_ref[...].astype(F32)
    wide_u = wu_ref[...].astype(F32)
    for k in range(SEQ):
        at = slice(k // 2 * 128, k // 2 * 128 + 128)
        q, kk, v = (wide_q[:, n * D : n * D + D][:, at] for n in range(3))
        turned = [pltpu.roll(part_of, 64, 1) for part_of in (q, kk, v)]
        q, kk, v = (q, turned[1], v) if k % 2 == 0 else (turned[0], kk, turned[2])
        low = jnp.concatenate([pair(q, kk), pair(v, extra)], axis=1)
        block = jnp.concatenate([wide_u[:, k * HID : k * HID + HID], low], axis=0)
        wsend[k * 16 : k * 16 + 16, :] = block.astype(BF)

    wst[rows_at(s, 16), :] = wsend[rows_at(s, 16), :]
    wos[...] = wo_ref[...].astype(F32)
    wd2[rows_at(b, 32), :] = wd_ref[...]
    wo2[rows_at(b, 8), :] = wos[...]

    @pl.loop(0, 32)
    def _(i):
        place = jnp.int32(0)
        for j in range(32):
            place = place + jnp.where(order_ref[j] == i, j, 0)
        inv_ref[i] = jnp.minimum(place, 31)

    pl.semaphore_wait(barrier, SEQ - 1 + BATCH - 1)

    def seq_copy(j, k, src, dst):
        return remote(src, dst, sq_ss.at[k, j], sq_rs.at[k, j], (lax.rem(s + j, SEQ), b))

    def batch_copy(j, k, src, dst):
        return remote(src, dst, bt_ss.at[k, j], bt_rs.at[k, j], (s, lax.rem(b + j, BATCH)))

    @pl.loop(1, SEQ)
    def _(j):
        peer = lax.rem(s + j, SEQ)
        seq_copy(j, 0, wsend.at[rows_at(peer, 16)], wst.at[rows_at(s, 16)]).start()

    class Gather:
        def __init__(self, buf, k):
            self.buf, self.k = buf, k

        def copy(self, e, index, device, low=0, count=TOK):
            at = self.buf.at[pl.ds(pl.multiple_of(index * TOK + low, 64), count)]
            return remote(at, at, ag_ss.at[self.k, e], ag_rs.at[self.k, e], device)

        def sends(self):
            own, far = s, slot(zo, x, c)
            return {
                0: (own, right, 0, TOK), 1: (own, left, 0, TOK),
                2: (own, across, 0, TOK), 3: (own, sibling, 0, TOK),
                4: (far, right, 0, TOK), 5: (far, left, 0, TOK), 6: (far, sibling, 0, TOK),
                7: (slot(z, xl, c), right, 0, 64), 8: (slot(z, xr, c), left, 64, 64),
                9: (slot(z, xl, c), sibling, 0, TOK), 10: (slot(z, xr, c), sibling, 0, TOK),
                11: (slot(zo, xl, c), right, 0, 64), 12: (slot(zo, xr, c), left, 64, 64),
                13: (slot(zo, xl, c), sibling, 0, TOK), 14: (slot(zo, xr, c), sibling, 0, TOK),
                15: (slot(z, xo, c), sibling, 0, TOK), 16: (slot(zo, xo, c), sibling, 0, TOK),
            }

        def receives(self):
            return {
                0: (slot(z, xl, c), 0, TOK), 1: (slot(z, xr, c), 0, TOK),
                2: (slot(zo, x, c), 0, TOK), 3: (slot(z, x, co), 0, TOK),
                4: (slot(zo, xl, c), 0, TOK), 5: (slot(zo, xr, c), 0, TOK), 6: (slot(zo, x, co), 0, TOK),
                7: (slot(z, xo, c), 0, 64), 8: (slot(z, xo, c), 64, 64),
                9: (slot(z, xl, co), 0, TOK), 10: (slot(z, xr, co), 0, TOK),
                11: (slot(zo, xo, c), 0, 64), 12: (slot(zo, xo, c), 64, 64),
                13: (slot(zo, xl, co), 0, TOK), 14: (slot(zo, xr, co), 0, TOK),
                15: (slot(z, xo, co), 0, TOK), 16: (slot(zo, xo, co), 0, TOK),
            }

        def start(self, *events):
            for e in events:
                index, device, low, count = self.sends()[e]
                self.copy(e, index, device, low, count).start()

        def wait(self, *events):
            for e in events:
                index, low, count = self.receives()[e]
                self.copy(e, index, right, low, count).wait_recv()

        def step(self, n):
            if n == 0:
                self.start(0, 1, 2, 3)
            elif n == 1:
                self.wait(2)
                self.start(4, 5, 6)
                self.wait(0)
                self.start(7, 9)
                self.wait(1)
                self.start(8, 10)
            elif n == 2:
                self.wait(4)
                self.start(11, 13)
                self.wait(5)
                self.start(12, 14)
            elif n == 3:
                self.wait(7, 8)
                self.start(15)
                self.wait(11, 12)
                self.start(16)
            else:
                self.wait(3, 6, 9, 10, 13, 14, 15, 16)

        def drain(self):
            for e, (index, device, low, count) in self.sends().items():
                self.copy(e, index, device, low, count).wait_send()

    normed_gather = Gather(nrm, 0)
    dy_gather = Gather(dya, 1)
    normed_gather.step(0)

    ends = [len_ref[0, 0]]
    for k in range(1, 4):
        ends.append(ends[-1] + len_ref[0, k])

    def begin_of(where):
        begin = jnp.zeros_like(where)
        for end in ends:
            begin = jnp.maximum(begin, jnp.where(where >= end, end, 0))
        return begin

    def doc_of(where):
        doc = jnp.zeros_like(where)
        for end in ends:
            doc = doc + jnp.where(where >= end, 1, 0)
        return doc

    def partner_of(part):
        lane = lax.rem(iota(part.shape, 1), 64)
        return jnp.where(lane < ROT // 2, pltpu.roll(part, 120, 1), pltpu.roll(part, 8, 1))

    rate = jnp.zeros((1, 128), F32)
    for k in range(ROT // 2):
        value = float(np.float32(10000.0) ** np.float32(-2.0 * k / ROT))
        rate = jnp.where(lax.rem(iota((1, 128), 1), 8) == k, value, rate)

    @pl.loop(1, SEQ)
    def _(j):
        giver = lax.rem(s + SEQ - j, SEQ)
        seq_copy(j, 0, wst.at[rows_at(giver, 16)], wst.at[rows_at(giver, 16)]).wait_recv()

    wbuf[rows_at(b, 256), :] = wst[...]

    @pl.loop(1, BATCH)
    def _(j):
        batch_copy(j, 0, wst, wbuf.at[rows_at(b, 256)]).start()

    @pl.loop(0, 8)
    def _(i):
        where = i * QB + iota((QB, 128), 0)
        angle = (where - begin_of(where)).astype(F32) * rate
        lane = lax.rem(iota((QB, 128), 1), 64)
        sine = jnp.sin(angle)
        tabc[rows_at(i, QB), :] = jnp.where(lane < ROT, jnp.cos(angle), 1.0)
        sine = jnp.where(lane < ROT // 2, -sine, sine)
        tabs[rows_at(i, QB), :] = jnp.where(lane < ROT, sine, 0.0)

    normed_gather.step(1)

    @pl.loop(1, BATCH)
    def _(j):
        batch_copy(j, 1, wd_ref, wd2.at[rows_at(b, 32)]).start()
        batch_copy(j, 2, wos, wo2.at[rows_at(b, 8)]).start()

    normed_gather.step(2)
    normed_gather.step(3)
    dy_gather.step(0)

    @pl.loop(1, BATCH)
    def _(j):
        giver = lax.rem(b + BATCH - j, BATCH)
        batch_copy(j, 0, wbuf.at[rows_at(giver, 256)], wbuf.at[rows_at(giver, 256)]).wait_recv()

    @pl.loop(0, SEQ)
    def _(i):
        for j in range(BATCH):
            block = wbuf[pl.ds(pl.multiple_of(j * 256 + i * 16, 16), 16), :].astype(F32)
            at = pl.ds(pl.multiple_of(i * 64 + j * 8, 8), 8)
            rawu[at, :] = block[0:8, :]
            rawq[at, :] = block[8:16, :]

    def small_window(start, count):
        return rawq[start : start + count, 128:256].astype(BF)

    def hot_of(line, number):
        low = (line // 8) * PER + lax.rem(line, 8) * 64
        high = jnp.where(lax.rem(line, 8) == 0, low + 64, low + PER - 64)
        high = jnp.where(lax.rem(line, 8) < 2, high, low)
        return ((low <= number) & (number < high)).astype(F32).astype(BF)

    def place_of(number):
        owner = jnp.floor((number.astype(F32) + 0.5) * (1.0 / PER)).astype(jnp.int32)
        place = number - PER * owner
        return 64 + jnp.where(place >= 64, place - 64, place)

    for k, start in enumerate((0, 72, 152, 232)):
        number = k * D + iota((D, 128), 0)
        found = dot(hot_of(iota((1, 128), 1) + start, number), small_window(start, 128))
        found = jnp.where(iota((D, 128), 1) == place_of(number), found, 0.0)
        cols[:, k : k + 1] = jnp.sum(found, axis=1, keepdims=True)

    def small_row(number, start, count):
        found = dot_tn(small_window(start, count), hot_of(iota((count, 1), 0) + start, number))
        found = jnp.where(iota((128, number.shape[1]), 0) == place_of(number), found, 0.0)
        return jnp.sum(found, axis=0, keepdims=True)

    lane = iota((1, 256), 1)
    number_q = 4 * D + (lane // 64) * D + s * 64 + lax.rem(lane, 64)
    bias_q = small_row(jnp.where(lane < 192, number_q, -1000), 312, 240)
    bias_u = small_row(8 * D + s * HID + lane, 624, 328)
    keep = iota((128, 256), 1) < 192
    row_q, row_u = bias_q, bias_u
    for i in range(8):
        at = slice(i * 128, i * 128 + 128)
        wq = jnp.where(keep, rawq[at, :], 0.0)
        wu = rawu[at, :]
        wcat[at, 0:256] = (wq * cols[at, 0:1]).astype(BF)
        wcat[at, 256:512] = (wu * cols[at, 2:3]).astype(BF)
        row_q = row_q + jnp.sum(wq * cols[at, 1:2], axis=0, keepdims=True)
        row_u = row_u + jnp.sum(wu * cols[at, 3:4], axis=0, keepdims=True)
    brow[:, 0:256] = row_q
    brow[:, 256:512] = row_u
    wide = iota((1, D), 1)
    drow[...] = small_row(7 * D + wide, 544, 128) + small_row(12 * D + wide, 896, 128)

    normed_gather.step(4)

    @pl.loop(0, 8)
    def _(i):
        at = rows_at(i, QB)
        out = dot(nrm[at, :], wcat[:, 0:256]) + brow[:, 0:256]
        prj[pl.ds(i * 4, 4)] = out.reshape(4, 64, 256)

    dy_gather.step(1)

    def pieces_of(value):
        high = value.astype(BF).astype(F32)
        mid = (value - high).astype(BF).astype(F32)
        return high, mid, value - high - mid

    def with_lanes(base, first, values):
        lane = iota(base.shape, 1)
        for k, value in enumerate(values):
            base = jnp.where(lane == first + k, value, base)
        return base

    @pl.loop(0, 32)
    def _(i):
        at = rows_at(i, 64)
        come = prj[inv_ref[i]]
        both = come[:, 0:128]
        both = both * tabc[at, :] + partner_of(both) * tabs[at, :]
        lane = iota((64, 128), 1)
        own = doc_of(i * 64 + iota((64, 1), 0)) == lane - 64
        front = lane < 64
        qa[at, :] = jnp.where(front, both * 0.125, jnp.where(own | (lane >= 68), 0.0, NEG)).astype(BF)
        tail = jnp.where(lane < 68, own.astype(F32), (lane < 71).astype(F32))
        ka[at, :] = jnp.where(front, pltpu.roll(both, 64, 1), tail).astype(BF)
        va[at, :] = jnp.where(front, come[:, 128:256], (lane < 67).astype(F32)).astype(BF)

    @pl.loop(0, 8)
    def _(i):
        at = rows_at(i, QB)
        kat[:, at] = ka[at, :].T
        vat[:, at] = va[at, :].T
        qat[:, at] = qa[at, :].T[0:64, :]

    lower = iota((AB, AB), 1) <= iota((AB, AB), 0)

    @pl.loop(0, ROW // AB)
    def _(i):
        at = rows_at(i, AB)

        def step(j, carry, masked):
            top, total = carry
            k_at = rows_at(j, AB)
            scores = dot(qa[at, :], kat[:, k_at])
            if masked:
                scores = jnp.where(lower, scores, NEG)
            peak = jnp.maximum(top, jnp.max(scores, axis=1, keepdims=True))
            expos = jnp.exp(scores - peak).astype(BF)
            return peak, total * jnp.exp(top - peak) + dot(expos, va[k_at, :])

        start = (jnp.full((AB, 1), NEG, F32), jnp.zeros((AB, 128), F32))
        carry = lax.fori_loop(0, i, lambda j, carry: step(j, carry, False), start)
        top, total = step(i, carry, True)
        norm = total[:, 64:65]
        osort[pl.ds(i * (AB // 64), AB // 64)] = (total / norm)[:, 0:64].reshape(AB // 64, 64, HD)
        qa[at, :] = with_lanes(qa[at, :].astype(F32), 68, pieces_of(-(top + jnp.log(norm)))).astype(BF)

    dy_gather.step(2)

    @pl.loop(0, 8)
    def _(i):
        at = rows_at(i, QB)
        hidden = dot(nrm[at, :], wcat[:, 256:512]) + brow[:, 256:512]
        share = 0.5 * (1.0 + lax.erf(hidden * (2.0**-0.5)))
        act[at, :] = (hidden * share).astype(BF)
        dge[at, :] = share + hidden * jnp.exp(-0.5 * hidden * hidden) * ((2.0 * np.pi) ** -0.5)

    dy_gather.step(3)

    @pl.loop(0, 32)
    def _(j):
        ost[rows_at(j, 64), :] = osort[order_ref[j]].astype(BF)

    @pl.loop(1, BATCH)
    def _(j):
        giver = lax.rem(b + BATCH - j, BATCH)
        batch_copy(j, 1, wd2.at[rows_at(giver, 32)], wd2.at[rows_at(giver, 32)]).wait_recv()
        batch_copy(j, 2, wo2.at[rows_at(giver, 8)], wo2.at[rows_at(giver, 8)]).wait_recv()

    wob[...] = wo2[...].astype(BF)

    class Scatter:
        def __init__(self, part, sib, half, full, zed, k):
            self.part, self.sib, self.half, self.full, self.zed, self.k = part, sib, half, full, zed, k
            self.order = [(zo, xo), (zo, xr), (zo, xl), (zo, x), (z, xo), (z, xr), (z, xl), (z, x)]

        def copy(self, e, src, dst, device):
            return remote(src, dst, rs_ss.at[self.k, e], rs_rs.at[self.k, e], device)

        def chip(self, n):
            return pl.ds(pl.multiple_of((self.order[n][0] * 4 + self.order[n][1]) * 256, 256), 256)

        def at(self, n, core, low=0, count=TOK):
            zz, xx = self.order[n]
            return pl.ds(pl.multiple_of(slot(zz, xx, core) * TOK + low, 64), count)

        def out(self, e):
            part, sib, half, full = self.part, self.sib, self.half, self.full
            if e < 8:
                return part.at[self.at(e, co)], sib.at[rows_at(e, TOK)], sibling
            if e == 16:
                return part.at[self.at(3, c)], self.zed, across
            g, kind = (e - 8) // 4, (e - 8) % 4
            if kind == 0:
                return part.at[self.at(4 * g, c, 0, 64)], half.at[rows_at(2 * g, 64)], left
            if kind == 1:
                return part.at[self.at(4 * g, c, 64, 64)], half.at[rows_at(2 * g + 1, 64)], right
            if kind == 2:
                return part.at[self.at(4 * g + 1, c)], full.at[rows_at(2 * g, TOK)], right
            return part.at[self.at(4 * g + 2, c)], full.at[rows_at(2 * g + 1, TOK)], left

        def start(self, e):
            self.copy(e, *self.out(e)).start()

        def wait(self, e):
            src, dst, device = self.out(e)
            self.copy(e, dst, dst, device).wait_recv()

        def add_sibling(self, n):
            self.wait(n)
            at = self.at(n, c)
            self.part[at, :] = (
                self.part[at, :].astype(F32) + self.sib[n * TOK : n * TOK + TOK, :].astype(F32)
            ).astype(BF)

        def add_half(self, n, e, low, index):
            self.wait(e)
            at = self.at(n, c, low, 64)
            self.part[at, :] = (
                self.part[at, :].astype(F32) + self.half[index * 64 : index * 64 + 64, :].astype(F32)
            ).astype(BF)

        def full_sum(self, n, g):
            self.wait(8 + 4 * g + 2)
            self.wait(8 + 4 * g + 3)
            total = self.part[self.at(n, c), :].astype(F32)
            for index in (2 * g, 2 * g + 1):
                total = total + self.full[index * TOK : index * TOK + TOK, :].astype(F32)
            return total

        def step(self, n):
            if n == 0 or n == 3:
                g = n // 3
                self.add_sibling(4 * g)
                self.start(8 + 4 * g)
                self.start(8 + 4 * g + 1)
                self.add_sibling(4 * g + 1)
                self.add_sibling(4 * g + 2)
            elif n == 1 or n == 4:
                g = n // 4
                self.add_half(4 * g + 1, 8 + 4 * g + 1, 64, 2 * g + 1)
                self.start(8 + 4 * g + 2)
                self.add_half(4 * g + 2, 8 + 4 * g, 0, 2 * g)
                self.start(8 + 4 * g + 3)
                self.add_sibling(4 * g + 3)
            elif n == 2:
                self.part[self.at(3, c), :] = self.full_sum(3, 0).astype(BF)
                self.start(16)

        def result(self):
            total = self.full_sum(7, 1)
            self.wait(16)
            return total + self.zed[...].astype(F32)

        def drain(self):
            for e in range(17):
                self.copy(e, *self.out(e)).wait_send()

    mixed_sum = Scatter(part, sib_m, half_m, full_m, zed_m, 0)
    dn_sum = Scatter(part, sib_d, half_d, full_d, zed_d, 1)

    for n in range(8):
        at = mixed_sum.chip(n)
        part[at, :] = (dot(act[at, :], wd2[...]) + dot(ost[at, :], wob[...])).astype(BF)
        mixed_sum.start(n)

    mixed_sum.step(0)
    dy_gather.step(4)

    @pl.loop(0, 8)
    def _(i):
        at = rows_at(i, QB)
        dy = dya[at, :]
        dcat[at, 256:512] = (dot_nt(dy, wd2[...]) * dge[at, :]).astype(BF)
        dost[pl.ds(i * 4, 4)] = dot_nt(dy, wob[...]).astype(BF).reshape(4, 64, HD)

    mixed_sum.step(1)
    mixed_sum.step(3)

    gdacc[...] = jnp.zeros_like(gdacc)

    @pl.loop(0, 4)
    def _(i):
        at = rows_at(i, 512)
        gdacc[0:256, :] += dot_tn(act[at, :], dya[at, :])
        gdacc[256:320, :] += dot_tn(ost[at, :], dya[at, :])

    gdsend[...] = gdacc[0:256, :].astype(BF)
    gosend[...] = gdacc[256:320, :]
    gdrecv[rows_at(b, 32), :] = gdsend[rows_at(b, 32), :]
    gorecv[rows_at(b, 8), :] = gosend[rows_at(b, 8), :]

    @pl.loop(1, BATCH)
    def _(j):
        peer = lax.rem(b + j, BATCH)
        batch_copy(j, 3, gdsend.at[rows_at(peer, 32)], gdrecv.at[rows_at(b, 32)]).start()
        batch_copy(j, 4, gosend.at[rows_at(peer, 8)], gorecv.at[rows_at(b, 8)]).start()

    mixed_sum.step(2)
    mixed_sum.step(4)

    gtu[...] = jnp.zeros_like(gtu)

    @pl.loop(0, 4)
    def _(i):
        at = rows_at(i, 512)
        gtu[...] += dot_tn(dcat[at, 256:512], nrm[at, :])

    def column_sum(low):
        def add(i, total):
            return total + jnp.sum(dcat[rows_at(i, QB), low : low + 256].astype(F32), axis=0, keepdims=True)

        return lax.fori_loop(0, 8, add, jnp.zeros((1, 256), F32))

    def to_flat(line, values):
        for k in range(values.shape[1] // 128):
            flat[line + k : line + k + 1, :] = values[:, k * 128 : k * 128 + 128]

    def hand_out(gt, raw, sums, k, send, recv, copy_k):
        for i in range(4):
            at = slice(i * 256, i * 256 + 256)
            grad = gt[0:256, at].T
            gain = jnp.sum(grad * raw[at, :], axis=1, keepdims=True)
            shift = jnp.sum(sums * raw[at, :], axis=1, keepdims=True)
            lane = iota((256, 128), 1)
            spread = jnp.where(lane == 0, gain, jnp.where(lane == 1, shift, 0.0)).T
            to_flat(k * 8 + i * 2, spread[0:1, :])
            to_flat(k * 8 + 8 + i * 2, spread[1:2, :])
            grad = grad * cols[at, k : k + 1] + cols[at, k + 1 : k + 2] * sums
            for m in range(8):
                for h in range(2):
                    place = m * 128 + i * 32 + h * 16
                    first, second = (h * 2) * 64 + m * 8, (h * 2 + 1) * 64 + m * 8
                    send[place : place + 16, :] = jnp.concatenate(
                        [grad[first : first + 8, :], grad[second : second + 8, :]], axis=0
                    ).astype(BF)
        recv[rows_at(b, 128), :] = send[rows_at(b, 128), :]

        @pl.loop(1, BATCH)
        def _(j):
            peer = lax.rem(b + j, BATCH)
            batch_copy(j, copy_k, send.at[rows_at(peer, 128)], recv.at[rows_at(b, 128)]).start()

    def sum_rows(recv, total_ref, final, copy_k, seq_k):
        @pl.loop(1, BATCH)
        def _(j):
            giver = lax.rem(b + BATCH - j, BATCH)
            batch_copy(j, copy_k, recv.at[rows_at(giver, 128)], recv.at[rows_at(giver, 128)]).wait_recv()

        total = recv[0:128, :].astype(F32)
        for k in range(1, BATCH):
            total = total + recv[k * 128 : k * 128 + 128, :].astype(F32)
        total_ref[...] = total
        final[rows_at(s, 8), :] = total_ref[rows_at(s, 8), :]

        @pl.loop(1, SEQ)
        def _(j):
            peer = lax.rem(s + j, SEQ)
            seq_copy(j, seq_k, total_ref.at[rows_at(peer, 8)], final.at[rows_at(s, 8)]).start()

    sum_u = column_sum(256)
    hand_out(gtu, rawu, sum_u, 2, gusend, gurecv, 5)

    @pl.loop(0, 8)
    def _(i):
        at = rows_at(i, QB)
        come = [dost[inv_ref[i * 4 + k]] for k in range(4)]
        grads = jnp.concatenate(come, axis=0).astype(F32)
        past = osort[pl.ds(i * 4, 4)].reshape(QB, HD)
        delta = jnp.sum(grads * past, axis=1, keepdims=True)
        wide = jnp.concatenate([grads, jnp.zeros((QB, 64), F32)], axis=1)
        wide = with_lanes(wide, 64, pieces_of(-delta)).astype(BF)
        doa[at, :] = wide
        doat[:, at] = wide.T[0:64, :]

    dkt[...] = jnp.zeros_like(dkt)
    dvt[...] = jnp.zeros_like(dvt)
    mixed_ref[...] = (mixed_sum.result() + x_ref[...].astype(F32) + drow[...]).astype(BF)

    @pl.loop(0, ROW // AB)
    def _(i):
        at = rows_at(i, AB)

        def step(j, dq, masked):
            k_at = rows_at(j, AB)
            probs = jnp.exp(dot(qa[at, :], kat[:, k_at]))
            if masked:
                probs = jnp.where(lower, probs, 0.0)
            grads = (probs * dot(doa[at, :], vat[:, k_at])).astype(BF)
            dkt[:, k_at] += dot(qat[:, at], grads)
            dvt[:, k_at] += dot(doat[:, at], probs.astype(BF))
            return dq + dot(grads, ka[k_at, :])

        dq = lax.fori_loop(0, i, lambda j, dq: step(j, dq, False), jnp.zeros((AB, 128), F32))
        dqs[at, :] = step(i, dq, True) * 0.125

    @pl.loop(0, 8)
    def _(i):
        at = rows_at(i, QB)
        both = jnp.concatenate([dqs[at, 0:64], dkt[:, at].T], axis=1)
        both = both * tabc[at, :] - partner_of(both) * tabs[at, :]
        last = jnp.concatenate([dvt[:, at].T, jnp.zeros((QB, 64), F32)], axis=1)
        whole = jnp.concatenate([both, last], axis=1).astype(BF)
        dsort[pl.ds(i * 4, 4)] = whole.reshape(4, 64, 256)

    @pl.loop(0, 32)
    def _(j):
        dcat[rows_at(j, 64), 0:256] = dsort[order_ref[j]]

    mixed_sum.drain()
    for n in range(8):
        at = dn_sum.chip(n)
        part[at, :] = dot_nt(dcat[at, :], wcat[...]).astype(BF)
        dn_sum.start(n)
    dn_sum.step(0)
    dn_sum.step(3)

    gdacc[0:256, :] = jnp.zeros((256, D), F32)

    @pl.loop(0, 4)
    def _(i):
        at = rows_at(i, 512)
        gdacc[0:256, :] += dot_tn(dcat[at, 0:256], nrm[at, :])

    dn_sum.step(1)
    sum_q = column_sum(0)
    hand_out(gdacc, rawq, sum_q, 0, gqsend, gqrecv, 6)

    def low_half(part_of):
        return jnp.concatenate([part_of[:, 0:64], jnp.zeros((1, 64), F32)], axis=1)

    flat[32:56, :] = jnp.zeros((24, 128), F32)
    flat[64:96, :] = jnp.zeros((32, 128), F32)
    flat[104:112, :] = jnp.zeros((8, 128), F32)
    upper = lax.rem(s, 2) == 1
    spans = (sum_q[:, 0:128], pltpu.roll(sum_q[:, 0:128], 64, 1), sum_q[:, 128:256])
    for k in range(3):
        mine = low_half(spans[k])
        mine = jnp.where(upper, pltpu.roll(mine, 64, 1), mine)
        flat[pl.ds(32 + k * 8 + s // 2, 1), :] = mine
    flat[pl.ds(64 + 2 * s, 1), :] = sum_u[:, 0:128]
    flat[pl.ds(65 + 2 * s, 1), :] = sum_u[:, 128:256]
    dy_total = jnp.sum(dy_ref[...].astype(F32), axis=0, keepdims=True)
    to_flat(56, dy_total)
    to_flat(96, dy_total)
    for k in range(SEQ):
        fsend[k * 8 : k * 8 + 8, :] = flat[13 * k // 2 : 13 * k // 2 + 8, :]
    frecv[rows_at(s, 8), :] = fsend[rows_at(s, 8), :]

    @pl.loop(1, SEQ)
    def _(j):
        peer = lax.rem(s + j, SEQ)
        seq_copy(j, 3, fsend.at[rows_at(peer, 8)], frecv.at[rows_at(s, 8)]).start()

    dn_sum.step(4)
    dn_sum.step(2)

    sum_rows(gurecv, gusum, gufin, 5, 1)
    sum_rows(gqrecv, gqsum, gqfin, 6, 2)

    @pl.loop(1, SEQ)
    def _(j):
        giver = lax.rem(s + SEQ - j, SEQ)
        seq_copy(j, 3, frecv.at[rows_at(giver, 8)], frecv.at[rows_at(giver, 8)]).wait_recv()

    total = frecv[0:8, :]
    for k in range(1, SEQ):
        total = total + frecv[k * 8 : k * 8 + 8, :]
    fsum[...] = total
    fall[rows_at(b, 8), :] = total

    @pl.loop(1, BATCH)
    def _(j):
        batch_copy(j, 7, fsum, fall.at[rows_at(b, 8)]).start()

    @pl.loop(1, BATCH)
    def _(j):
        giver = lax.rem(b + BATCH - j, BATCH)
        batch_copy(j, 3, gdrecv.at[rows_at(giver, 32)], gdrecv.at[rows_at(giver, 32)]).wait_recv()
        batch_copy(j, 4, gorecv.at[rows_at(giver, 8)], gorecv.at[rows_at(giver, 8)]).wait_recv()

    total_d = gdrecv[0:32, :].astype(F32)
    total_o = gorecv[0:8, :]
    for k in range(1, BATCH):
        total_d = total_d + gdrecv[k * 32 : k * 32 + 32, :].astype(F32)
        total_o = total_o + gorecv[k * 8 : k * 8 + 8, :]
    gd_ref[...] = total_d
    go_ref[...] = total_o

    merged = dn_sum.result()
    _, normed, inverse = normed_of()
    grad_norm = inverse * (
        merged
        - jnp.mean(merged, axis=-1, keepdims=True)
        - normed * jnp.mean(merged * normed, axis=-1, keepdims=True)
    )
    gtok_ref[...] = (dy_ref[...].astype(F32) + grad_norm).astype(BF)

    @pl.loop(1, SEQ)
    def _(j):
        giver = lax.rem(s + SEQ - j, SEQ)
        seq_copy(j, 1, gufin.at[rows_at(giver, 8)], gufin.at[rows_at(giver, 8)]).wait_recv()
        seq_copy(j, 2, gqfin.at[rows_at(giver, 8)], gqfin.at[rows_at(giver, 8)]).wait_recv()

    @pl.loop(1, BATCH)
    def _(j):
        giver = lax.rem(b + BATCH - j, BATCH)
        batch_copy(j, 7, fall.at[rows_at(giver, 8)], fall.at[rows_at(giver, 8)]).wait_recv()

    gu_ref[...] = gufin[...]
    gq_ref[...] = gqfin[...]
    total = fall[0:8, :]
    for k in range(1, BATCH):
        total = total + fall[k * 8 : k * 8 + 8, :]
    small_ref[...] = total

    normed_gather.drain()
    dy_gather.drain()
    dn_sum.drain()

    @pl.loop(1, SEQ)
    def _(j):
        peer = lax.rem(s + j, SEQ)
        seq_copy(j, 0, wsend.at[rows_at(peer, 16)], wst.at[rows_at(s, 16)]).wait_send()
        seq_copy(j, 1, gusum.at[rows_at(peer, 8)], gufin.at[rows_at(s, 8)]).wait_send()
        seq_copy(j, 2, gqsum.at[rows_at(peer, 8)], gqfin.at[rows_at(s, 8)]).wait_send()
        seq_copy(j, 3, fsend.at[rows_at(peer, 8)], frecv.at[rows_at(s, 8)]).wait_send()

    @pl.loop(1, BATCH)
    def _(j):
        peer = lax.rem(b + j, BATCH)
        batch_copy(j, 0, wst, wbuf.at[rows_at(b, 256)]).wait_send()
        batch_copy(j, 1, wd_ref, wd2.at[rows_at(b, 32)]).wait_send()
        batch_copy(j, 2, wos, wo2.at[rows_at(b, 8)]).wait_send()
        batch_copy(j, 3, gdsend.at[rows_at(peer, 32)], gdrecv.at[rows_at(b, 32)]).wait_send()
        batch_copy(j, 4, gosend.at[rows_at(peer, 8)], gorecv.at[rows_at(b, 8)]).wait_send()
        batch_copy(j, 5, gusend.at[rows_at(peer, 128)], gurecv.at[rows_at(b, 128)]).wait_send()
        batch_copy(j, 6, gqsend.at[rows_at(peer, 128)], gqrecv.at[rows_at(b, 128)]).wait_send()
        batch_copy(j, 7, fsum, fall.at[rows_at(b, 8)]).wait_send()


def finish(
    mixed_ref, gtok_ref, gu_ref, gq_ref, gd_ref, go_ref, small_ref,
    mixed_out, gtok_out, small_out, qkv_out, out_out, up_out, down_out,
):
    s = lax.axis_index("seq")
    b = lax.axis_index("batch")
    mixed_out[...] = mixed_ref[...]
    gtok_out[...] = gtok_ref[...]
    out_out[...] = go_ref[...]
    down_out[...] = gd_ref[...]
    low = iota((8, 128), 1) < 64
    for k in range(SEQ):
        up_out[:, k * HID : k * HID + HID] = gu_ref[k * 8 : k * 8 + 8, :]
    for k in range(0, SEQ, 2):
        one, two = (gq_ref[n * 8 : n * 8 + 8, 0:128] for n in (k, k + 1))
        one_v, two_v = (gq_ref[n * 8 : n * 8 + 8, 128:256] for n in (k, k + 1))
        at = k * HD
        qkv_out[:, at : at + 128] = jnp.where(low, one, pltpu.roll(two, 64, 1))
        qkv_out[:, D + at : D + at + 128] = jnp.where(low, pltpu.roll(one, 64, 1), two)
        qkv_out[:, 2 * D + at : 2 * D + at + 128] = jnp.where(low, one_v, pltpu.roll(two_v, 64, 1))
    begin = b * PER + lax.rem(s, 2) * 64
    line = begin // 128
    both = jnp.concatenate([small_ref[pl.ds(line, 1), :], small_ref[pl.ds(line + 1, 1), :]], axis=1)
    both = pltpu.roll(jnp.broadcast_to(both, (8, 256)), 256 - lax.rem(begin, 128), 1)
    small_out[...] = both[0:1, 0:PER]


def layer(x, dy, wq, wo, wu, wd, sp, order, lengths):
    vmem = pl.BlockSpec(memory_space=pltpu.VMEM)
    smem = pl.BlockSpec(memory_space=pltpu.SMEM)
    scratch = [
        ((ROW, D), BF), ((ROW, D), BF), ((256, 256), BF), ((256, 256), BF), ((2048, 256), BF),
        ((256, D), BF), ((8, D), F32), ((64, D), F32), ((64, D), BF),
        ((D, 256), F32), ((D, 256), F32), ((D, 128), F32), ((D, 512), BF),
        ((1, 512), F32), ((1, D), F32),
        ((32, 64, 256), F32), ((ROW, HID), BF), ((ROW, HID), F32),
        ((ROW, 128), F32), ((ROW, 128), F32),
        ((ROW, 128), BF), ((ROW, 128), BF), ((ROW, 128), BF),
        ((128, ROW), BF), ((128, ROW), BF), ((64, ROW), BF), ((ROW, 128), BF), ((64, ROW), BF),
        ((32, 64, HD), BF), ((32, 64, HD), F32), ((ROW, HD), BF),
        ((ROW, 512), BF), ((HD, ROW), F32), ((HD, ROW), F32),
        ((32, 64, 256), BF), ((ROW, 128), F32),
        ((ROW, D), BF),
        ((8 * TOK, D), BF), ((4 * 64, D), BF), ((4 * TOK, D), BF), ((TOK, D), BF),
        ((8 * TOK, D), BF), ((4 * 64, D), BF), ((4 * TOK, D), BF), ((TOK, D), BF),
        ((320, D), F32), ((256, D), F32),
        ((256, D), BF), ((64, D), F32), ((256, D), BF), ((64, D), F32),
        ((D, 256), BF), ((D, 256), BF), ((128, 256), F32), ((128, 256), F32),
        ((D, 256), BF), ((D, 256), BF), ((128, 256), F32), ((128, 256), F32),
        ((112, 128), F32), ((128, 128), F32), ((128, 128), F32), ((8, 128), F32), ((64, 128), F32),
    ]
    shapes = [pltpu.VMEM(shape, dtype) for shape, dtype in scratch]
    shapes += [
        pltpu.SMEM((32,), jnp.int32),
        pltpu.SemaphoreType.DMA((2, 17)), pltpu.SemaphoreType.DMA((2, 17)),
        pltpu.SemaphoreType.DMA((2, 17)), pltpu.SemaphoreType.DMA((2, 17)),
        pltpu.SemaphoreType.DMA((4, SEQ)), pltpu.SemaphoreType.DMA((4, SEQ)),
        pltpu.SemaphoreType.DMA((8, BATCH)), pltpu.SemaphoreType.DMA((8, BATCH)),
    ]
    parts = pl.pallas_call(
        kernel,
        out_shape=(
            jax.ShapeDtypeStruct((TOK, D), BF),
            jax.ShapeDtypeStruct((TOK, D), BF),
            jax.ShapeDtypeStruct((128, 256), F32),
            jax.ShapeDtypeStruct((128, 256), F32),
            jax.ShapeDtypeStruct((32, D), F32),
            jax.ShapeDtypeStruct((8, D), F32),
            jax.ShapeDtypeStruct((8, 128), F32),
        ),
        in_specs=[vmem] * 7 + [smem] * 2,
        out_specs=(vmem,) * 7,
        scratch_shapes=shapes,
        compiler_params=pltpu.CompilerParams(
            collective_id=0, has_side_effects=True, vmem_limit_bytes=62 * 2**20
        ),
    )(x, dy, wq, wo, wu, wd, sp, order, lengths)
    return pl.pallas_call(
        finish,
        out_shape=(
            jax.ShapeDtypeStruct((TOK, D), BF),
            jax.ShapeDtypeStruct((TOK, D), BF),
            jax.ShapeDtypeStruct((1, PER), F32),
            jax.ShapeDtypeStruct((8, 3 * D), F32),
            jax.ShapeDtypeStruct((8, D), F32),
            jax.ShapeDtypeStruct((8, SEQ * HID), F32),
            jax.ShapeDtypeStruct((32, D), F32),
        ),
        in_specs=[vmem] * 7,
        out_specs=(vmem,) * 7,
    )(*parts)


def local(tokens, doc_lengths, block_order, small_params, w_qkv, w_out, w_up, w_down, cotangent):
    mixed, grad_tokens, grad_small, grad_qkv, grad_out, grad_up, grad_down = layer(
        tokens[0], cotangent[0], w_qkv, w_out, w_up, w_down,
        small_params.reshape(1, PER), block_order, doc_lengths,
    )
    return (
        mixed[None], grad_tokens[None], grad_small.reshape(PER), grad_qkv, grad_out, grad_up, grad_down,
    )


def solution(mesh):
    placed = (
        P("batch", "seq", None),
        P("batch", None),
        P(),
        P(("seq", "batch")),
        P(("seq", "batch"), None),
        P(("seq", "batch"), None),
        P(("seq", "batch"), None),
        P(("seq", "batch"), None),
        P("batch", "seq", None),
    )
    return jax.shard_map(
        local,
        mesh=mesh,
        in_specs=placed,
        out_specs=(
            P("batch", "seq", None),
            P("batch", "seq", None),
            P(("seq", "batch")),
            P(("seq", "batch"), None),
            P(("seq", "batch"), None),
            P(("seq", "batch"), None),
            P(("seq", "batch"), None),
        ),
        check_vma=False,
    )
```

```python
import jax
import jax.numpy as jnp
import numpy as np
from jax import lax
from jax.experimental import pallas as pl
from jax.experimental.pallas import tpu as pltpu
from jax.sharding import PartitionSpec as P

HD = 64
ROT = 16
EPS = 1e-05
NEG = -1e30
MESH = pl.DeviceIdType.MESH
BF = jnp.bfloat16
F32 = jnp.float32

SEQ = 16
BATCH = 8
TOK = 128
ROW = SEQ * TOK
D = 1024
HID = 256
PER = 104
QB = 256
AB = 512


def dot(a, b):
    return lax.dot_general(a, b, (((1,), (0,)), ((), ())), preferred_element_type=F32)


def dot_nt(a, b):
    return lax.dot_general(a, b, (((1,), (1,)), ((), ())), preferred_element_type=F32)


def dot_tn(a, b):
    return lax.dot_general(a, b, (((0,), (0,)), ((), ())), preferred_element_type=F32)


def iota(shape, dim):
    return lax.broadcasted_iota(jnp.int32, shape, dim)


def slot(z, x, c):
    return z * 8 + x * 2 + c


def rows_at(index, count):
    return pl.ds(pl.multiple_of(index * count, count), count)


def kernel(
    x_ref, dy_ref, wq_ref, wo_ref, wu_ref, wd_ref, sp_ref, order_ref, len_ref,
    mixed_out, gtok_out, gu_out, gq_out, gd_out, go_out, small_out,
    mixed_ref, gtok_ref, gd_ref, go_ref, small_ref, nrm, dya, ssend, sgot, sall, wsend, wst, wbuf, wd2, wos, wo2, wob, rawq, rawu, cols, wcat, brow, drow,
    prj, act, dge, tabc, tabs, qa, ka, va, kat, vat, qat, doa, doat, dost, osort, ost,
    dcat, dkt, dvt, dsort, dqs,
    part_m, part_d, land_m, land_d, gdpair, gdland, gopair, goland, gupair, guland,
    gdacc, gtq, gtu, gdsend, gosend, gdrecv, gorecv,
    gusend, gurecv, gusum, gufin, gqsend, gqrecv, gqsum, gqfin,
    flat, fsend, frecv, fsum, fall,
    inv_ref, out_ss, ag_ss, ag_rs, rs_ss, rs_rs, sq_ss, sq_rs, bt_ss, bt_rs,
):
    s = lax.axis_index("seq")
    b = lax.axis_index("batch")
    z, x, c = s // 8, lax.rem(s // 2, 4), lax.rem(s, 2)
    xr, xl, xo = lax.rem(x + 1, 4), lax.rem(x + 3, 4), lax.rem(x + 2, 4)
    zo, co = 1 - z, 1 - c
    y, w = b // 2, lax.rem(b, 2)
    yr, yl, yo, wo_ = lax.rem(y + 1, 4), lax.rem(y + 3, 4), lax.rem(y + 2, 4), 1 - w
    right, left = (slot(z, xr, c), b), (slot(z, xl, c), b)
    across, sibling = (slot(zo, x, c), b), (slot(z, x, co), b)

    def remote(src, dst, send, recv, device):
        return pltpu.make_async_remote_copy(
            src_ref=src, dst_ref=dst, send_sem=send, recv_sem=recv,
            device_id=device, device_id_type=MESH,
        )

    barrier = pltpu.get_barrier_semaphore()

    @pl.loop(1, SEQ)
    def _(j):
        pl.semaphore_signal(barrier, inc=1, device_id=(lax.rem(s + j, SEQ), b), device_id_type=MESH)

    @pl.loop(1, BATCH)
    def _(j):
        pl.semaphore_signal(barrier, inc=1, device_id=(s, lax.rem(b + j, BATCH)), device_id_type=MESH)

    def normed_of():
        inputs = x_ref[...].astype(F32)
        centred = inputs - jnp.mean(inputs, axis=-1, keepdims=True)
        inverse = lax.rsqrt(jnp.mean(centred * centred, axis=-1, keepdims=True) + EPS)
        return inputs, centred * inverse, inverse

    nrm[rows_at(s, TOK), :] = normed_of()[1].astype(BF)
    dya[rows_at(s, TOK), :] = dy_ref[...]

    def pair(one, two):
        return jnp.where(iota((8, 128), 1) < 64, one, two)

    small = jnp.concatenate([sp_ref[...].astype(F32), jnp.zeros((1, 128 - PER), F32)], axis=1)
    ssend[...] = jnp.broadcast_to(small, (16, 128)).astype(BF)
    wide_q = wq_ref[...].astype(F32)
    wide_u = wu_ref[...].astype(F32)
    for k in range(SEQ):
        at = slice(k // 2 * 128, k // 2 * 128 + 128)
        q, kk, v = (wide_q[:, n * D : n * D + D][:, at] for n in range(3))
        turned = [pltpu.roll(part_of, 64, 1) for part_of in (q, kk, v)]
        q, kk, v = (q, turned[1], v) if k % 2 == 0 else (turned[0], kk, turned[2])
        low = jnp.concatenate([pair(q, kk), pair(v, jnp.zeros_like(v))], axis=1)
        block = jnp.concatenate([wide_u[:, k * HID : k * HID + HID], low], axis=0)
        wsend[k * 16 : k * 16 + 16, :] = block.astype(BF)

    wst[rows_at(s, 16), :] = wsend[rows_at(s, 16), :]
    sgot[rows_at(s, 16), :] = ssend[...]
    wos[...] = wo_ref[...].astype(F32)
    wd2[rows_at(b, 32), :] = wd_ref[...]
    wo2[rows_at(b, 8), :] = wos[...]

    pl.semaphore_wait(barrier, SEQ - 1 + BATCH - 1)

    def seq_copy(j, k, src, dst):
        return remote(src, dst, sq_ss.at[k], sq_rs.at[k], (lax.rem(s + j, SEQ), b))

    def seq_all(k, ref, count):
        ref = ref.at[pl.ds(0, (SEQ - 1) * count)]
        return seq_copy(1, k, ref, ref)

    def column_copy(j, k, src, dst):
        return remote(src, dst, bt_ss.at[k], bt_rs.at[k], (s, lax.rem(y + j, 4) * 2 + w))

    def column_start(k, send, recv, count):
        @pl.loop(1, 4)
        def _(j):
            peer = lax.rem(y + j, 4)
            column_copy(j, k, send.at[rows_at(peer, 2 * count)], recv.at[rows_at(y, 2 * count)]).start()

    def column_all(k, ref, count):
        ref = ref.at[pl.ds(0, 6 * count)]
        return column_copy(1, k, ref, ref)

    def pair_copy(k, pair, land, count):
        src = pair.at[rows_at(wo_, count)]
        return remote(src, land, bt_ss.at[k], bt_rs.at[k], (s, y * 2 + wo_))

    def column_sums(k, recv, pair, land, count):
        column_all(k, recv, count).wait_recv()
        total = recv[0 : 2 * count, :].astype(F32)
        for n in range(1, 4):
            total = total + recv[2 * n * count : 2 * (n + 1) * count, :].astype(F32)
        pair[...] = total.astype(pair.dtype)
        pair_copy(k + 5, pair, land, count).start()

    def pair_sum(k, pair, land, count):
        pair_copy(k + 5, pair, land, count).wait_recv()
        return pair[rows_at(w, count), :].astype(F32) + land[...].astype(F32)

    def batch_all(k, ref, count):
        ref = ref.at[pl.ds(0, (BATCH - 1) * count)]
        return batch_copy(1, k, ref, ref)

    def batch_copy(j, k, src, dst):
        return remote(src, dst, bt_ss.at[k], bt_rs.at[k], (s, lax.rem(b + j, BATCH)))

    @pl.loop(1, SEQ)
    def _(j):
        peer = lax.rem(s + j, SEQ)
        seq_copy(j, 0, wsend.at[rows_at(peer, 16)], wst.at[rows_at(s, 16)]).start()

    class Gather:
        def __init__(self, buf, k, size, slots, right, left, across, sibling=None):
            self.buf, self.k, self.size = buf, k, size
            own, far, of_left, of_right, far_left, far_right, opposite, far_opposite = slots[0]
            half = size // 2
            self.sends = {
                0: (own, right, 0, size), 1: (own, left, 0, size), 2: (own, across, 0, size),
                4: (far, right, 0, size), 5: (far, left, 0, size),
                7: (of_left, right, 0, half), 8: (of_right, left, half, half),
                11: (far_left, right, 0, half), 12: (far_right, left, half, half),
            }
            self.receives = {
                0: (of_left, 0, size), 1: (of_right, 0, size), 2: (far, 0, size),
                4: (far_left, 0, size), 5: (far_right, 0, size),
                7: (opposite, 0, half), 8: (opposite, half, half),
                11: (far_opposite, 0, half), 12: (far_opposite, half, half),
            }
            if sibling is not None:
                for e, n in ((3, 0), (6, 1), (9, 2), (10, 3), (13, 4), (14, 5), (15, 6), (16, 7)):
                    self.sends[e] = (slots[0][n], sibling, 0, size)
                    self.receives[e] = (slots[1][n], 0, size)

        def copy(self, e, index, device, low, count):
            at = self.buf.at[pl.ds(pl.multiple_of(index * self.size + low, self.size // 2), count)]
            return remote(at, at, ag_ss.at[self.k], ag_rs.at[self.k, e], device)

        def start(self, *events):
            for e in events:
                if e in self.sends:
                    self.copy(e, self.sends[e][0], *self.sends[e][1:]).start()

        def wait(self, *events):
            for e in events:
                if e in self.receives:
                    index, low, count = self.receives[e]
                    self.copy(e, index, self.sends[e][1], low, count).wait_recv()

        def step(self, n):
            if n == 0:
                self.start(0, 1, 2, 3)
            elif n == 1:
                self.wait(2)
                self.start(4, 5, 6)
                self.wait(0)
                self.start(7, 9)
                self.wait(1)
                self.start(8, 10)
            elif n == 2:
                self.wait(4)
                self.start(11, 13)
                self.wait(5)
                self.start(12, 14)
            elif n == 3:
                self.wait(7, 8)
                self.start(15)
                self.wait(11, 12)
                self.start(16)
            else:
                self.wait(3, 6, 9, 10, 13, 14, 15, 16)

        def drain(self):
            sent = self.buf.at[pl.ds(0, sum(what[3] for what in self.sends.values()))]
            remote(sent, sent, ag_ss.at[self.k], ag_rs.at[self.k, 0], right).wait_send()

    def row_slots(core):
        return [slot(p, q, core) for p, q in ((z, x), (zo, x), (z, xl), (z, xr), (zo, xl), (zo, xr), (z, xo), (zo, xo))]

    rows_slots = [q * 2 + p for p, q in ((w, y), (wo_, y), (w, yl), (w, yr), (wo_, yl), (wo_, yr), (w, yo), (wo_, yo))]

    normed_gather = Gather(nrm, 0, TOK, (row_slots(c), row_slots(co)), right, left, across, sibling)
    dy_gather = Gather(dya, 1, TOK, (row_slots(c), row_slots(co)), right, left, across, sibling)
    weight_gather = Gather(
        wbuf, 2, 256, (rows_slots,), (s, yr * 2 + w), (s, yl * 2 + w), (s, y * 2 + wo_)
    )
    @pl.loop(0, 32)
    def _(i):
        place = jnp.int32(0)
        for j in range(32):
            place = place + jnp.where(order_ref[j] == i, j, 0)
        inv_ref[i] = jnp.minimum(place, 31)

    normed_gather.step(0)

    @pl.loop(1, SEQ)
    def _(j):
        seq_copy(j, 4, ssend, sgot.at[rows_at(s, 16)]).start()

    outputs = (
        (mixed_ref, mixed_out), (gtok_ref, gtok_out), (gufin, gu_out), (gqfin, gq_out),
        (gd_ref, gd_out), (go_ref, go_out), (small_ref, small_out),
    )

    def output(n):
        return pltpu.make_async_copy(*outputs[n], out_ss.at[n])

    ends = [len_ref[0, 0]]
    for k in range(1, 4):
        ends.append(ends[-1] + len_ref[0, k])

    def begin_of(where):
        begin = jnp.zeros_like(where)
        for end in ends:
            begin = jnp.maximum(begin, jnp.where(where >= end, end, 0))
        return begin

    def doc_of(where):
        doc = jnp.zeros_like(where)
        for end in ends:
            doc = doc + jnp.where(where >= end, 1, 0)
        return doc

    def partner_of(part):
        lane = lax.rem(iota(part.shape, 1), 64)
        return jnp.where(lane < ROT // 2, pltpu.roll(part, 120, 1), pltpu.roll(part, 8, 1))

    rate = jnp.zeros((1, 128), F32)
    for k in range(ROT // 2):
        value = float(np.float32(10000.0) ** np.float32(-2.0 * k / ROT))
        rate = jnp.where(lax.rem(iota((1, 128), 1), 8) == k, value, rate)

    @pl.loop(0, 8)
    def _(i):
        where = i * QB + iota((QB, 128), 0)
        angle = (where - begin_of(where)).astype(F32) * rate
        lane = lax.rem(iota((QB, 128), 1), 64)
        sine = jnp.sin(angle)
        tabc[rows_at(i, QB), :] = jnp.where(lane < ROT, jnp.cos(angle), 1.0)
        sine = jnp.where(lane < ROT // 2, -sine, sine)
        tabs[rows_at(i, QB), :] = jnp.where(lane < ROT, sine, 0.0)

    seq_all(0, wst, 16).wait_recv()
    seq_all(4, sgot, 16).wait_recv()

    wbuf[rows_at(b, 256), :] = wst[...]
    weight_gather.step(0)
    lines = [sgot[k * 16 : k * 16 + 16, :].astype(F32)[0:1, :] for k in range(SEQ)]
    sall[rows_at(b, 16), :] = jnp.concatenate(lines, axis=0).astype(BF)

    @pl.loop(1, BATCH)
    def _(j):
        batch_copy(j, 0, sall.at[rows_at(b, 16)], sall.at[rows_at(b, 16)]).start()

    normed_gather.step(1)
    weight_gather.step(1)

    batch_all(0, sall, 16).wait_recv()

    def hot_of(line, number):
        low = (lax.rem(line, 16) * BATCH + line // 16) * PER
        return ((low <= number) & (number < low + PER)).astype(F32).astype(BF)

    def place_of(number):
        owner = jnp.floor((number.astype(F32) + 0.5) * (1.0 / PER)).astype(jnp.int32)
        return number - PER * owner

    for k in range(4):
        number = k * D + iota((D, 1), 0)
        found = dot(hot_of(iota((1, 128), 1), number), sall[...])
        found = jnp.where(iota((D, 128), 1) == place_of(number), found, 0.0)
        cols[:, k : k + 1] = jnp.sum(found, axis=1, keepdims=True)

    def small_row(number):
        found = dot_tn(sall[...], hot_of(iota((128, 1), 0), number))
        found = jnp.where(iota((128, number.shape[1]), 0) == place_of(number), found, 0.0)
        return jnp.sum(found, axis=0, keepdims=True)

    lane = iota((1, 256), 1)
    number_q = 4 * D + (lane // 64) * D + s * 64 + lax.rem(lane, 64)
    bias_q = small_row(jnp.where(lane < 192, number_q, -1000))
    bias_u = small_row(8 * D + s * HID + lane)
    wide = iota((1, D), 1)
    drow[...] = small_row(7 * D + wide) + small_row(12 * D + wide)

    dy_gather.start(2)
    weight_gather.step(2)
    normed_gather.step(2)
    dy_gather.start(0, 1)
    weight_gather.step(3)

    @pl.loop(0, SEQ)
    def _(i):
        for j in range(BATCH):
            block = wbuf[pl.ds(pl.multiple_of(j * 256 + i * 16, 16), 16), :].astype(F32)
            at = pl.ds(pl.multiple_of(i * 64 + j * 8, 8), 8)
            rawu[at, :] = block[0:8, :]
            rawq[at, :] = block[8:16, :]

    row_q, row_u = bias_q, bias_u
    for i in range(8):
        at = slice(i * 128, i * 128 + 128)
        wq, wu = rawq[at, :], rawu[at, :]
        wcat[at, 0:256] = (wq * cols[at, 0:1]).astype(BF)
        wcat[at, 256:512] = (wu * cols[at, 2:3]).astype(BF)
        row_q = row_q + jnp.sum(wq * cols[at, 1:2], axis=0, keepdims=True)
        row_u = row_u + jnp.sum(wu * cols[at, 3:4], axis=0, keepdims=True)
    brow[:, 0:256] = row_q
    brow[:, 256:512] = row_u

    normed_gather.step(3)
    dy_gather.wait(2)
    dy_gather.start(4, 5, 3, 6)
    normed_gather.step(4)

    @pl.loop(0, 4)
    def _(i):
        out = dot(nrm[rows_at(i, 512), :], wcat[:, 0:256]) + brow[:, 0:256]
        prj[pl.ds(i * 8, 8)] = out.reshape(8, 64, 256)

    @pl.loop(1, BATCH)
    def _(j):
        batch_copy(j, 1, wd_ref, wd2.at[rows_at(b, 32)]).start()
        batch_copy(j, 2, wos, wo2.at[rows_at(b, 8)]).start()

    def pieces_of(value):
        high = value.astype(BF).astype(F32)
        mid = (value - high).astype(BF).astype(F32)
        return high, mid, value - high - mid

    def with_lanes(base, first, values):
        lane = iota(base.shape, 1)
        for k, value in enumerate(values):
            base = jnp.where(lane == first + k, value, base)
        return base

    def blocks_of(ref, order, i):
        return jnp.concatenate([ref[order[i * 4 + k]] for k in range(4)], axis=0)

    @pl.loop(0, 8)
    def _(i):
        at = rows_at(i, QB)
        come = blocks_of(prj, inv_ref, i)
        both = come[:, 0:128]
        both = both * tabc[at, :] + partner_of(both) * tabs[at, :]
        lane = iota((QB, 128), 1)
        own = doc_of(i * QB + iota((QB, 128), 0)) == lane - 64
        front = lane < 64
        query = jnp.where(front, both * 0.125, jnp.where(own | (lane >= 68), 0.0, NEG)).astype(BF)
        tail = jnp.where(lane < 68, own.astype(F32), (lane < 71).astype(F32))
        key = jnp.where(front, pltpu.roll(both, 64, 1), tail).astype(BF)
        value = jnp.where(front, come[:, 128:256], (lane < 67).astype(F32)).astype(BF)
        qa[at, :], ka[at, :], va[at, :] = query, key, value
        qat[:, at] = query.T[0:64, :]
        kat[:, at] = key.T
        vat[:, at] = value.T

    dy_gather.wait(0)
    dy_gather.start(7)
    dy_gather.wait(1)
    dy_gather.start(8)

    lower = iota((AB, AB), 1) <= iota((AB, AB), 0)

    def attend(i):
        at = rows_at(i, AB)

        def step(j, carry, masked):
            top, total = carry
            k_at = rows_at(j, AB)
            scores = dot(qa[at, :], kat[:, k_at])
            if masked:
                scores = jnp.where(lower, scores, NEG)
            peak = jnp.maximum(top, jnp.max(scores, axis=1, keepdims=True))
            expos = jnp.exp(scores - peak).astype(BF)
            return peak, total * jnp.exp(top - peak) + dot(expos, va[k_at, :])

        start = (jnp.full((AB, 1), NEG, F32), jnp.zeros((AB, 128), F32))
        carry = lax.fori_loop(0, i, lambda j, carry: step(j, carry, False), start)
        top, total = step(i, carry, True)
        norm = total[:, 64:65]
        osort[pl.ds(i * (AB // 64), AB // 64)] = (total / norm)[:, 0:64].reshape(AB // 64, 64, HD)
        qa[at, :] = with_lanes(qa[at, :].astype(F32), 68, pieces_of(-(top + jnp.log(norm)))).astype(BF)

    pl.loop(0, 3)(attend)
    dy_gather.wait(4)
    dy_gather.start(11)
    dy_gather.wait(5)
    dy_gather.start(12, 9, 10)
    pl.loop(3, 4)(attend)

    @pl.loop(0, 4)
    def _(i):
        at = rows_at(i, 512)
        hidden = dot(nrm[at, :], wcat[:, 256:512]) + brow[:, 256:512]
        share = 0.5 * (1.0 + lax.erf(hidden * (2.0**-0.5)))
        act[at, :] = (hidden * share).astype(BF)
        dge[at, :] = share + hidden * jnp.exp(-0.5 * hidden * hidden) * ((2.0 * np.pi) ** -0.5)

    dy_gather.wait(7, 8, 11, 12)
    dy_gather.start(13, 14, 15, 16)

    @pl.loop(0, 8)
    def _(j):
        ost[rows_at(j, QB), :] = blocks_of(osort, order_ref, j).astype(BF)

    batch_all(1, wd2, 32).wait_recv()
    batch_all(2, wo2, 8).wait_recv()

    wob[...] = wo2[...].astype(BF)

    class Scatter:
        def __init__(self, part, land, k):
            self.part, self.land, self.k = part, land, k
            self.order = [(zo, xo), (zo, xr), (zo, xl), (zo, x), (z, xo), (z, xr), (z, xl), (z, x)]
            table = [(n, co, 0, TOK, sibling, None) for n in range(8)]
            for g in (0, 4):
                table += [
                    (g, c, 0, 64, left, g + 2), (g, c, 64, 64, right, g + 1),
                    (g + 1, c, 0, 64, right, g + 3), (g + 2, c, 64, 64, left, g + 3),
                    (g + 1, c, 64, 64, right, g + 3), (g + 2, c, 0, 64, left, g + 3),
                ]
            table += [(3, c, 0, TOK, across, 7)]
            self.table, self.begin, at = table, [], 0
            for entry in table:
                self.begin.append(at)
                at += entry[3]

        def chip(self, n):
            return pl.ds(pl.multiple_of((self.order[n][0] * 4 + self.order[n][1]) * 256, 256), 256)

        def at(self, n, core, low, count):
            zz, xx = self.order[n]
            return pl.ds(pl.multiple_of(slot(zz, xx, core) * TOK + low, 16), count)

        def copy(self, e, src, dst, device):
            return remote(src, dst, rs_ss.at[self.k], rs_rs.at[self.k, e], device)

        def out(self, e):
            n, core, low, count, device, _ = self.table[e]
            return self.part.at[self.at(n, core, low, count)], self.land.at[pl.ds(self.begin[e], count)], device

        def start(self, *events):
            for e in events:
                self.copy(e, *self.out(e)).start()

        def wait(self, e):
            src, dst, device = self.out(e)
            self.copy(e, dst, dst, device).wait_recv()

        def landed(self, e):
            self.wait(e)
            return self.land[self.begin[e] : self.begin[e] + self.table[e][3], :].astype(F32)

        def add(self, *events):
            for e in events:
                n, core, low, count, _, to = self.table[e]
                to = e if e < 8 else to
                at = self.at(to, c, low, count)
                self.part[at, :] = (self.part[at, :].astype(F32) + self.landed(e)).astype(BF)

        def step(self, n):
            if n == 0 or n == 1:
                self.add(4 * n)
                self.start(8 + 6 * n, 9 + 6 * n)
            elif n == 2 or n == 3:
                g = n - 2
                self.add(4 * g + 1, 4 * g + 2)
                self.start(10 + 6 * g, 11 + 6 * g)
                self.add(4 * g + 3)
            elif n == 4 or n == 5:
                g = n - 4
                self.add(8 + 6 * g, 9 + 6 * g)
                self.start(12 + 6 * g, 13 + 6 * g)
            else:
                self.add(10, 11, 12, 13)
                self.start(20)

        def result(self):
            total = self.part[self.at(7, c, 0, TOK), :].astype(F32)
            low = total[0:64, :] + self.landed(16) + self.landed(19)
            high = total[64:TOK, :] + self.landed(17) + self.landed(18)
            return jnp.concatenate([low, high], axis=0) + self.landed(20)

        def drain(self):
            sent = self.part.at[pl.ds(0, sum(entry[3] for entry in self.table))]
            self.copy(0, sent, sent, sibling).wait_send()

    mixed_sum = Scatter(part_m, land_m, 0)
    dn_sum = Scatter(part_d, land_d, 1)

    for n in range(8):
        at = mixed_sum.chip(n)
        part_m[at, :] = (dot(act[at, :], wd2[...]) + dot(ost[at, :], wob[...])).astype(BF)
        mixed_sum.start(n)

    dy_gather.step(4)

    @pl.loop(0, 4)
    def _(i):
        at = rows_at(i, 512)
        dy = dya[at, :]
        dcat[at, 256:512] = (dot_nt(dy, wd2[...]) * dge[at, :]).astype(BF)
        dost[pl.ds(i * 8, 8)] = dot_nt(dy, wob[...]).astype(BF).reshape(8, 64, HD)

    mixed_sum.step(0)
    mixed_sum.step(2)
    mixed_sum.step(1)
    mixed_sum.step(3)

    gdacc[...] = jnp.zeros_like(gdacc)

    @pl.loop(0, 4)
    def _(i):
        at = rows_at(i, 512)
        gdacc[0:256, :] += dot_tn(act[at, :], dya[at, :])
        gdacc[256:320, :] += dot_tn(ost[at, :], dya[at, :])

    gdsend[...] = gdacc[0:256, :].astype(BF)
    gosend[...] = gdacc[256:320, :]
    gdrecv[rows_at(y, 64), :] = gdsend[rows_at(y, 64), :]
    gorecv[rows_at(y, 16), :] = gosend[rows_at(y, 16), :]
    column_start(3, gdsend, gdrecv, 32)
    column_start(4, gosend, gorecv, 8)

    def column_sum(low):
        def add(i, total):
            return total + jnp.sum(dcat[rows_at(i, QB), low : low + 256].astype(F32), axis=0, keepdims=True)

        return lax.fori_loop(0, 8, add, jnp.zeros((1, 256), F32))

    def to_flat(line, values):
        for k in range(values.shape[1] // 128):
            flat[line + k : line + k + 1, :] = values[:, k * 128 : k * 128 + 128]

    def hand_out(gt, raw, sums, k, send):
        for i in range(4):
            at = slice(i * 256, i * 256 + 256)
            grad = gt[0:256, at].T
            gain = jnp.sum(grad * raw[at, :], axis=1, keepdims=True)
            shift = jnp.sum(sums * raw[at, :], axis=1, keepdims=True)
            lane = iota((256, 128), 1)
            spread = jnp.where(lane == 0, gain, jnp.where(lane == 1, shift, 0.0)).T
            to_flat(k * 8 + i * 2, spread[0:1, :])
            to_flat(k * 8 + 8 + i * 2, spread[1:2, :])
            grad = grad * cols[at, k : k + 1] + cols[at, k + 1 : k + 2] * sums
            for m in range(8):
                for h in range(2):
                    place = m * 128 + i * 32 + h * 16
                    first, second = (h * 2) * 64 + m * 8, (h * 2 + 1) * 64 + m * 8
                    send[place : place + 16, :] = jnp.concatenate(
                        [grad[first : first + 8, :], grad[second : second + 8, :]], axis=0
                    ).astype(BF)
    def to_owners(total, total_ref, final, k):
        total_ref[...] = total
        final[rows_at(s, 8), :] = total_ref[rows_at(s, 8), :]

        @pl.loop(1, SEQ)
        def _(j):
            peer = lax.rem(s + j, SEQ)
            seq_copy(j, k, total_ref.at[rows_at(peer, 8)], final.at[rows_at(s, 8)]).start()

    gtu[...] = jnp.zeros_like(gtu)

    @pl.loop(0, 4)
    def _(i):
        at = rows_at(i, 512)
        gtu[...] += dot_tn(dcat[at, 256:512], nrm[at, :])

    sum_u = column_sum(256)
    mixed_sum.step(4)
    hand_out(gtu, rawu, sum_u, 2, gusend)
    gurecv[rows_at(y, 256), :] = gusend[rows_at(y, 256), :]
    column_start(5, gusend, gurecv, 128)


    @pl.loop(0, 8)
    def _(i):
        at = rows_at(i, QB)
        grads = blocks_of(dost, inv_ref, i).astype(F32)
        past = osort[pl.ds(i * 4, 4)].reshape(QB, HD)
        delta = jnp.sum(grads * past, axis=1, keepdims=True)
        wide = jnp.concatenate([grads, jnp.zeros((QB, 64), F32)], axis=1)
        wide = with_lanes(wide, 64, pieces_of(-delta)).astype(BF)
        doa[at, :] = wide
        doat[:, at] = wide.T[0:64, :]

    dkt[...] = jnp.zeros_like(dkt)
    dvt[...] = jnp.zeros_like(dvt)

    mixed_sum.step(5)

    @pl.loop(0, ROW // AB)
    def _(i):
        at = rows_at(i, AB)

        def step(j, dq, masked):
            k_at = rows_at(j, AB)
            probs = jnp.exp(dot(qa[at, :], kat[:, k_at]))
            if masked:
                probs = jnp.where(lower, probs, 0.0)
            grads = (probs * dot(doa[at, :], vat[:, k_at])).astype(BF)
            dkt[:, k_at] += dot(qat[:, at], grads)
            dvt[:, k_at] += dot(doat[:, at], probs.astype(BF))
            return dq + dot(grads, ka[k_at, :])

        dq = lax.fori_loop(0, i, lambda j, dq: step(j, dq, False), jnp.zeros((AB, 128), F32))
        dqs[at, :] = step(i, dq, True) * 0.125

    mixed_sum.step(6)
    column_sums(3, gdrecv, gdpair, gdland, 32)
    column_sums(4, gorecv, gopair, goland, 8)
    column_sums(5, gurecv, gupair, guland, 128)

    @pl.loop(0, 8)
    def _(i):
        at = rows_at(i, QB)
        both = jnp.concatenate([dqs[at, 0:64], dkt[:, at].T], axis=1)
        both = both * tabc[at, :] - partner_of(both) * tabs[at, :]
        last = jnp.concatenate([dvt[:, at].T, jnp.zeros((QB, 64), F32)], axis=1)
        whole = jnp.concatenate([both, last], axis=1).astype(BF)
        dsort[pl.ds(i * 4, 4)] = whole.reshape(4, 64, 256)

    @pl.loop(0, 8)
    def _(j):
        dcat[rows_at(j, QB), 0:256] = blocks_of(dsort, order_ref, j)

    for n in range(8):
        at = dn_sum.chip(n)
        part_d[at, :] = dot_nt(dcat[at, :], wcat[...]).astype(BF)
        dn_sum.start(n)
        if n == 3:
            dn_sum.step(0)

    dn_sum.step(2)

    gtq[...] = jnp.zeros_like(gtq)

    def add_gtq(i):
        at = rows_at(i, 512)
        gtq[...] += dot_tn(dcat[at, 0:256], nrm[at, :])

    pl.loop(0, 2)(add_gtq)
    dn_sum.step(1)
    dn_sum.step(3)
    pl.loop(2, 4)(add_gtq)

    sum_q = column_sum(0)
    dn_sum.step(4)
    hand_out(gtq, rawq, sum_q, 0, gqsend)
    gqrecv[rows_at(b, 128), :] = gqsend[rows_at(b, 128), :]

    @pl.loop(1, BATCH)
    def _(j):
        peer = lax.rem(b + j, BATCH)
        batch_copy(j, 6, gqsend.at[rows_at(peer, 128)], gqrecv.at[rows_at(b, 128)]).start()

    to_owners(pair_sum(5, gupair, guland, 128), gusum, gufin, 1)
    def low_half(part_of):
        return jnp.concatenate([part_of[:, 0:64], jnp.zeros((1, 64), F32)], axis=1)

    flat[32:56, :] = jnp.zeros((24, 128), F32)
    flat[64:96, :] = jnp.zeros((32, 128), F32)
    flat[104:112, :] = jnp.zeros((8, 128), F32)
    upper = lax.rem(s, 2) == 1
    spans = (sum_q[:, 0:128], pltpu.roll(sum_q[:, 0:128], 64, 1), sum_q[:, 128:256])
    for k in range(3):
        mine = low_half(spans[k])
        mine = jnp.where(upper, pltpu.roll(mine, 64, 1), mine)
        flat[pl.ds(32 + k * 8 + s // 2, 1), :] = mine
    flat[pl.ds(64 + 2 * s, 1), :] = sum_u[:, 0:128]
    flat[pl.ds(65 + 2 * s, 1), :] = sum_u[:, 128:256]
    dy_total = jnp.sum(dy_ref[...].astype(F32), axis=0, keepdims=True)
    to_flat(56, dy_total)
    to_flat(96, dy_total)
    for k in range(SEQ):
        fsend[k * 8 : k * 8 + 8, :] = flat[13 * k // 2 : 13 * k // 2 + 8, :]
    frecv[rows_at(s, 8), :] = fsend[rows_at(s, 8), :]

    @pl.loop(1, SEQ)
    def _(j):
        peer = lax.rem(s + j, SEQ)
        seq_copy(j, 3, fsend.at[rows_at(peer, 8)], frecv.at[rows_at(s, 8)]).start()

    dn_sum.step(5)
    dn_sum.step(6)
    batch_all(6, gqrecv, 128).wait_recv()
    total = gqrecv[0:128, :].astype(F32)
    for k in range(1, BATCH):
        total = total + gqrecv[k * 128 : k * 128 + 128, :].astype(F32)
    to_owners(total, gqsum, gqfin, 2)
    mixed_ref[...] = (mixed_sum.result() + x_ref[...].astype(F32) + drow[...]).astype(BF)
    output(0).start()

    seq_all(3, frecv, 8).wait_recv()

    total = frecv[0:8, :]
    for k in range(1, SEQ):
        total = total + frecv[k * 8 : k * 8 + 8, :]
    fsum[...] = total
    fall[rows_at(b, 8), :] = total

    @pl.loop(1, BATCH)
    def _(j):
        batch_copy(j, 7, fsum, fall.at[rows_at(b, 8)]).start()

    gd_ref[...] = pair_sum(3, gdpair, gdland, 32)
    go_ref[...] = pair_sum(4, gopair, goland, 8)
    output(4).start()
    output(5).start()

    merged = dn_sum.result()
    _, normed, inverse = normed_of()
    grad_norm = inverse * (
        merged
        - jnp.mean(merged, axis=-1, keepdims=True)
        - normed * jnp.mean(merged * normed, axis=-1, keepdims=True)
    )
    gtok_ref[...] = (dy_ref[...].astype(F32) + grad_norm).astype(BF)
    output(1).start()

    seq_all(1, gufin, 8).wait_recv()
    seq_all(2, gqfin, 8).wait_recv()

    batch_all(7, fall, 8).wait_recv()

    output(2).start()
    output(3).start()
    total = fall[0:8, :]
    for k in range(1, BATCH):
        total = total + fall[k * 8 : k * 8 + 8, :]
    small_ref[...] = total
    output(6).start()

    normed_gather.drain()
    dy_gather.drain()
    weight_gather.drain()
    mixed_sum.drain()
    dn_sum.drain()

    for k, ref, count in ((0, wst, 16), (1, gufin, 8), (2, gqfin, 8), (3, frecv, 8), (4, sgot, 16)):
        seq_all(k, ref, count).wait_send()
    for k, ref, count in (
        (0, sall, 16), (1, wd2, 32), (2, wo2, 8), (6, gqrecv, 128), (7, fall, 8),
    ):
        batch_all(k, ref, count).wait_send()
    for k, ref, pair, land, count in (
        (3, gdrecv, gdpair, gdland, 32), (4, gorecv, gopair, goland, 8), (5, gurecv, gupair, guland, 128),
    ):
        column_all(k, ref, count).wait_send()
        pair_copy(k + 5, pair, land, count).wait_send()

    for n in range(7):
        output(n).wait()


def finish(
    mixed_ref, gtok_ref, gu_ref, gq_ref, gd_ref, go_ref, small_ref,
    mixed_out, gtok_out, small_out, qkv_out, out_out, up_out, down_out,
):
    s = lax.axis_index("seq")
    b = lax.axis_index("batch")
    mixed_out[...] = mixed_ref[...]
    gtok_out[...] = gtok_ref[...]
    out_out[...] = go_ref[...]
    down_out[...] = gd_ref[...]
    low = iota((8, 128), 1) < 64
    for k in range(SEQ):
        up_out[:, k * HID : k * HID + HID] = gu_ref[k * 8 : k * 8 + 8, :]
    for k in range(0, SEQ, 2):
        one, two = (gq_ref[n * 8 : n * 8 + 8, 0:128] for n in (k, k + 1))
        one_v, two_v = (gq_ref[n * 8 : n * 8 + 8, 128:256] for n in (k, k + 1))
        at = k * HD
        qkv_out[:, at : at + 128] = jnp.where(low, one, pltpu.roll(two, 64, 1))
        qkv_out[:, D + at : D + at + 128] = jnp.where(low, pltpu.roll(one, 64, 1), two)
        qkv_out[:, 2 * D + at : 2 * D + at + 128] = jnp.where(low, one_v, pltpu.roll(two_v, 64, 1))
    begin = b * PER + lax.rem(s, 2) * 64
    line = begin // 128
    both = jnp.concatenate([small_ref[pl.ds(line, 1), :], small_ref[pl.ds(line + 1, 1), :]], axis=1)
    both = pltpu.roll(jnp.broadcast_to(both, (8, 256)), 256 - lax.rem(begin, 128), 1)
    small_out[...] = both[0:1, 0:PER]


def layer(x, dy, wq, wo, wu, wd, sp, order, lengths):
    vmem = pl.BlockSpec(memory_space=pltpu.VMEM)
    smem = pl.BlockSpec(memory_space=pltpu.SMEM)
    scratch = [
        ((TOK, D), BF), ((TOK, D), BF), ((32, D), F32), ((8, D), F32), ((8, 128), F32),
        ((ROW, D), BF), ((ROW, D), BF), ((16, 128), BF), ((256, 128), BF), ((128, 128), BF),
        ((256, 256), BF), ((256, 256), BF), ((2048, 256), BF),
        ((256, D), BF), ((8, D), F32), ((64, D), F32), ((64, D), BF),
        ((D, 256), F32), ((D, 256), F32), ((D, 128), F32), ((D, 512), BF),
        ((1, 512), F32), ((1, D), F32),
        ((32, 64, 256), F32), ((ROW, HID), BF), ((ROW, HID), F32),
        ((ROW, 128), F32), ((ROW, 128), F32),
        ((ROW, 128), BF), ((ROW, 128), BF), ((ROW, 128), BF),
        ((128, ROW), BF), ((128, ROW), BF), ((64, ROW), BF), ((ROW, 128), BF), ((64, ROW), BF),
        ((32, 64, HD), BF), ((32, 64, HD), F32), ((ROW, HD), BF),
        ((ROW, 512), BF), ((HD, ROW), F32), ((HD, ROW), F32),
        ((32, 64, 256), BF), ((ROW, 128), F32),
        ((ROW, D), BF), ((ROW, D), BF),
        ((1920, D), BF), ((1920, D), BF), ((64, D), BF), ((32, D), BF), ((16, D), F32), ((8, D), F32),
        ((256, 256), BF), ((128, 256), BF),
        ((320, D), F32), ((256, D), F32), ((256, D), F32),
        ((256, D), BF), ((64, D), F32), ((256, D), BF), ((64, D), F32),
        ((D, 256), BF), ((D, 256), BF), ((128, 256), F32), ((128, 256), F32),
        ((D, 256), BF), ((D, 256), BF), ((128, 256), F32), ((128, 256), F32),
        ((112, 128), F32), ((128, 128), F32), ((128, 128), F32), ((8, 128), F32), ((64, 128), F32),
    ]
    shapes = [pltpu.VMEM(shape, dtype) for shape, dtype in scratch]
    shapes += [
        pltpu.SMEM((32,), jnp.int32),
        pltpu.SemaphoreType.DMA((7,)),
        pltpu.SemaphoreType.DMA((3,)), pltpu.SemaphoreType.DMA((3, 17)),
        pltpu.SemaphoreType.DMA((2,)), pltpu.SemaphoreType.DMA((2, 21)),
        pltpu.SemaphoreType.DMA((5,)), pltpu.SemaphoreType.DMA((5,)),
        pltpu.SemaphoreType.DMA((11,)), pltpu.SemaphoreType.DMA((11,)),
    ]
    parts = pl.pallas_call(
        kernel,
        out_shape=(
            jax.ShapeDtypeStruct((TOK, D), BF),
            jax.ShapeDtypeStruct((TOK, D), BF),
            jax.ShapeDtypeStruct((128, 256), F32),
            jax.ShapeDtypeStruct((128, 256), F32),
            jax.ShapeDtypeStruct((32, D), F32),
            jax.ShapeDtypeStruct((8, D), F32),
            jax.ShapeDtypeStruct((8, 128), F32),
        ),
        in_specs=[vmem] * 7 + [smem] * 2,
        out_specs=(pl.BlockSpec(memory_space=pl.ANY),) * 7,
        scratch_shapes=shapes,
        compiler_params=pltpu.CompilerParams(
            collective_id=0, has_side_effects=True, vmem_limit_bytes=62 * 2**20
        ),
    )(x, dy, wq, wo, wu, wd, sp, order, lengths)
    return pl.pallas_call(
        finish,
        out_shape=(
            jax.ShapeDtypeStruct((TOK, D), BF),
            jax.ShapeDtypeStruct((TOK, D), BF),
            jax.ShapeDtypeStruct((1, PER), F32),
            jax.ShapeDtypeStruct((8, 3 * D), F32),
            jax.ShapeDtypeStruct((8, D), F32),
            jax.ShapeDtypeStruct((8, SEQ * HID), F32),
            jax.ShapeDtypeStruct((32, D), F32),
        ),
        in_specs=[vmem] * 7,
        out_specs=(vmem,) * 7,
    )(*parts)


def local(tokens, doc_lengths, block_order, small_params, w_qkv, w_out, w_up, w_down, cotangent):
    mixed, grad_tokens, grad_small, grad_qkv, grad_out, grad_up, grad_down = layer(
        tokens[0], cotangent[0], w_qkv, w_out, w_up, w_down,
        small_params.reshape(1, PER), block_order, doc_lengths,
    )
    return (
        mixed[None], grad_tokens[None], grad_small.reshape(PER), grad_qkv, grad_out, grad_up, grad_down,
    )


def solution(mesh):
    placed = (
        P("batch", "seq", None),
        P("batch", None),
        P(),
        P(("seq", "batch")),
        P(("seq", "batch"), None),
        P(("seq", "batch"), None),
        P(("seq", "batch"), None),
        P(("seq", "batch"), None),
        P("batch", "seq", None),
    )
    return jax.shard_map(
        local,
        mesh=mesh,
        in_specs=placed,
        out_specs=(
            P("batch", "seq", None),
            P("batch", "seq", None),
            P(("seq", "batch")),
            P(("seq", "batch"), None),
            P(("seq", "batch"), None),
            P(("seq", "batch"), None),
            P(("seq", "batch"), None),
        ),
        check_vma=False,
    )
```

```python
import jax
import jax.numpy as jnp
import numpy as np
from jax import lax
from jax.experimental import pallas as pl
from jax.experimental.pallas import tpu as pltpu
from jax.sharding import PartitionSpec as P

HD = 64
ROT = 16
EPS = 1e-05
NEG = -1e30
MESH = pl.DeviceIdType.MESH
BF = jnp.bfloat16
F32 = jnp.float32

SEQ = 16
BATCH = 8
TOK = 128
ROW = SEQ * TOK
D = 1024
HID = 256
PER = 104
QB = 256
AB = 512


def dot(a, b):
    return lax.dot_general(a, b, (((1,), (0,)), ((), ())), preferred_element_type=F32)


def dot_nt(a, b):
    return lax.dot_general(a, b, (((1,), (1,)), ((), ())), preferred_element_type=F32)


def dot_tn(a, b):
    return lax.dot_general(a, b, (((0,), (0,)), ((), ())), preferred_element_type=F32)


def iota(shape, dim):
    return lax.broadcasted_iota(jnp.int32, shape, dim)


def slot(z, x, c):
    return z * 8 + x * 2 + c


def rows_at(index, count):
    return pl.ds(pl.multiple_of(index * count, count), count)


def kernel(
    x_ref, dy_ref, wq_ref, wo_ref, wu_ref, wd_ref, sp_ref, order_ref, len_ref,
    mixed_out, gtok_out, gu_out, gq_out, gd_out, go_out, small_out,
    mixed_ref, gtok_ref, gd_ref, go_ref, small_ref, nrm, dya, ssend, sgot, sall, wsend, wst, wbuf, wd2, wos, wo2, wob, rawq, rawu, cols, wcat, brow, drow,
    prj, act, dge, tabc, tabs, qa, ka, va, kat, vat, qat, doa, doat, dost, osort, ost,
    dcat, dkt, dvt, dsort, dqs,
    part_m, part_d, land_m, land_d, gdpair, gdland, gopair, goland, gupair, guland,
    gdacc, gtq, gtu, gdsend, gosend, gdrecv, gorecv,
    gusend, gurecv, gusum, gufin, gqsend, gqrecv, gqsum, gqfin,
    flat, fsend, frecv, fsum, fall,
    inv_ref, out_ss, ag_ss, ag_rs, rs_ss, rs_rs, sq_ss, sq_rs, bt_ss, bt_rs,
):
    s = lax.axis_index("seq")
    b = lax.axis_index("batch")
    z, x, c = s // 8, lax.rem(s // 2, 4), lax.rem(s, 2)
    xr, xl, xo = lax.rem(x + 1, 4), lax.rem(x + 3, 4), lax.rem(x + 2, 4)
    zo, co = 1 - z, 1 - c
    y, w = b // 2, lax.rem(b, 2)
    yr, yl, yo, wo_ = lax.rem(y + 1, 4), lax.rem(y + 3, 4), lax.rem(y + 2, 4), 1 - w
    right, left = (slot(z, xr, c), b), (slot(z, xl, c), b)
    across, sibling = (slot(zo, x, c), b), (slot(z, x, co), b)

    def remote(src, dst, send, recv, device):
        return pltpu.make_async_remote_copy(
            src_ref=src, dst_ref=dst, send_sem=send, recv_sem=recv,
            device_id=device, device_id_type=MESH,
        )

    barrier = pltpu.get_barrier_semaphore()

    @pl.loop(1, SEQ)
    def _(j):
        pl.semaphore_signal(barrier, inc=1, device_id=(lax.rem(s + j, SEQ), b), device_id_type=MESH)

    @pl.loop(1, BATCH)
    def _(j):
        pl.semaphore_signal(barrier, inc=1, device_id=(s, lax.rem(b + j, BATCH)), device_id_type=MESH)

    def normed_of():
        inputs = x_ref[...].astype(F32)
        centred = inputs - jnp.mean(inputs, axis=-1, keepdims=True)
        inverse = lax.rsqrt(jnp.mean(centred * centred, axis=-1, keepdims=True) + EPS)
        return inputs, centred * inverse, inverse

    nrm[rows_at(s, TOK), :] = normed_of()[1].astype(BF)
    dya[rows_at(s, TOK), :] = dy_ref[...]

    def pair(one, two):
        return jnp.where(iota((8, 128), 1) < 64, one, two)

    small = jnp.concatenate([sp_ref[...].astype(F32), jnp.zeros((1, 128 - PER), F32)], axis=1)
    ssend[...] = jnp.broadcast_to(small, (16, 128)).astype(BF)
    wide_q = wq_ref[...].astype(F32)
    wide_u = wu_ref[...].astype(F32)
    for k in range(SEQ):
        at = slice(k // 2 * 128, k // 2 * 128 + 128)
        q, kk, v = (wide_q[:, n * D : n * D + D][:, at] for n in range(3))
        turned = [pltpu.roll(part_of, 64, 1) for part_of in (q, kk, v)]
        q, kk, v = (q, turned[1], v) if k % 2 == 0 else (turned[0], kk, turned[2])
        low = jnp.concatenate([pair(q, kk), pair(v, jnp.zeros_like(v))], axis=1)
        block = jnp.concatenate([wide_u[:, k * HID : k * HID + HID], low], axis=0)
        wsend[k * 16 : k * 16 + 16, :] = block.astype(BF)

    wst[rows_at(s, 16), :] = wsend[rows_at(s, 16), :]
    sgot[rows_at(s, 16), :] = ssend[...]
    wos[...] = wo_ref[...].astype(F32)
    wd2[rows_at(b, 32), :] = wd_ref[...]
    wo2[rows_at(b, 8), :] = wos[...]

    pl.semaphore_wait(barrier, SEQ - 1 + BATCH - 1)

    def seq_copy(j, k, src, dst):
        return remote(src, dst, sq_ss.at[k], sq_rs.at[k], (lax.rem(s + j, SEQ), b))

    def seq_all(k, ref, count):
        ref = ref.at[pl.ds(0, (SEQ - 1) * count)]
        return seq_copy(1, k, ref, ref)

    def column_copy(j, k, src, dst):
        return remote(src, dst, bt_ss.at[k], bt_rs.at[k], (s, lax.rem(y + j, 4) * 2 + w))

    def column_start(k, send, recv, count):
        @pl.loop(1, 4)
        def _(j):
            peer = lax.rem(y + j, 4)
            column_copy(j, k, send.at[rows_at(peer, 2 * count)], recv.at[rows_at(y, 2 * count)]).start()

    def column_all(k, ref, count):
        ref = ref.at[pl.ds(0, 6 * count)]
        return column_copy(1, k, ref, ref)

    def pair_copy(k, pair, land, count):
        src = pair.at[rows_at(wo_, count)]
        return remote(src, land, bt_ss.at[k], bt_rs.at[k], (s, y * 2 + wo_))

    def column_sums(k, recv, pair, land, count):
        column_all(k, recv, count).wait_recv()
        total = recv[0 : 2 * count, :].astype(F32)
        for n in range(1, 4):
            total = total + recv[2 * n * count : 2 * (n + 1) * count, :].astype(F32)
        pair[...] = total.astype(pair.dtype)
        pair_copy(k + 5, pair, land, count).start()

    def pair_sum(k, pair, land, count):
        pair_copy(k + 5, pair, land, count).wait_recv()
        return pair[rows_at(w, count), :].astype(F32) + land[...].astype(F32)

    def batch_all(k, ref, count):
        ref = ref.at[pl.ds(0, (BATCH - 1) * count)]
        return batch_copy(1, k, ref, ref)

    def batch_copy(j, k, src, dst):
        return remote(src, dst, bt_ss.at[k], bt_rs.at[k], (s, lax.rem(b + j, BATCH)))

    @pl.loop(1, SEQ)
    def _(j):
        peer = lax.rem(s + j, SEQ)
        seq_copy(j, 0, wsend.at[rows_at(peer, 16)], wst.at[rows_at(s, 16)]).start()

    class Gather:
        def __init__(self, buf, k, size, slots, right, left, across, sibling=None):
            self.buf, self.k, self.size = buf, k, size
            own, far, of_left, of_right, far_left, far_right, opposite, far_opposite = slots[0]
            half = size // 2
            self.sends = {
                0: (own, right, 0, size), 1: (own, left, 0, size), 2: (own, across, 0, size),
                4: (far, right, 0, size), 5: (far, left, 0, size),
                7: (of_left, right, 0, half), 8: (of_right, left, half, half),
                11: (far_left, right, 0, half), 12: (far_right, left, half, half),
            }
            self.receives = {
                0: (of_left, 0, size), 1: (of_right, 0, size), 2: (far, 0, size),
                4: (far_left, 0, size), 5: (far_right, 0, size),
                7: (opposite, 0, half), 8: (opposite, half, half),
                11: (far_opposite, 0, half), 12: (far_opposite, half, half),
            }
            if sibling is not None:
                for e, n in ((3, 0), (6, 1), (9, 2), (10, 3), (13, 4), (14, 5), (15, 6), (16, 7)):
                    self.sends[e] = (slots[0][n], sibling, 0, size)
                    self.receives[e] = (slots[1][n], 0, size)

        def copy(self, e, index, device, low, count):
            at = self.buf.at[pl.ds(pl.multiple_of(index * self.size + low, self.size // 2), count)]
            return remote(at, at, ag_ss.at[self.k], ag_rs.at[self.k, e], device)

        def start(self, *events):
            for e in events:
                if e in self.sends:
                    self.copy(e, self.sends[e][0], *self.sends[e][1:]).start()

        def wait(self, *events):
            for e in events:
                if e in self.receives:
                    index, low, count = self.receives[e]
                    self.copy(e, index, self.sends[e][1], low, count).wait_recv()

        def step(self, n):
            if n == 0:
                self.start(0, 1, 2, 3)
            elif n == 1:
                self.wait(2)
                self.start(4, 5, 6)
                self.wait(0)
                self.start(7, 9)
                self.wait(1)
                self.start(8, 10)
            elif n == 2:
                self.wait(4)
                self.start(11, 13)
                self.wait(5)
                self.start(12, 14)
            elif n == 3:
                self.wait(7, 8)
                self.start(15)
                self.wait(11, 12)
                self.start(16)
            else:
                self.wait(3, 6, 9, 10, 13, 14, 15, 16)

        def drain(self):
            sent = self.buf.at[pl.ds(0, sum(what[3] for what in self.sends.values()))]
            remote(sent, sent, ag_ss.at[self.k], ag_rs.at[self.k, 0], right).wait_send()

    def row_slots(core):
        return [slot(p, q, core) for p, q in ((z, x), (zo, x), (z, xl), (z, xr), (zo, xl), (zo, xr), (z, xo), (zo, xo))]

    rows_slots = [q * 2 + p for p, q in ((w, y), (wo_, y), (w, yl), (w, yr), (wo_, yl), (wo_, yr), (w, yo), (wo_, yo))]

    normed_gather = Gather(nrm, 0, TOK, (row_slots(c), row_slots(co)), right, left, across, sibling)
    dy_gather = Gather(dya, 1, TOK, (row_slots(c), row_slots(co)), right, left, across, sibling)
    weight_gather = Gather(
        wbuf, 2, 256, (rows_slots,), (s, yr * 2 + w), (s, yl * 2 + w), (s, y * 2 + wo_)
    )
    @pl.loop(0, 32)
    def _(i):
        place = jnp.int32(0)
        for j in range(32):
            place = place + jnp.where(order_ref[j] == i, j, 0)
        inv_ref[i] = jnp.minimum(place, 31)

    normed_gather.step(0)

    @pl.loop(1, SEQ)
    def _(j):
        seq_copy(j, 4, ssend, sgot.at[rows_at(s, 16)]).start()

    outputs = (
        (mixed_ref, mixed_out), (gtok_ref, gtok_out), (gufin, gu_out), (gqfin, gq_out),
        (gd_ref, gd_out), (go_ref, go_out), (small_ref, small_out),
    )

    def output(n):
        return pltpu.make_async_copy(*outputs[n], out_ss.at[n])

    ends = [len_ref[0, 0]]
    for k in range(1, 4):
        ends.append(ends[-1] + len_ref[0, k])

    def begin_of(where):
        begin = jnp.zeros_like(where)
        for end in ends:
            begin = jnp.maximum(begin, jnp.where(where >= end, end, 0))
        return begin

    def doc_of(where):
        doc = jnp.zeros_like(where)
        for end in ends:
            doc = doc + jnp.where(where >= end, 1, 0)
        return doc

    def partner_of(part):
        lane = lax.rem(iota(part.shape, 1), 64)
        return jnp.where(lane < ROT // 2, pltpu.roll(part, 120, 1), pltpu.roll(part, 8, 1))

    rate = jnp.zeros((1, 128), F32)
    for k in range(ROT // 2):
        value = float(np.float32(10000.0) ** np.float32(-2.0 * k / ROT))
        rate = jnp.where(lax.rem(iota((1, 128), 1), 8) == k, value, rate)

    @pl.loop(0, 8, unroll=2)
    def _(i):
        where = i * QB + iota((QB, 128), 0)
        angle = (where - begin_of(where)).astype(F32) * rate
        lane = lax.rem(iota((QB, 128), 1), 64)
        sine = jnp.sin(angle)
        tabc[rows_at(i, QB), :] = jnp.where(lane < ROT, jnp.cos(angle), 1.0)
        sine = jnp.where(lane < ROT // 2, -sine, sine)
        tabs[rows_at(i, QB), :] = jnp.where(lane < ROT, sine, 0.0)

    normed_gather.step(1)
    seq_all(0, wst, 16).wait_recv()
    seq_all(4, sgot, 16).wait_recv()

    wbuf[rows_at(b, 256), :] = wst[...]
    weight_gather.step(0)
    lines = [sgot[k * 16 : k * 16 + 16, :].astype(F32)[0:1, :] for k in range(SEQ)]
    sall[rows_at(b, 16), :] = jnp.concatenate(lines, axis=0).astype(BF)

    @pl.loop(1, BATCH)
    def _(j):
        batch_copy(j, 0, sall.at[rows_at(b, 16)], sall.at[rows_at(b, 16)]).start()

    weight_gather.step(1)

    batch_all(0, sall, 16).wait_recv()

    def hot_of(line, number):
        low = (lax.rem(line, 16) * BATCH + line // 16) * PER
        return ((low <= number) & (number < low + PER)).astype(F32).astype(BF)

    def place_of(number):
        owner = jnp.floor((number.astype(F32) + 0.5) * (1.0 / PER)).astype(jnp.int32)
        return number - PER * owner

    for k in range(4):
        number = k * D + iota((D, 1), 0)
        found = dot(hot_of(iota((1, 128), 1), number), sall[...])
        found = jnp.where(iota((D, 128), 1) == place_of(number), found, 0.0)
        cols[:, k : k + 1] = jnp.sum(found, axis=1, keepdims=True)

    def small_row(number):
        found = dot_tn(sall[...], hot_of(iota((128, 1), 0), number))
        found = jnp.where(iota((128, number.shape[1]), 0) == place_of(number), found, 0.0)
        return jnp.sum(found, axis=0, keepdims=True)

    lane = iota((1, 256), 1)
    number_q = 4 * D + (lane // 64) * D + s * 64 + lax.rem(lane, 64)
    bias_q = small_row(jnp.where(lane < 192, number_q, -1000))
    bias_u = small_row(8 * D + s * HID + lane)
    wide = iota((1, D), 1)
    drow[...] = small_row(7 * D + wide) + small_row(12 * D + wide)

    dy_gather.start(2)
    weight_gather.step(2)
    normed_gather.step(2)
    dy_gather.start(0, 1)
    weight_gather.step(3)

    @pl.loop(0, SEQ)
    def _(i):
        for j in range(BATCH):
            block = wbuf[pl.ds(pl.multiple_of(j * 256 + i * 16, 16), 16), :].astype(F32)
            at = pl.ds(pl.multiple_of(i * 64 + j * 8, 8), 8)
            rawu[at, :] = block[0:8, :]
            rawq[at, :] = block[8:16, :]

    row_q, row_u = bias_q, bias_u
    for i in range(8):
        at = slice(i * 128, i * 128 + 128)
        wq, wu = rawq[at, :], rawu[at, :]
        wcat[at, 0:256] = (wq * cols[at, 0:1]).astype(BF)
        wcat[at, 256:512] = (wu * cols[at, 2:3]).astype(BF)
        row_q = row_q + jnp.sum(wq * cols[at, 1:2], axis=0, keepdims=True)
        row_u = row_u + jnp.sum(wu * cols[at, 3:4], axis=0, keepdims=True)
    brow[:, 0:256] = row_q
    brow[:, 256:512] = row_u

    normed_gather.step(3)
    dy_gather.wait(2)
    dy_gather.start(4, 5, 3, 6)
    normed_gather.step(4)

    @pl.loop(0, 4, unroll=4)
    def _(i):
        out = dot(nrm[rows_at(i, 512), :], wcat[:, 0:256]) + brow[:, 0:256]
        prj[pl.ds(i * 8, 8)] = out.reshape(8, 64, 256)

    @pl.loop(1, BATCH)
    def _(j):
        batch_copy(j, 1, wd_ref, wd2.at[rows_at(b, 32)]).start()
        batch_copy(j, 2, wos, wo2.at[rows_at(b, 8)]).start()

    def pieces_of(value):
        high = value.astype(BF).astype(F32)
        mid = (value - high).astype(BF).astype(F32)
        return high, mid, value - high - mid

    def with_lanes(base, first, values):
        lane = iota(base.shape, 1)
        for k, value in enumerate(values):
            base = jnp.where(lane == first + k, value, base)
        return base

    def blocks_of(ref, order, i):
        return jnp.concatenate([ref[order[i * 4 + k]] for k in range(4)], axis=0)

    @pl.loop(0, 8, unroll=4)
    def _(i):
        at = rows_at(i, QB)
        come = blocks_of(prj, inv_ref, i)
        both = come[:, 0:128]
        both = both * tabc[at, :] + partner_of(both) * tabs[at, :]
        lane = iota((QB, 128), 1)
        own = doc_of(i * QB + iota((QB, 128), 0)) == lane - 64
        front = lane < 64
        query = jnp.where(front, both * 0.125, jnp.where(own | (lane >= 68), 0.0, NEG)).astype(BF)
        tail = jnp.where(lane < 68, own.astype(F32), (lane < 71).astype(F32))
        key = jnp.where(front, pltpu.roll(both, 64, 1), tail).astype(BF)
        value = jnp.where(front, come[:, 128:256], (lane < 67).astype(F32)).astype(BF)
        qa[at, :], ka[at, :], va[at, :] = query, key, value
        qat[:, at] = query.T[0:64, :]
        kat[:, at] = key.T
        vat[:, at] = value.T

    dy_gather.wait(0)
    dy_gather.start(7)
    dy_gather.wait(1)
    dy_gather.start(8)

    lower = iota((AB, AB), 1) <= iota((AB, AB), 0)

    def attend(i):
        at = rows_at(i, AB)

        def step(j, carry, masked):
            top, total = carry
            k_at = rows_at(j, AB)
            scores = dot(qa[at, :], kat[:, k_at])
            if masked:
                scores = jnp.where(lower, scores, NEG)
            peak = jnp.maximum(top, jnp.max(scores, axis=1, keepdims=True))
            expos = jnp.exp(scores - peak).astype(BF)
            return peak, total * jnp.exp(top - peak) + dot(expos, va[k_at, :])

        carry = (jnp.full((AB, 1), NEG, F32), jnp.zeros((AB, 128), F32))
        for j in range(i + 1):
            carry = step(j, carry, j == i)
        top, total = carry
        norm = total[:, 64:65]
        osort[pl.ds(i * (AB // 64), AB // 64)] = (total / norm)[:, 0:64].reshape(AB // 64, 64, HD)
        qa[at, :] = with_lanes(qa[at, :].astype(F32), 68, pieces_of(-(top + jnp.log(norm)))).astype(BF)

    for i in range(3):
        attend(i)
    dy_gather.wait(4)
    dy_gather.start(11)
    dy_gather.wait(5)
    dy_gather.start(12, 9, 10)
    attend(3)

    @pl.loop(0, 4, unroll=4)
    def _(i):
        at = rows_at(i, 512)
        hidden = dot(nrm[at, :], wcat[:, 256:512]) + brow[:, 256:512]
        share = 0.5 * (1.0 + lax.erf(hidden * (2.0**-0.5)))
        act[at, :] = (hidden * share).astype(BF)
        dge[at, :] = share + hidden * jnp.exp(-0.5 * hidden * hidden) * ((2.0 * np.pi) ** -0.5)

    dy_gather.wait(7, 8, 11, 12)
    dy_gather.start(13, 14, 15, 16)

    @pl.loop(0, 8)
    def _(j):
        ost[rows_at(j, QB), :] = blocks_of(osort, order_ref, j).astype(BF)

    batch_all(1, wd2, 32).wait_recv()
    batch_all(2, wo2, 8).wait_recv()

    wob[...] = wo2[...].astype(BF)

    class Scatter:
        def __init__(self, part, land, k):
            self.part, self.land, self.k = part, land, k
            self.order = [(zo, xo), (zo, xr), (zo, xl), (zo, x), (z, xo), (z, xr), (z, xl), (z, x)]
            table = [(n, co, 0, TOK, sibling, None) for n in range(8)]
            for g in (0, 4):
                table += [
                    (g, c, 0, 64, left, g + 2), (g, c, 64, 64, right, g + 1),
                    (g + 1, c, 0, 64, right, g + 3), (g + 2, c, 64, 64, left, g + 3),
                    (g + 1, c, 64, 64, right, g + 3), (g + 2, c, 0, 64, left, g + 3),
                ]
            table += [(3, c, 0, TOK, across, 7)]
            self.table, self.begin, at = table, [], 0
            for entry in table:
                self.begin.append(at)
                at += entry[3]

        def at(self, n, core, low, count):
            zz, xx = self.order[n]
            return pl.ds(pl.multiple_of(slot(zz, xx, core) * TOK + low, 16), count)

        def copy(self, e, src, dst, device):
            return remote(src, dst, rs_ss.at[self.k], rs_rs.at[self.k, e], device)

        def out(self, e):
            n, core, low, count, device, _ = self.table[e]
            return self.part.at[self.at(n, core, low, count)], self.land.at[pl.ds(self.begin[e], count)], device

        def start(self, *events):
            for e in events:
                self.copy(e, *self.out(e)).start()

        def wait(self, e):
            src, dst, device = self.out(e)
            self.copy(e, dst, dst, device).wait_recv()

        def landed(self, e):
            self.wait(e)
            return self.land[self.begin[e] : self.begin[e] + self.table[e][3], :].astype(F32)

        def add(self, *events):
            for e in events:
                n, core, low, count, _, to = self.table[e]
                to = e if e < 8 else to
                at = self.at(to, c, low, count)
                self.part[at, :] = (self.part[at, :].astype(F32) + self.landed(e)).astype(BF)

        def step(self, n):
            if n == 0 or n == 1:
                self.add(4 * n)
                self.start(8 + 6 * n, 9 + 6 * n)
            elif n == 2 or n == 3:
                g = n - 2
                self.add(4 * g + 1, 4 * g + 2)
                self.start(10 + 6 * g, 11 + 6 * g)
                self.add(4 * g + 3)
            elif n == 4 or n == 5:
                g = n - 4
                self.add(8 + 6 * g, 9 + 6 * g)
                self.start(12 + 6 * g, 13 + 6 * g)
            else:
                self.add(10, 11, 12, 13)
                self.start(20)

        def result(self):
            total = self.part[self.at(7, c, 0, TOK), :].astype(F32)
            low = total[0:64, :] + self.landed(16) + self.landed(19)
            high = total[64:TOK, :] + self.landed(17) + self.landed(18)
            return jnp.concatenate([low, high], axis=0) + self.landed(20)

        def drain(self):
            sent = self.part.at[pl.ds(0, sum(entry[3] for entry in self.table))]
            self.copy(0, sent, sent, sibling).wait_send()

    mixed_sum = Scatter(part_m, land_m, 0)
    dn_sum = Scatter(part_d, land_d, 1)

    def halves_of(which):
        return [(which, xo // 2), (which, 1 - xo // 2)]

    for which, side in halves_of(zo) + halves_of(z):
        at = rows_at(which * 2 + side, 512)
        part_m[at, :] = (dot(act[at, :], wd2[...]) + dot(ost[at, :], wob[...])).astype(BF)
    for n in range(8):
        mixed_sum.start(n)

    dy_gather.step(4)

    @pl.loop(0, 4, unroll=4)
    def _(i):
        at = rows_at(i, 512)
        dy = dya[at, :]
        dcat[at, 256:512] = (dot_nt(dy, wd2[...]) * dge[at, :]).astype(BF)
        dost[pl.ds(i * 8, 8)] = dot_nt(dy, wob[...]).astype(BF).reshape(8, 64, HD)

    mixed_sum.step(0)
    mixed_sum.step(2)
    mixed_sum.step(1)
    mixed_sum.step(3)

    gdacc[...] = jnp.zeros_like(gdacc)

    @pl.loop(0, 2, unroll=2)
    def _(i):
        at = rows_at(i, 1024)
        gdacc[0:256, :] += dot_tn(act[at, :], dya[at, :])
        gdacc[256:320, :] += dot_tn(ost[at, :], dya[at, :])

    gdsend[...] = gdacc[0:256, :].astype(BF)
    gosend[...] = gdacc[256:320, :]
    gdrecv[rows_at(y, 64), :] = gdsend[rows_at(y, 64), :]
    gorecv[rows_at(y, 16), :] = gosend[rows_at(y, 16), :]
    column_start(3, gdsend, gdrecv, 32)
    column_start(4, gosend, gorecv, 8)

    def column_sum(low):
        def add(i, total):
            return total + jnp.sum(dcat[rows_at(i, QB), low : low + 256].astype(F32), axis=0, keepdims=True)

        return lax.fori_loop(0, 8, add, jnp.zeros((1, 256), F32))

    def to_flat(line, values):
        for k in range(values.shape[1] // 128):
            flat[line + k : line + k + 1, :] = values[:, k * 128 : k * 128 + 128]

    def hand_out(gt, raw, sums, k, send):
        for i in range(4):
            at = slice(i * 256, i * 256 + 256)
            grad = gt[0:256, at].T
            gain = jnp.sum(grad * raw[at, :], axis=1, keepdims=True)
            shift = jnp.sum(sums * raw[at, :], axis=1, keepdims=True)
            lane = iota((256, 128), 1)
            spread = jnp.where(lane == 0, gain, jnp.where(lane == 1, shift, 0.0)).T
            to_flat(k * 8 + i * 2, spread[0:1, :])
            to_flat(k * 8 + 8 + i * 2, spread[1:2, :])
            grad = grad * cols[at, k : k + 1] + cols[at, k + 1 : k + 2] * sums
            for m in range(8):
                for h in range(2):
                    place = m * 128 + i * 32 + h * 16
                    first, second = (h * 2) * 64 + m * 8, (h * 2 + 1) * 64 + m * 8
                    send[place : place + 16, :] = jnp.concatenate(
                        [grad[first : first + 8, :], grad[second : second + 8, :]], axis=0
                    ).astype(BF)
    def to_owners(total, total_ref, final, k):
        total_ref[...] = total
        final[rows_at(s, 8), :] = total_ref[rows_at(s, 8), :]

        @pl.loop(1, SEQ)
        def _(j):
            peer = lax.rem(s + j, SEQ)
            seq_copy(j, k, total_ref.at[rows_at(peer, 8)], final.at[rows_at(s, 8)]).start()

    gtu[...] = jnp.zeros_like(gtu)

    @pl.loop(0, 2, unroll=2)
    def _(i):
        at = rows_at(i, 1024)
        gtu[...] += dot_tn(dcat[at, 256:512], nrm[at, :])

    sum_u = column_sum(256)
    mixed_sum.step(4)
    hand_out(gtu, rawu, sum_u, 2, gusend)
    gurecv[rows_at(y, 256), :] = gusend[rows_at(y, 256), :]
    column_start(5, gusend, gurecv, 128)


    @pl.loop(0, 8, unroll=4)
    def _(i):
        at = rows_at(i, QB)
        grads = blocks_of(dost, inv_ref, i).astype(F32)
        past = osort[pl.ds(i * 4, 4)].reshape(QB, HD)
        delta = jnp.sum(grads * past, axis=1, keepdims=True)
        wide = jnp.concatenate([grads, jnp.zeros((QB, 64), F32)], axis=1)
        wide = with_lanes(wide, 64, pieces_of(-delta)).astype(BF)
        doa[at, :] = wide
        doat[:, at] = wide.T[0:64, :]

    dkt[...] = jnp.zeros_like(dkt)
    dvt[...] = jnp.zeros_like(dvt)

    def attend_back(i):
        at = rows_at(i, AB)

        def step(j, dq, masked):
            k_at = rows_at(j, AB)
            probs = jnp.exp(dot(qa[at, :], kat[:, k_at]))
            if masked:
                probs = jnp.where(lower, probs, 0.0)
            grads = (probs * dot(doa[at, :], vat[:, k_at])).astype(BF)
            dkt[:, k_at] += dot(qat[:, at], grads)
            dvt[:, k_at] += dot(doat[:, at], probs.astype(BF))
            return dq + dot(grads, ka[k_at, :])

        dq = jnp.zeros((AB, 128), F32)
        for j in range(i + 1):
            dq = step(j, dq, j == i)
        dqs[at, :] = dq * 0.125

    for i in range(ROW // AB):
        attend_back(i)

    mixed_sum.step(6)
    mixed_sum.step(5)
    column_sums(3, gdrecv, gdpair, gdland, 32)
    column_sums(4, gorecv, gopair, goland, 8)

    @pl.loop(0, 8, unroll=4)
    def _(i):
        at = rows_at(i, QB)
        both = jnp.concatenate([dqs[at, 0:64], dkt[:, at].T], axis=1)
        both = both * tabc[at, :] - partner_of(both) * tabs[at, :]
        last = jnp.concatenate([dvt[:, at].T, jnp.zeros((QB, 64), F32)], axis=1)
        whole = jnp.concatenate([both, last], axis=1).astype(BF)
        dsort[pl.ds(i * 4, 4)] = whole.reshape(4, 64, 256)

    @pl.loop(0, 8)
    def _(j):
        dcat[rows_at(j, QB), 0:256] = blocks_of(dsort, order_ref, j)

    for k, (which, side) in enumerate(halves_of(zo) + halves_of(z)):
        at = rows_at(which * 2 + side, 512)
        part_d[at, :] = dot_nt(dcat[at, :], wcat[...]).astype(BF)
        if k == 0:
            dn_sum.start(0)
        elif k == 1:
            dn_sum.start(1, 2, 3)
    dn_sum.step(0)
    dn_sum.start(4, 5, 6, 7)
    column_sums(5, gurecv, gupair, guland, 128)

    gtq[...] = jnp.zeros_like(gtq)

    def add_gtq(i):
        at = rows_at(i, 512)
        gtq[...] += dot_tn(dcat[at, 0:256], nrm[at, :])

    pl.loop(0, 2)(add_gtq)
    pl.loop(2, 4)(add_gtq)

    dn_sum.step(2)
    sum_q = column_sum(0)
    dn_sum.step(4)
    hand_out(gtq, rawq, sum_q, 0, gqsend)
    gqrecv[rows_at(b, 128), :] = gqsend[rows_at(b, 128), :]

    @pl.loop(1, BATCH)
    def _(j):
        peer = lax.rem(b + j, BATCH)
        batch_copy(j, 6, gqsend.at[rows_at(peer, 128)], gqrecv.at[rows_at(b, 128)]).start()

    dn_sum.step(1)
    dn_sum.step(3)

    to_owners(pair_sum(5, gupair, guland, 128), gusum, gufin, 1)
    def low_half(part_of):
        return jnp.concatenate([part_of[:, 0:64], jnp.zeros((1, 64), F32)], axis=1)

    flat[32:56, :] = jnp.zeros((24, 128), F32)
    flat[64:96, :] = jnp.zeros((32, 128), F32)
    flat[104:112, :] = jnp.zeros((8, 128), F32)
    upper = lax.rem(s, 2) == 1
    spans = (sum_q[:, 0:128], pltpu.roll(sum_q[:, 0:128], 64, 1), sum_q[:, 128:256])
    for k in range(3):
        mine = low_half(spans[k])
        mine = jnp.where(upper, pltpu.roll(mine, 64, 1), mine)
        flat[pl.ds(32 + k * 8 + s // 2, 1), :] = mine
    flat[pl.ds(64 + 2 * s, 1), :] = sum_u[:, 0:128]
    flat[pl.ds(65 + 2 * s, 1), :] = sum_u[:, 128:256]
    dy_total = jnp.sum(dy_ref[...].astype(F32), axis=0, keepdims=True)
    to_flat(56, dy_total)
    to_flat(96, dy_total)
    for k in range(SEQ):
        fsend[k * 8 : k * 8 + 8, :] = flat[13 * k // 2 : 13 * k // 2 + 8, :]
    frecv[rows_at(s, 8), :] = fsend[rows_at(s, 8), :]

    @pl.loop(1, SEQ)
    def _(j):
        peer = lax.rem(s + j, SEQ)
        seq_copy(j, 3, fsend.at[rows_at(peer, 8)], frecv.at[rows_at(s, 8)]).start()

    dn_sum.step(6)
    dn_sum.step(5)
    batch_all(6, gqrecv, 128).wait_recv()
    total = gqrecv[0:128, :].astype(F32)
    for k in range(1, BATCH):
        total = total + gqrecv[k * 128 : k * 128 + 128, :].astype(F32)
    to_owners(total, gqsum, gqfin, 2)
    mixed_ref[...] = (mixed_sum.result() + x_ref[...].astype(F32) + drow[...]).astype(BF)
    output(0).start()

    seq_all(3, frecv, 8).wait_recv()

    total = frecv[0:8, :]
    for k in range(1, SEQ):
        total = total + frecv[k * 8 : k * 8 + 8, :]
    fsum[...] = total
    fall[rows_at(b, 8), :] = total

    @pl.loop(1, BATCH)
    def _(j):
        batch_copy(j, 7, fsum, fall.at[rows_at(b, 8)]).start()

    gd_ref[...] = pair_sum(3, gdpair, gdland, 32)
    go_ref[...] = pair_sum(4, gopair, goland, 8)
    output(4).start()
    output(5).start()

    merged = dn_sum.result()
    _, normed, inverse = normed_of()
    grad_norm = inverse * (
        merged
        - jnp.mean(merged, axis=-1, keepdims=True)
        - normed * jnp.mean(merged * normed, axis=-1, keepdims=True)
    )
    gtok_ref[...] = (dy_ref[...].astype(F32) + grad_norm).astype(BF)
    output(1).start()

    seq_all(1, gufin, 8).wait_recv()
    seq_all(2, gqfin, 8).wait_recv()

    batch_all(7, fall, 8).wait_recv()

    output(2).start()
    output(3).start()
    total = fall[0:8, :]
    for k in range(1, BATCH):
        total = total + fall[k * 8 : k * 8 + 8, :]
    small_ref[...] = total
    output(6).start()

    normed_gather.drain()
    dy_gather.drain()
    weight_gather.drain()
    mixed_sum.drain()
    dn_sum.drain()

    for k, ref, count in ((0, wst, 16), (1, gufin, 8), (2, gqfin, 8), (3, frecv, 8), (4, sgot, 16)):
        seq_all(k, ref, count).wait_send()
    for k, ref, count in (
        (0, sall, 16), (1, wd2, 32), (2, wo2, 8), (6, gqrecv, 128), (7, fall, 8),
    ):
        batch_all(k, ref, count).wait_send()
    for k, ref, pair, land, count in (
        (3, gdrecv, gdpair, gdland, 32), (4, gorecv, gopair, goland, 8), (5, gurecv, gupair, guland, 128),
    ):
        column_all(k, ref, count).wait_send()
        pair_copy(k + 5, pair, land, count).wait_send()

    for n in range(7):
        output(n).wait()


def finish(
    mixed_ref, gtok_ref, gu_ref, gq_ref, gd_ref, go_ref, small_ref,
    mixed_out, gtok_out, small_out, qkv_out, out_out, up_out, down_out,
):
    s = lax.axis_index("seq")
    b = lax.axis_index("batch")
    mixed_out[...] = mixed_ref[...]
    gtok_out[...] = gtok_ref[...]
    out_out[...] = go_ref[...]
    down_out[...] = gd_ref[...]
    low = iota((8, 128), 1) < 64
    for k in range(SEQ):
        up_out[:, k * HID : k * HID + HID] = gu_ref[k * 8 : k * 8 + 8, :]
    for k in range(0, SEQ, 2):
        one, two = (gq_ref[n * 8 : n * 8 + 8, 0:128] for n in (k, k + 1))
        one_v, two_v = (gq_ref[n * 8 : n * 8 + 8, 128:256] for n in (k, k + 1))
        at = k * HD
        qkv_out[:, at : at + 128] = jnp.where(low, one, pltpu.roll(two, 64, 1))
        qkv_out[:, D + at : D + at + 128] = jnp.where(low, pltpu.roll(one, 64, 1), two)
        qkv_out[:, 2 * D + at : 2 * D + at + 128] = jnp.where(low, one_v, pltpu.roll(two_v, 64, 1))
    begin = b * PER + lax.rem(s, 2) * 64
    line = begin // 128
    both = jnp.concatenate([small_ref[pl.ds(line, 1), :], small_ref[pl.ds(line + 1, 1), :]], axis=1)
    both = pltpu.roll(jnp.broadcast_to(both, (8, 256)), 256 - lax.rem(begin, 128), 1)
    small_out[...] = both[0:1, 0:PER]


def layer(x, dy, wq, wo, wu, wd, sp, order, lengths):
    vmem = pl.BlockSpec(memory_space=pltpu.VMEM)
    smem = pl.BlockSpec(memory_space=pltpu.SMEM)
    scratch = [
        ((TOK, D), BF), ((TOK, D), BF), ((32, D), F32), ((8, D), F32), ((8, 128), F32),
        ((ROW, D), BF), ((ROW, D), BF), ((16, 128), BF), ((256, 128), BF), ((128, 128), BF),
        ((256, 256), BF), ((256, 256), BF), ((2048, 256), BF),
        ((256, D), BF), ((8, D), F32), ((64, D), F32), ((64, D), BF),
        ((D, 256), F32), ((D, 256), F32), ((D, 128), F32), ((D, 512), BF),
        ((1, 512), F32), ((1, D), F32),
        ((32, 64, 256), F32), ((ROW, HID), BF), ((ROW, HID), F32),
        ((ROW, 128), F32), ((ROW, 128), F32),
        ((ROW, 128), BF), ((ROW, 128), BF), ((ROW, 128), BF),
        ((128, ROW), BF), ((128, ROW), BF), ((64, ROW), BF), ((ROW, 128), BF), ((64, ROW), BF),
        ((32, 64, HD), BF), ((32, 64, HD), F32), ((ROW, HD), BF),
        ((ROW, 512), BF), ((HD, ROW), F32), ((HD, ROW), F32),
        ((32, 64, 256), BF), ((ROW, 128), F32),
        ((ROW, D), BF), ((ROW, D), BF),
        ((1920, D), BF), ((1920, D), BF), ((64, D), BF), ((32, D), BF), ((16, D), F32), ((8, D), F32),
        ((256, 256), BF), ((128, 256), BF),
        ((320, D), F32), ((256, D), F32), ((256, D), F32),
        ((256, D), BF), ((64, D), F32), ((256, D), BF), ((64, D), F32),
        ((D, 256), BF), ((D, 256), BF), ((128, 256), F32), ((128, 256), F32),
        ((D, 256), BF), ((D, 256), BF), ((128, 256), F32), ((128, 256), F32),
        ((112, 128), F32), ((128, 128), F32), ((128, 128), F32), ((8, 128), F32), ((64, 128), F32),
    ]
    shapes = [pltpu.VMEM(shape, dtype) for shape, dtype in scratch]
    shapes += [
        pltpu.SMEM((32,), jnp.int32),
        pltpu.SemaphoreType.DMA((7,)),
        pltpu.SemaphoreType.DMA((3,)), pltpu.SemaphoreType.DMA((3, 17)),
        pltpu.SemaphoreType.DMA((2,)), pltpu.SemaphoreType.DMA((2, 21)),
        pltpu.SemaphoreType.DMA((5,)), pltpu.SemaphoreType.DMA((5,)),
        pltpu.SemaphoreType.DMA((11,)), pltpu.SemaphoreType.DMA((11,)),
    ]
    parts = pl.pallas_call(
        kernel,
        out_shape=(
            jax.ShapeDtypeStruct((TOK, D), BF),
            jax.ShapeDtypeStruct((TOK, D), BF),
            jax.ShapeDtypeStruct((128, 256), F32),
            jax.ShapeDtypeStruct((128, 256), F32),
            jax.ShapeDtypeStruct((32, D), F32),
            jax.ShapeDtypeStruct((8, D), F32),
            jax.ShapeDtypeStruct((8, 128), F32),
        ),
        in_specs=[vmem] * 7 + [smem] * 2,
        out_specs=(pl.BlockSpec(memory_space=pl.ANY),) * 7,
        scratch_shapes=shapes,
        compiler_params=pltpu.CompilerParams(
            collective_id=0, has_side_effects=True, vmem_limit_bytes=62 * 2**20
        ),
    )(x, dy, wq, wo, wu, wd, sp, order, lengths)
    return pl.pallas_call(
        finish,
        out_shape=(
            jax.ShapeDtypeStruct((TOK, D), BF),
            jax.ShapeDtypeStruct((TOK, D), BF),
            jax.ShapeDtypeStruct((1, PER), F32),
            jax.ShapeDtypeStruct((8, 3 * D), F32),
            jax.ShapeDtypeStruct((8, D), F32),
            jax.ShapeDtypeStruct((8, SEQ * HID), F32),
            jax.ShapeDtypeStruct((32, D), F32),
        ),
        in_specs=[vmem] * 7,
        out_specs=(vmem,) * 7,
    )(*parts)


def local(tokens, doc_lengths, block_order, small_params, w_qkv, w_out, w_up, w_down, cotangent):
    mixed, grad_tokens, grad_small, grad_qkv, grad_out, grad_up, grad_down = layer(
        tokens[0], cotangent[0], w_qkv, w_out, w_up, w_down,
        small_params.reshape(1, PER), block_order, doc_lengths,
    )
    return (
        mixed[None], grad_tokens[None], grad_small.reshape(PER), grad_qkv, grad_out, grad_up, grad_down,
    )


def solution(mesh):
    placed = (
        P("batch", "seq", None),
        P("batch", None),
        P(),
        P(("seq", "batch")),
        P(("seq", "batch"), None),
        P(("seq", "batch"), None),
        P(("seq", "batch"), None),
        P(("seq", "batch"), None),
        P("batch", "seq", None),
    )
    return jax.shard_map(
        local,
        mesh=mesh,
        in_specs=placed,
        out_specs=(
            P("batch", "seq", None),
            P("batch", "seq", None),
            P(("seq", "batch")),
            P(("seq", "batch"), None),
            P(("seq", "batch"), None),
            P(("seq", "batch"), None),
            P(("seq", "batch"), None),
        ),
        check_vma=False,
    )
```

```python
import jax
import jax.numpy as jnp
import numpy as np
from jax import lax
from jax.experimental import pallas as pl
from jax.experimental.pallas import tpu as pltpu
from jax.sharding import PartitionSpec as P

HD = 64
ROT = 16
EPS = 1e-05
NEG = -1e30
MESH = pl.DeviceIdType.MESH
BF = jnp.bfloat16
F32 = jnp.float32

SEQ = 16
BATCH = 8
TOK = 128
ROW = SEQ * TOK
D = 1024
HID = 256
PER = 104
QB = 256
AB = 512


def dot(a, b):
    return lax.dot_general(a, b, (((1,), (0,)), ((), ())), preferred_element_type=F32)


def dot_nt(a, b):
    return lax.dot_general(a, b, (((1,), (1,)), ((), ())), preferred_element_type=F32)


def dot_tn(a, b):
    return lax.dot_general(a, b, (((0,), (0,)), ((), ())), preferred_element_type=F32)


def iota(shape, dim):
    return lax.broadcasted_iota(jnp.int32, shape, dim)


def slot(z, x, c):
    return z * 8 + x * 2 + c


def rows_at(index, count):
    return pl.ds(pl.multiple_of(index * count, count), count)


def kernel(
    x_ref, dy_ref, wq_ref, wo_ref, wu_ref, wd_ref, sp_ref, order_ref, len_ref,
    mixed_out, gtok_out, gu_out, gq_out, gd_out, go_out, small_out,
    mixed_ref, gtok_ref, gd_ref, go_ref, small_ref, nrm, dya, ssend, sgot, sall, wsend, wst, wbuf, wd2, wos, wo2, wob, rawq, rawu, cols, wcat, brow, drow,
    prj, act, dge, tabc, tabs, qa, ka, va, kat, vat, qat, doa, doat, dost, osort, ost,
    dcat, dkt, dvt, dsort, dqs,
    part_m, part_d, land_m, land_d, gdpair, gdland, gopair, goland, gupair, guland, keptu, keptq,
    gdacc, gtq, gtu, gdsend, gosend, gdrecv, gorecv,
    gusend, gurecv, gusum, gufin, gqsend, gqrecv, gqsum, gqfin,
    flat, fsend, frecv, fsum, fall,
    inv_ref, out_ss, ag_ss, ag_rs, rs_ss, rs_rs, sq_ss, sq_rs, bt_ss, bt_rs,
):
    s = lax.axis_index("seq")
    b = lax.axis_index("batch")
    z, x, c = s // 8, lax.rem(s // 2, 4), lax.rem(s, 2)
    xr, xl, xo = lax.rem(x + 1, 4), lax.rem(x + 3, 4), lax.rem(x + 2, 4)
    zo, co = 1 - z, 1 - c
    y, w = b // 2, lax.rem(b, 2)
    yr, yl, yo, wo_ = lax.rem(y + 1, 4), lax.rem(y + 3, 4), lax.rem(y + 2, 4), 1 - w
    right, left = (slot(z, xr, c), b), (slot(z, xl, c), b)
    across, sibling = (slot(zo, x, c), b), (slot(z, x, co), b)

    def remote(src, dst, send, recv, device):
        return pltpu.make_async_remote_copy(
            src_ref=src, dst_ref=dst, send_sem=send, recv_sem=recv,
            device_id=device, device_id_type=MESH,
        )

    barrier = pltpu.get_barrier_semaphore()

    @pl.loop(1, SEQ)
    def _(j):
        pl.semaphore_signal(barrier, inc=1, device_id=(lax.rem(s + j, SEQ), b), device_id_type=MESH)

    @pl.loop(1, BATCH)
    def _(j):
        pl.semaphore_signal(barrier, inc=1, device_id=(s, lax.rem(b + j, BATCH)), device_id_type=MESH)

    def normed_of():
        inputs = x_ref[...].astype(F32)
        centred = inputs - jnp.mean(inputs, axis=-1, keepdims=True)
        inverse = lax.rsqrt(jnp.mean(centred * centred, axis=-1, keepdims=True) + EPS)
        return inputs, centred * inverse, inverse

    nrm[rows_at(s, TOK), :] = normed_of()[1].astype(BF)
    dya[rows_at(s, TOK), :] = dy_ref[...]

    def pair(one, two):
        return jnp.where(iota((8, 128), 1) < 64, one, two)

    small = jnp.concatenate([sp_ref[...].astype(F32), jnp.zeros((1, 128 - PER), F32)], axis=1)
    ssend[...] = jnp.broadcast_to(small, (16, 128)).astype(BF)
    wide_q = wq_ref[...].astype(F32)
    wide_u = wu_ref[...].astype(F32)
    for k in range(SEQ):
        at = slice(k // 2 * 128, k // 2 * 128 + 128)
        q, kk, v = (wide_q[:, n * D : n * D + D][:, at] for n in range(3))
        turned = [pltpu.roll(part_of, 64, 1) for part_of in (q, kk, v)]
        q, kk, v = (q, turned[1], v) if k % 2 == 0 else (turned[0], kk, turned[2])
        low = jnp.concatenate([pair(q, kk), pair(v, jnp.zeros_like(v))], axis=1)
        block = jnp.concatenate([wide_u[:, k * HID : k * HID + HID], low], axis=0)
        wsend[k * 16 : k * 16 + 16, :] = block.astype(BF)

    wst[rows_at(s, 16), :] = wsend[rows_at(s, 16), :]
    sgot[rows_at(s, 16), :] = ssend[...]
    wos[...] = wo_ref[...].astype(F32)
    wd2[rows_at(b, 32), :] = wd_ref[...]
    wo2[rows_at(b, 8), :] = wos[...]

    pl.semaphore_wait(barrier, SEQ - 1 + BATCH - 1)

    def seq_copy(j, k, src, dst):
        return remote(src, dst, sq_ss.at[k], sq_rs.at[k], (lax.rem(s + j, SEQ), b))

    def seq_all(k, ref, count):
        ref = ref.at[pl.ds(0, (SEQ - 1) * count)]
        return seq_copy(1, k, ref, ref)

    def column_copy(j, k, src, dst):
        return remote(src, dst, bt_ss.at[k], bt_rs.at[k], (s, lax.rem(y + j, 4) * 2 + w))

    def column_start(k, send, recv, count):
        @pl.loop(1, 4)
        def _(j):
            peer = lax.rem(y + j, 4)
            column_copy(j, k, send.at[rows_at(peer, 2 * count)], recv.at[rows_at(y, 2 * count)]).start()

    def column_all(k, ref, count):
        ref = ref.at[pl.ds(0, 6 * count)]
        return column_copy(1, k, ref, ref)

    def pair_copy(k, pair, land, count):
        src = pair.at[rows_at(wo_, count)]
        return remote(src, land, bt_ss.at[k], bt_rs.at[k], (s, y * 2 + wo_))

    def column_sums(k, recv, pair, land, count):
        column_all(k, recv, count).wait_recv()
        total = recv[0 : 2 * count, :].astype(F32)
        for n in range(1, 4):
            total = total + recv[2 * n * count : 2 * (n + 1) * count, :].astype(F32)
        pair[...] = total.astype(pair.dtype)
        pair_copy(k + 5, pair, land, count).start()

    def pair_sum(k, pair, land, count):
        pair_copy(k + 5, pair, land, count).wait_recv()
        return pair[rows_at(w, count), :].astype(F32) + land[...].astype(F32)

    def batch_all(k, ref, count):
        ref = ref.at[pl.ds(0, (BATCH - 1) * count)]
        return batch_copy(1, k, ref, ref)

    def batch_copy(j, k, src, dst):
        return remote(src, dst, bt_ss.at[k], bt_rs.at[k], (s, lax.rem(b + j, BATCH)))

    @pl.loop(1, SEQ)
    def _(j):
        peer = lax.rem(s + j, SEQ)
        seq_copy(j, 0, wsend.at[rows_at(peer, 16)], wst.at[rows_at(s, 16)]).start()

    class Gather:
        def __init__(self, buf, k, size, slots, right, left, across, sibling=None):
            self.buf, self.k, self.size = buf, k, size
            own, far, of_left, of_right, far_left, far_right, opposite, far_opposite = slots[0]
            half = size // 2
            self.sends = {
                0: (own, right, 0, size), 1: (own, left, 0, size), 2: (own, across, 0, size),
                4: (far, right, 0, size), 5: (far, left, 0, size),
                7: (of_left, right, 0, half), 8: (of_right, left, half, half),
                11: (far_left, right, 0, half), 12: (far_right, left, half, half),
            }
            self.receives = {
                0: (of_left, 0, size), 1: (of_right, 0, size), 2: (far, 0, size),
                4: (far_left, 0, size), 5: (far_right, 0, size),
                7: (opposite, 0, half), 8: (opposite, half, half),
                11: (far_opposite, 0, half), 12: (far_opposite, half, half),
            }
            if sibling is not None:
                for e, n in ((3, 0), (6, 1), (9, 2), (10, 3), (13, 4), (14, 5), (15, 6), (16, 7)):
                    self.sends[e] = (slots[0][n], sibling, 0, size)
                    self.receives[e] = (slots[1][n], 0, size)

        def copy(self, e, index, device, low, count):
            at = self.buf.at[pl.ds(pl.multiple_of(index * self.size + low, self.size // 2), count)]
            return remote(at, at, ag_ss.at[self.k], ag_rs.at[self.k, e], device)

        def start(self, *events):
            for e in events:
                if e in self.sends:
                    self.copy(e, self.sends[e][0], *self.sends[e][1:]).start()

        def wait(self, *events):
            for e in events:
                if e in self.receives:
                    index, low, count = self.receives[e]
                    self.copy(e, index, self.sends[e][1], low, count).wait_recv()

        def step(self, n):
            if n == 0:
                self.start(0, 1, 2, 3)
            elif n == 1:
                self.wait(0)
                self.start(7)
                self.wait(1)
                self.start(8)
                self.wait(2)
                self.start(4, 5, 6, 9, 10)
            elif n == 2:
                self.wait(4)
                self.start(11, 13)
                self.wait(5)
                self.start(12, 14)
            elif n == 3:
                self.wait(7, 8)
                self.start(15)
                self.wait(11, 12)
                self.start(16)
            else:
                self.wait(3, 6, 9, 10, 13, 14, 15, 16)

        def drain(self):
            sent = self.buf.at[pl.ds(0, sum(what[3] for what in self.sends.values()))]
            remote(sent, sent, ag_ss.at[self.k], ag_rs.at[self.k, 0], right).wait_send()

    def row_slots(core):
        return [slot(p, q, core) for p, q in ((z, x), (zo, x), (z, xl), (z, xr), (zo, xl), (zo, xr), (z, xo), (zo, xo))]

    rows_slots = [q * 2 + p for p, q in ((w, y), (wo_, y), (w, yl), (w, yr), (wo_, yl), (wo_, yr), (w, yo), (wo_, yo))]

    normed_gather = Gather(nrm, 0, TOK, (row_slots(c), row_slots(co)), right, left, across, sibling)
    dy_gather = Gather(dya, 1, TOK, (row_slots(c), row_slots(co)), right, left, across, sibling)
    weight_gather = Gather(
        wbuf, 2, 256, (rows_slots,), (s, yr * 2 + w), (s, yl * 2 + w), (s, y * 2 + wo_)
    )
    @pl.loop(0, 32)
    def _(i):
        place = jnp.int32(0)
        for j in range(32):
            place = place + jnp.where(order_ref[j] == i, j, 0)
        inv_ref[i] = jnp.minimum(place, 31)

    normed_gather.step(0)

    @pl.loop(1, SEQ)
    def _(j):
        seq_copy(j, 4, ssend, sgot.at[rows_at(s, 16)]).start()

    outputs = (
        (mixed_ref, mixed_out), (gtok_ref, gtok_out), (gufin, gu_out), (gqfin, gq_out),
        (gd_ref, gd_out), (go_ref, go_out), (small_ref, small_out),
    )

    def output(n):
        return pltpu.make_async_copy(*outputs[n], out_ss.at[n])

    ends = [len_ref[0, 0]]
    for k in range(1, 4):
        ends.append(ends[-1] + len_ref[0, k])

    def begin_of(where):
        begin = jnp.zeros_like(where)
        for end in ends:
            begin = jnp.maximum(begin, jnp.where(where >= end, end, 0))
        return begin

    def doc_of(where):
        doc = jnp.zeros_like(where)
        for end in ends:
            doc = doc + jnp.where(where >= end, 1, 0)
        return doc

    def partner_of(part):
        lane = lax.rem(iota(part.shape, 1), 64)
        return jnp.where(lane < ROT // 2, pltpu.roll(part, 120, 1), pltpu.roll(part, 8, 1))

    rate = jnp.zeros((1, 128), F32)
    for k in range(ROT // 2):
        value = float(np.float32(10000.0) ** np.float32(-2.0 * k / ROT))
        rate = jnp.where(lax.rem(iota((1, 128), 1), 8) == k, value, rate)

    @pl.loop(0, 8, unroll=2)
    def _(i):
        where = i * QB + iota((QB, 128), 0)
        angle = (where - begin_of(where)).astype(F32) * rate
        lane = lax.rem(iota((QB, 128), 1), 64)
        sine = jnp.sin(angle)
        tabc[rows_at(i, QB), :] = jnp.where(lane < ROT, jnp.cos(angle), 1.0)
        sine = jnp.where(lane < ROT // 2, -sine, sine)
        tabs[rows_at(i, QB), :] = jnp.where(lane < ROT, sine, 0.0)

    normed_gather.step(1)
    seq_all(0, wst, 16).wait_recv()
    seq_all(4, sgot, 16).wait_recv()

    wbuf[rows_at(b, 256), :] = wst[...]
    weight_gather.step(0)
    lines = [sgot[k * 16 : k * 16 + 16, :].astype(F32)[0:1, :] for k in range(SEQ)]
    sall[rows_at(b, 16), :] = jnp.concatenate(lines, axis=0).astype(BF)

    @pl.loop(1, BATCH)
    def _(j):
        batch_copy(j, 0, sall.at[rows_at(b, 16)], sall.at[rows_at(b, 16)]).start()

    weight_gather.step(1)
    dy_gather.start(2)

    batch_all(0, sall, 16).wait_recv()

    def hot_of(line, number):
        low = (lax.rem(line, 16) * BATCH + line // 16) * PER
        return ((low <= number) & (number < low + PER)).astype(F32).astype(BF)

    def place_of(number):
        owner = jnp.floor((number.astype(F32) + 0.5) * (1.0 / PER)).astype(jnp.int32)
        return number - PER * owner

    for k in range(4):
        number = k * D + iota((D, 1), 0)
        found = dot(hot_of(iota((1, 128), 1), number), sall[...])
        found = jnp.where(iota((D, 128), 1) == place_of(number), found, 0.0)
        cols[:, k : k + 1] = jnp.sum(found, axis=1, keepdims=True)

    def small_row(number):
        found = dot_tn(sall[...], hot_of(iota((128, 1), 0), number))
        found = jnp.where(iota((128, number.shape[1]), 0) == place_of(number), found, 0.0)
        return jnp.sum(found, axis=0, keepdims=True)

    lane = iota((1, 256), 1)
    number_q = 4 * D + (lane // 64) * D + s * 64 + lax.rem(lane, 64)
    bias_q = small_row(jnp.where(lane < 192, number_q, -1000))
    bias_u = small_row(8 * D + s * HID + lane)
    wide = iota((1, D), 1)
    drow[...] = small_row(7 * D + wide) + small_row(12 * D + wide)

    normed_gather.step(2)
    weight_gather.step(2)
    dy_gather.start(0, 1)
    weight_gather.step(3)

    @pl.loop(0, SEQ)
    def _(i):
        for j in range(BATCH):
            block = wbuf[pl.ds(pl.multiple_of(j * 256 + i * 16, 16), 16), :].astype(F32)
            at = pl.ds(pl.multiple_of(i * 64 + j * 8, 8), 8)
            rawu[at, :] = block[0:8, :]
            rawq[at, :] = block[8:16, :]

    row_q, row_u = bias_q, bias_u
    for i in range(8):
        at = slice(i * 128, i * 128 + 128)
        wq, wu = rawq[at, :], rawu[at, :]
        wcat[at, 0:256] = (wq * cols[at, 0:1]).astype(BF)
        wcat[at, 256:512] = (wu * cols[at, 2:3]).astype(BF)
        row_q = row_q + jnp.sum(wq * cols[at, 1:2], axis=0, keepdims=True)
        row_u = row_u + jnp.sum(wu * cols[at, 3:4], axis=0, keepdims=True)
    brow[:, 0:256] = row_q
    brow[:, 256:512] = row_u

    normed_gather.step(3)
    dy_gather.wait(2)
    dy_gather.start(4, 5, 3, 6)
    normed_gather.step(4)

    @pl.loop(0, 4, unroll=4)
    def _(i):
        out = dot(nrm[rows_at(i, 512), :], wcat[:, 0:256]) + brow[:, 0:256]
        prj[pl.ds(i * 8, 8)] = out.reshape(8, 64, 256)

    @pl.loop(1, BATCH)
    def _(j):
        batch_copy(j, 1, wd_ref, wd2.at[rows_at(b, 32)]).start()
        batch_copy(j, 2, wos, wo2.at[rows_at(b, 8)]).start()

    def pieces_of(value):
        high = value.astype(BF).astype(F32)
        mid = (value - high).astype(BF).astype(F32)
        return high, mid, value - high - mid

    def with_lanes(base, first, values):
        lane = iota(base.shape, 1)
        for k, value in enumerate(values):
            base = jnp.where(lane == first + k, value, base)
        return base

    def blocks_of(ref, order, i):
        return jnp.concatenate([ref[order[i * 4 + k]] for k in range(4)], axis=0)

    @pl.loop(0, 8, unroll=4)
    def _(i):
        at = rows_at(i, QB)
        come = blocks_of(prj, inv_ref, i)
        both = come[:, 0:128]
        both = both * tabc[at, :] + partner_of(both) * tabs[at, :]
        lane = iota((QB, 128), 1)
        own = doc_of(i * QB + iota((QB, 128), 0)) == lane - 64
        front = lane < 64
        query = jnp.where(front, both * 0.125, jnp.where(own | (lane >= 68), 0.0, NEG)).astype(BF)
        tail = jnp.where(lane < 68, own.astype(F32), (lane < 71).astype(F32))
        key = jnp.where(front, pltpu.roll(both, 64, 1), tail).astype(BF)
        value = jnp.where(front, come[:, 128:256], (lane < 67).astype(F32)).astype(BF)
        qa[at, :], ka[at, :], va[at, :] = query, key, value
        qat[:, at] = query.T[0:64, :]
        kat[:, at] = key.T
        vat[:, at] = value.T

    dy_gather.wait(0)
    dy_gather.start(7)
    dy_gather.wait(1)
    dy_gather.start(8)

    lower = iota((AB, AB), 1) <= iota((AB, AB), 0)

    def attend(i):
        at = rows_at(i, AB)

        def step(j, carry, masked):
            top, total = carry
            k_at = rows_at(j, AB)
            scores = dot(qa[at, :], kat[:, k_at])
            if masked:
                scores = jnp.where(lower, scores, NEG)
            peak = jnp.maximum(top, jnp.max(scores, axis=1, keepdims=True))
            expos = jnp.exp(scores - peak).astype(BF)
            return peak, total * jnp.exp(top - peak) + dot(expos, va[k_at, :])

        carry = (jnp.full((AB, 1), NEG, F32), jnp.zeros((AB, 128), F32))
        for j in range(i + 1):
            carry = step(j, carry, j == i)
        top, total = carry
        norm = total[:, 64:65]
        osort[pl.ds(i * (AB // 64), AB // 64)] = (total / norm)[:, 0:64].reshape(AB // 64, 64, HD)
        qa[at, :] = with_lanes(qa[at, :].astype(F32), 68, pieces_of(-(top + jnp.log(norm)))).astype(BF)

    for i in range(3):
        attend(i)
    dy_gather.wait(4)
    dy_gather.start(11)
    dy_gather.wait(5)
    dy_gather.start(12, 9, 10)
    attend(3)

    @pl.loop(0, 4, unroll=4)
    def _(i):
        at = rows_at(i, 512)
        hidden = dot(nrm[at, :], wcat[:, 256:512]) + brow[:, 256:512]
        share = 0.5 * (1.0 + lax.erf(hidden * (2.0**-0.5)))
        act[at, :] = (hidden * share).astype(BF)
        dge[at, :] = share + hidden * jnp.exp(-0.5 * hidden * hidden) * ((2.0 * np.pi) ** -0.5)

    dy_gather.wait(7, 8, 11, 12)
    dy_gather.start(13, 14, 15, 16)

    @pl.loop(0, 8)
    def _(j):
        ost[rows_at(j, QB), :] = blocks_of(osort, order_ref, j).astype(BF)

    batch_all(1, wd2, 32).wait_recv()
    batch_all(2, wo2, 8).wait_recv()

    wob[...] = wo2[...].astype(BF)

    class Scatter:
        def __init__(self, part, land, k):
            self.part, self.land, self.k = part, land, k
            self.order = [(zo, xo), (zo, xr), (zo, xl), (zo, x), (z, xo), (z, xr), (z, xl), (z, x)]
            table = [(n, co, 0, TOK, sibling, None) for n in range(8)]
            for g in (0, 4):
                table += [
                    (g, c, 0, 64, left, g + 2), (g, c, 64, 64, right, g + 1),
                    (g + 1, c, 0, 64, right, g + 3), (g + 2, c, 64, 64, left, g + 3),
                    (g + 1, c, 64, 64, right, g + 3), (g + 2, c, 0, 64, left, g + 3),
                ]
            table += [(3, c, 0, TOK, across, 7)]
            self.table, self.begin, at = table, [], 0
            for entry in table:
                self.begin.append(at)
                at += entry[3]

        def at(self, n, core, low, count):
            zz, xx = self.order[n]
            return pl.ds(pl.multiple_of(slot(zz, xx, core) * TOK + low, 16), count)

        def copy(self, e, src, dst, device):
            return remote(src, dst, rs_ss.at[self.k], rs_rs.at[self.k, e], device)

        def out(self, e):
            n, core, low, count, device, _ = self.table[e]
            return self.part.at[self.at(n, core, low, count)], self.land.at[pl.ds(self.begin[e], count)], device

        def start(self, *events):
            for e in events:
                self.copy(e, *self.out(e)).start()

        def wait(self, e):
            src, dst, device = self.out(e)
            self.copy(e, dst, dst, device).wait_recv()

        def landed(self, e):
            self.wait(e)
            return self.land[self.begin[e] : self.begin[e] + self.table[e][3], :].astype(F32)

        def add(self, *events):
            for e in events:
                n, core, low, count, _, to = self.table[e]
                to = e if e < 8 else to
                at = self.at(to, c, low, count)
                self.part[at, :] = (self.part[at, :].astype(F32) + self.landed(e)).astype(BF)

        def step(self, n):
            if n == 0 or n == 1:
                self.add(4 * n)
                self.start(8 + 6 * n, 9 + 6 * n)
            elif n == 2 or n == 3:
                g = n - 2
                self.add(4 * g + 1, 4 * g + 2)
                self.start(10 + 6 * g, 11 + 6 * g)
                self.add(4 * g + 3)
            elif n == 4 or n == 5:
                g = n - 4
                self.add(8 + 6 * g, 9 + 6 * g)
                self.start(12 + 6 * g, 13 + 6 * g)
            else:
                self.add(10, 11, 12, 13)
                self.start(20)

        def result(self):
            total = self.part[self.at(7, c, 0, TOK), :].astype(F32)
            low = total[0:64, :] + self.landed(16) + self.landed(19)
            high = total[64:TOK, :] + self.landed(17) + self.landed(18)
            return jnp.concatenate([low, high], axis=0) + self.landed(20)

        def drain(self):
            sent = self.part.at[pl.ds(0, sum(entry[3] for entry in self.table))]
            self.copy(0, sent, sent, sibling).wait_send()

    mixed_sum = Scatter(part_m, land_m, 0)
    dn_sum = Scatter(part_d, land_d, 1)

    def halves_of(which):
        return [(which, xo // 2), (which, 1 - xo // 2)]

    for k, (which, side) in enumerate(halves_of(zo) + halves_of(z)):
        at = rows_at(which * 2 + side, 512)
        part_m[at, :] = (dot(act[at, :], wd2[...]) + dot(ost[at, :], wob[...])).astype(BF)
        if k == 0:
            mixed_sum.start(0)
        elif k == 1:
            mixed_sum.start(1, 2, 3)
    mixed_sum.step(0)
    mixed_sum.start(4, 5, 6, 7)

    dy_gather.step(4)

    @pl.loop(0, 4, unroll=4)
    def _(i):
        at = rows_at(i, 512)
        dy = dya[at, :]
        dcat[at, 256:512] = (dot_nt(dy, wd2[...]) * dge[at, :]).astype(BF)
        dost[pl.ds(i * 8, 8)] = dot_nt(dy, wob[...]).astype(BF).reshape(8, 64, HD)

    mixed_sum.step(2)

    gdacc[...] = jnp.zeros_like(gdacc)

    @pl.loop(0, 2, unroll=2)
    def _(i):
        at = rows_at(i, 1024)
        gdacc[0:256, :] += dot_tn(act[at, :], dya[at, :])
        gdacc[256:320, :] += dot_tn(ost[at, :], dya[at, :])

    gdsend[...] = gdacc[0:256, :].astype(BF)
    gosend[...] = gdacc[256:320, :]
    gdrecv[rows_at(y, 64), :] = gdsend[rows_at(y, 64), :]
    gorecv[rows_at(y, 16), :] = gosend[rows_at(y, 16), :]
    column_start(3, gdsend, gdrecv, 32)
    column_start(4, gosend, gorecv, 8)

    mixed_sum.step(4)
    mixed_sum.step(1)
    mixed_sum.step(3)

    def column_sum(low):
        def add(i, total):
            return total + jnp.sum(dcat[rows_at(i, QB), low : low + 256].astype(F32), axis=0, keepdims=True)

        return lax.fori_loop(0, 8, add, jnp.zeros((1, 256), F32))

    def to_flat(line, values):
        for k in range(values.shape[1] // 128):
            flat[line + k : line + k + 1, :] = values[:, k * 128 : k * 128 + 128]

    def hand_out(gt, kept, sums, k, send):
        for i in range(4):
            at = slice(i * 256, i * 256 + 256)
            grad = gt[0:256, at].T
            kept[at, :] = grad
            grad = grad * cols[at, k : k + 1] + cols[at, k + 1 : k + 2] * sums
            for m in range(8):
                for h in range(2):
                    place = m * 128 + i * 32 + h * 16
                    first, second = (h * 2) * 64 + m * 8, (h * 2 + 1) * 64 + m * 8
                    send[place : place + 16, :] = jnp.concatenate(
                        [grad[first : first + 8, :], grad[second : second + 8, :]], axis=0
                    ).astype(BF)

    def small_sums(kept, raw, sums, k):
        for i in range(4):
            at = slice(i * 256, i * 256 + 256)
            gain = jnp.sum(kept[at, :] * raw[at, :], axis=1, keepdims=True)
            shift = jnp.sum(sums * raw[at, :], axis=1, keepdims=True)
            lane = iota((256, 128), 1)
            spread = jnp.where(lane == 0, gain, jnp.where(lane == 1, shift, 0.0)).T
            to_flat(k * 8 + i * 2, spread[0:1, :])
            to_flat(k * 8 + 8 + i * 2, spread[1:2, :])

    def to_owners(total, total_ref, final, k):
        total_ref[...] = total
        final[rows_at(s, 8), :] = total_ref[rows_at(s, 8), :]

        @pl.loop(1, SEQ)
        def _(j):
            peer = lax.rem(s + j, SEQ)
            seq_copy(j, k, total_ref.at[rows_at(peer, 8)], final.at[rows_at(s, 8)]).start()

    gtu[...] = jnp.zeros_like(gtu)

    @pl.loop(0, 2, unroll=2)
    def _(i):
        at = rows_at(i, 1024)
        gtu[...] += dot_tn(dcat[at, 256:512], nrm[at, :])

    sum_u = column_sum(256)
    hand_out(gtu, keptu, sum_u, 2, gusend)
    gurecv[rows_at(y, 256), :] = gusend[rows_at(y, 256), :]
    column_start(5, gusend, gurecv, 128)


    @pl.loop(0, 8, unroll=4)
    def _(i):
        at = rows_at(i, QB)
        grads = blocks_of(dost, inv_ref, i).astype(F32)
        past = osort[pl.ds(i * 4, 4)].reshape(QB, HD)
        delta = jnp.sum(grads * past, axis=1, keepdims=True)
        wide = jnp.concatenate([grads, jnp.zeros((QB, 64), F32)], axis=1)
        wide = with_lanes(wide, 64, pieces_of(-delta)).astype(BF)
        doa[at, :] = wide
        doat[:, at] = wide.T[0:64, :]

    dkt[...] = jnp.zeros_like(dkt)
    dvt[...] = jnp.zeros_like(dvt)

    def attend_back(i):
        at = rows_at(i, AB)

        def step(j, dq, masked):
            k_at = rows_at(j, AB)
            probs = jnp.exp(dot(qa[at, :], kat[:, k_at]))
            if masked:
                probs = jnp.where(lower, probs, 0.0)
            grads = (probs * dot(doa[at, :], vat[:, k_at])).astype(BF)
            dkt[:, k_at] += dot(qat[:, at], grads)
            dvt[:, k_at] += dot(doat[:, at], probs.astype(BF))
            return dq + dot(grads, ka[k_at, :])

        dq = jnp.zeros((AB, 128), F32)
        for j in range(i + 1):
            dq = step(j, dq, j == i)
        dqs[at, :] = dq * 0.125

    for i in range(ROW // AB):
        attend_back(i)

    mixed_sum.step(6)
    mixed_sum.step(5)

    @pl.loop(0, 8, unroll=4)
    def _(i):
        at = rows_at(i, QB)
        both = jnp.concatenate([dqs[at, 0:64], dkt[:, at].T], axis=1)
        both = both * tabc[at, :] - partner_of(both) * tabs[at, :]
        last = jnp.concatenate([dvt[:, at].T, jnp.zeros((QB, 64), F32)], axis=1)
        whole = jnp.concatenate([both, last], axis=1).astype(BF)
        dsort[pl.ds(i * 4, 4)] = whole.reshape(4, 64, 256)

    @pl.loop(0, 8)
    def _(j):
        dcat[rows_at(j, QB), 0:256] = blocks_of(dsort, order_ref, j)

    def dn_part(which, side):
        at = rows_at(which * 2 + side, 512)
        part_d[at, :] = dot_nt(dcat[at, :], wcat[...]).astype(BF)

    dn_part(*halves_of(zo)[0])
    dn_sum.start(0)
    dn_part(*halves_of(zo)[1])
    dn_sum.start(1, 2, 3)
    dn_sum.step(0)
    gtq[...] = jnp.zeros_like(gtq)

    @pl.loop(0, 2, unroll=2)
    def _(i):
        at = rows_at(i, 1024)
        gtq[...] += dot_tn(dcat[at, 0:256], nrm[at, :])

    dn_sum.step(2)
    sum_q = column_sum(0)
    hand_out(gtq, keptq, sum_q, 0, gqsend)
    gqrecv[rows_at(b, 128), :] = gqsend[rows_at(b, 128), :]

    @pl.loop(1, BATCH)
    def _(j):
        peer = lax.rem(b + j, BATCH)
        batch_copy(j, 6, gqsend.at[rows_at(peer, 128)], gqrecv.at[rows_at(b, 128)]).start()

    column_sums(5, gurecv, gupair, guland, 128)
    dn_sum.step(4)
    for which, side in halves_of(z):
        dn_part(which, side)
    dn_sum.start(4, 5, 6, 7)
    small_sums(keptu, rawu, sum_u, 2)
    small_sums(keptq, rawq, sum_q, 0)

    def low_half(part_of):
        return jnp.concatenate([part_of[:, 0:64], jnp.zeros((1, 64), F32)], axis=1)

    flat[32:56, :] = jnp.zeros((24, 128), F32)
    flat[64:96, :] = jnp.zeros((32, 128), F32)
    flat[104:112, :] = jnp.zeros((8, 128), F32)
    upper = lax.rem(s, 2) == 1
    spans = (sum_q[:, 0:128], pltpu.roll(sum_q[:, 0:128], 64, 1), sum_q[:, 128:256])
    for k in range(3):
        mine = low_half(spans[k])
        mine = jnp.where(upper, pltpu.roll(mine, 64, 1), mine)
        flat[pl.ds(32 + k * 8 + s // 2, 1), :] = mine
    flat[pl.ds(64 + 2 * s, 1), :] = sum_u[:, 0:128]
    flat[pl.ds(65 + 2 * s, 1), :] = sum_u[:, 128:256]
    dy_total = jnp.sum(dy_ref[...].astype(F32), axis=0, keepdims=True)
    to_flat(56, dy_total)
    to_flat(96, dy_total)
    for k in range(SEQ):
        fsend[k * 8 : k * 8 + 8, :] = flat[13 * k // 2 : 13 * k // 2 + 8, :]
    frecv[rows_at(s, 8), :] = fsend[rows_at(s, 8), :]

    @pl.loop(1, SEQ)
    def _(j):
        peer = lax.rem(s + j, SEQ)
        seq_copy(j, 3, fsend.at[rows_at(peer, 8)], frecv.at[rows_at(s, 8)]).start()

    column_sums(3, gdrecv, gdpair, gdland, 32)
    column_sums(4, gorecv, gopair, goland, 8)
    dn_sum.step(1)
    dn_sum.step(3)

    dn_sum.step(6)
    to_owners(pair_sum(5, gupair, guland, 128), gusum, gufin, 1)
    batch_all(6, gqrecv, 128).wait_recv()
    total = gqrecv[0:128, :].astype(F32)
    for k in range(1, BATCH):
        total = total + gqrecv[k * 128 : k * 128 + 128, :].astype(F32)
    to_owners(total, gqsum, gqfin, 2)
    dn_sum.step(5)
    mixed_ref[...] = (mixed_sum.result() + x_ref[...].astype(F32) + drow[...]).astype(BF)
    output(0).start()

    seq_all(3, frecv, 8).wait_recv()

    total = frecv[0:8, :]
    for k in range(1, SEQ):
        total = total + frecv[k * 8 : k * 8 + 8, :]
    fsum[...] = total
    fall[rows_at(b, 8), :] = total

    @pl.loop(1, BATCH)
    def _(j):
        batch_copy(j, 7, fsum, fall.at[rows_at(b, 8)]).start()

    gd_ref[...] = pair_sum(3, gdpair, gdland, 32)
    go_ref[...] = pair_sum(4, gopair, goland, 8)
    output(4).start()
    output(5).start()

    merged = dn_sum.result()
    _, normed, inverse = normed_of()
    grad_norm = inverse * (
        merged
        - jnp.mean(merged, axis=-1, keepdims=True)
        - normed * jnp.mean(merged * normed, axis=-1, keepdims=True)
    )
    gtok_ref[...] = (dy_ref[...].astype(F32) + grad_norm).astype(BF)
    output(1).start()

    seq_all(1, gufin, 8).wait_recv()
    seq_all(2, gqfin, 8).wait_recv()

    batch_all(7, fall, 8).wait_recv()

    output(2).start()
    output(3).start()
    total = fall[0:8, :]
    for k in range(1, BATCH):
        total = total + fall[k * 8 : k * 8 + 8, :]
    small_ref[...] = total
    output(6).start()

    normed_gather.drain()
    dy_gather.drain()
    weight_gather.drain()
    mixed_sum.drain()
    dn_sum.drain()

    for k, ref, count in ((0, wst, 16), (1, gufin, 8), (2, gqfin, 8), (3, frecv, 8), (4, sgot, 16)):
        seq_all(k, ref, count).wait_send()
    for k, ref, count in (
        (0, sall, 16), (1, wd2, 32), (2, wo2, 8), (6, gqrecv, 128), (7, fall, 8),
    ):
        batch_all(k, ref, count).wait_send()
    for k, ref, pair, land, count in (
        (3, gdrecv, gdpair, gdland, 32), (4, gorecv, gopair, goland, 8), (5, gurecv, gupair, guland, 128),
    ):
        column_all(k, ref, count).wait_send()
        pair_copy(k + 5, pair, land, count).wait_send()

    for n in range(7):
        output(n).wait()


def finish(
    mixed_ref, gtok_ref, gu_ref, gq_ref, gd_ref, go_ref, small_ref,
    mixed_out, gtok_out, small_out, qkv_out, out_out, up_out, down_out,
):
    s = lax.axis_index("seq")
    b = lax.axis_index("batch")
    mixed_out[...] = mixed_ref[...]
    gtok_out[...] = gtok_ref[...]
    out_out[...] = go_ref[...]
    down_out[...] = gd_ref[...]
    low = iota((8, 128), 1) < 64
    for k in range(SEQ):
        up_out[:, k * HID : k * HID + HID] = gu_ref[k * 8 : k * 8 + 8, :]
    for k in range(0, SEQ, 2):
        one, two = (gq_ref[n * 8 : n * 8 + 8, 0:128] for n in (k, k + 1))
        one_v, two_v = (gq_ref[n * 8 : n * 8 + 8, 128:256] for n in (k, k + 1))
        at = k * HD
        qkv_out[:, at : at + 128] = jnp.where(low, one, pltpu.roll(two, 64, 1))
        qkv_out[:, D + at : D + at + 128] = jnp.where(low, pltpu.roll(one, 64, 1), two)
        qkv_out[:, 2 * D + at : 2 * D + at + 128] = jnp.where(low, one_v, pltpu.roll(two_v, 64, 1))
    begin = b * PER + lax.rem(s, 2) * 64
    line = begin // 128
    both = jnp.concatenate([small_ref[pl.ds(line, 1), :], small_ref[pl.ds(line + 1, 1), :]], axis=1)
    both = pltpu.roll(jnp.broadcast_to(both, (8, 256)), 256 - lax.rem(begin, 128), 1)
    small_out[...] = both[0:1, 0:PER]


def layer(x, dy, wq, wo, wu, wd, sp, order, lengths):
    vmem = pl.BlockSpec(memory_space=pltpu.VMEM)
    smem = pl.BlockSpec(memory_space=pltpu.SMEM)
    scratch = [
        ((TOK, D), BF), ((TOK, D), BF), ((32, D), F32), ((8, D), F32), ((8, 128), F32),
        ((ROW, D), BF), ((ROW, D), BF), ((16, 128), BF), ((256, 128), BF), ((128, 128), BF),
        ((256, 256), BF), ((256, 256), BF), ((2048, 256), BF),
        ((256, D), BF), ((8, D), F32), ((64, D), F32), ((64, D), BF),
        ((D, 256), F32), ((D, 256), F32), ((D, 128), F32), ((D, 512), BF),
        ((1, 512), F32), ((1, D), F32),
        ((32, 64, 256), F32), ((ROW, HID), BF), ((ROW, HID), F32),
        ((ROW, 128), F32), ((ROW, 128), F32),
        ((ROW, 128), BF), ((ROW, 128), BF), ((ROW, 128), BF),
        ((128, ROW), BF), ((128, ROW), BF), ((64, ROW), BF), ((ROW, 128), BF), ((64, ROW), BF),
        ((32, 64, HD), BF), ((32, 64, HD), F32), ((ROW, HD), BF),
        ((ROW, 512), BF), ((HD, ROW), F32), ((HD, ROW), F32),
        ((32, 64, 256), BF), ((ROW, 128), F32),
        ((ROW, D), BF), ((ROW, D), BF),
        ((1920, D), BF), ((1920, D), BF), ((64, D), BF), ((32, D), BF), ((16, D), F32), ((8, D), F32),
        ((256, 256), BF), ((128, 256), BF), ((D, 256), F32), ((D, 256), F32),
        ((320, D), F32), ((256, D), F32), ((256, D), F32),
        ((256, D), BF), ((64, D), F32), ((256, D), BF), ((64, D), F32),
        ((D, 256), BF), ((D, 256), BF), ((128, 256), F32), ((128, 256), F32),
        ((D, 256), BF), ((D, 256), BF), ((128, 256), F32), ((128, 256), F32),
        ((112, 128), F32), ((128, 128), F32), ((128, 128), F32), ((8, 128), F32), ((64, 128), F32),
    ]
    shapes = [pltpu.VMEM(shape, dtype) for shape, dtype in scratch]
    shapes += [
        pltpu.SMEM((32,), jnp.int32),
        pltpu.SemaphoreType.DMA((7,)),
        pltpu.SemaphoreType.DMA((3,)), pltpu.SemaphoreType.DMA((3, 17)),
        pltpu.SemaphoreType.DMA((2,)), pltpu.SemaphoreType.DMA((2, 21)),
        pltpu.SemaphoreType.DMA((5,)), pltpu.SemaphoreType.DMA((5,)),
        pltpu.SemaphoreType.DMA((11,)), pltpu.SemaphoreType.DMA((11,)),
    ]
    parts = pl.pallas_call(
        kernel,
        out_shape=(
            jax.ShapeDtypeStruct((TOK, D), BF),
            jax.ShapeDtypeStruct((TOK, D), BF),
            jax.ShapeDtypeStruct((128, 256), F32),
            jax.ShapeDtypeStruct((128, 256), F32),
            jax.ShapeDtypeStruct((32, D), F32),
            jax.ShapeDtypeStruct((8, D), F32),
            jax.ShapeDtypeStruct((8, 128), F32),
        ),
        in_specs=[vmem] * 7 + [smem] * 2,
        out_specs=(pl.BlockSpec(memory_space=pl.ANY),) * 7,
        scratch_shapes=shapes,
        compiler_params=pltpu.CompilerParams(
            collective_id=0, has_side_effects=True, vmem_limit_bytes=62 * 2**20
        ),
    )(x, dy, wq, wo, wu, wd, sp, order, lengths)
    return pl.pallas_call(
        finish,
        out_shape=(
            jax.ShapeDtypeStruct((TOK, D), BF),
            jax.ShapeDtypeStruct((TOK, D), BF),
            jax.ShapeDtypeStruct((1, PER), F32),
            jax.ShapeDtypeStruct((8, 3 * D), F32),
            jax.ShapeDtypeStruct((8, D), F32),
            jax.ShapeDtypeStruct((8, SEQ * HID), F32),
            jax.ShapeDtypeStruct((32, D), F32),
        ),
        in_specs=[vmem] * 7,
        out_specs=(vmem,) * 7,
    )(*parts)


def local(tokens, doc_lengths, block_order, small_params, w_qkv, w_out, w_up, w_down, cotangent):
    mixed, grad_tokens, grad_small, grad_qkv, grad_out, grad_up, grad_down = layer(
        tokens[0], cotangent[0], w_qkv, w_out, w_up, w_down,
        small_params.reshape(1, PER), block_order, doc_lengths,
    )
    return (
        mixed[None], grad_tokens[None], grad_small.reshape(PER), grad_qkv, grad_out, grad_up, grad_down,
    )


def solution(mesh):
    placed = (
        P("batch", "seq", None),
        P("batch", None),
        P(),
        P(("seq", "batch")),
        P(("seq", "batch"), None),
        P(("seq", "batch"), None),
        P(("seq", "batch"), None),
        P(("seq", "batch"), None),
        P("batch", "seq", None),
    )
    return jax.shard_map(
        local,
        mesh=mesh,
        in_specs=placed,
        out_specs=(
            P("batch", "seq", None),
            P("batch", "seq", None),
            P(("seq", "batch")),
            P(("seq", "batch"), None),
            P(("seq", "batch"), None),
            P(("seq", "batch"), None),
            P(("seq", "batch"), None),
        ),
        check_vma=False,
    )
```

```python
import jax
import jax.numpy as jnp
import numpy as np
from jax import lax
from jax.experimental import pallas as pl
from jax.experimental.pallas import tpu as pltpu
from jax.sharding import PartitionSpec as P

HD = 64
ROT = 16
EPS = 1e-05
NEG = -1e30
MESH = pl.DeviceIdType.MESH
BF = jnp.bfloat16
F32 = jnp.float32

SEQ = 16
BATCH = 8
TOK = 128
ROW = SEQ * TOK
D = 1024
HID = 256
PER = 104
QB = 256
AB = 512


def dot(a, b):
    return lax.dot_general(a, b, (((1,), (0,)), ((), ())), preferred_element_type=F32)


def dot_nt(a, b):
    return lax.dot_general(a, b, (((1,), (1,)), ((), ())), preferred_element_type=F32)


def dot_tn(a, b):
    return lax.dot_general(a, b, (((0,), (0,)), ((), ())), preferred_element_type=F32)


def iota(shape, dim):
    return lax.broadcasted_iota(jnp.int32, shape, dim)


def slot(z, x, c):
    return z * 8 + x * 2 + c


def rows_at(index, count):
    return pl.ds(pl.multiple_of(index * count, count), count)


def kernel(
    x_ref, dy_ref, wq_ref, wo_ref, wu_ref, wd_ref, sp_ref, order_ref, len_ref,
    mixed_out, gtok_out, gu_out, gq_out, gd_out, go_out, small_out,
    mixed_ref, gtok_ref, gd_ref, go_ref, small_ref, nrm, dya, ssend, sgot, sall, wsend, wst, wbuf, wd2, wos, wo2, wob, rawq, rawu, cols, wcat, brow, drow,
    prj, act, dge, tabc, tabs, qa, ka, va, kat, vat, qat, doa, doat, dost, osort, ost,
    dcat, dkt, dvt, dsort, dqs,
    part_m, part_d, land_m, land_d, gdpair, gdland, gopair, goland, gupair, guland, keptu, keptq,
    gdacc, gtq, gtu, gdsend, gosend, gdrecv, gorecv,
    gusend, gurecv, gusum, gufin, gqsend, gqrecv, gqsum, gqfin,
    flat, fsend, frecv, fsum, fall,
    inv_ref, out_ss, ag_ss, ag_rs, rs_ss, rs_rs, sq_ss, sq_rs, bt_ss, bt_rs,
):
    s = lax.axis_index("seq")
    b = lax.axis_index("batch")
    z, x, c = s // 8, lax.rem(s // 2, 4), lax.rem(s, 2)
    xr, xl, xo = lax.rem(x + 1, 4), lax.rem(x + 3, 4), lax.rem(x + 2, 4)
    zo, co = 1 - z, 1 - c
    y, w = b // 2, lax.rem(b, 2)
    yr, yl, yo, wo_ = lax.rem(y + 1, 4), lax.rem(y + 3, 4), lax.rem(y + 2, 4), 1 - w
    right, left = (slot(z, xr, c), b), (slot(z, xl, c), b)
    across, sibling = (slot(zo, x, c), b), (slot(z, x, co), b)

    def remote(src, dst, send, recv, device):
        return pltpu.make_async_remote_copy(
            src_ref=src, dst_ref=dst, send_sem=send, recv_sem=recv,
            device_id=device, device_id_type=MESH,
        )

    barrier = pltpu.get_barrier_semaphore()

    @pl.loop(1, SEQ)
    def _(j):
        pl.semaphore_signal(barrier, inc=1, device_id=(lax.rem(s + j, SEQ), b), device_id_type=MESH)

    @pl.loop(1, BATCH)
    def _(j):
        pl.semaphore_signal(barrier, inc=1, device_id=(s, lax.rem(b + j, BATCH)), device_id_type=MESH)

    def normed_of():
        inputs = x_ref[...].astype(F32)
        centred = inputs - jnp.mean(inputs, axis=-1, keepdims=True)
        inverse = lax.rsqrt(jnp.mean(centred * centred, axis=-1, keepdims=True) + EPS)
        return inputs, centred * inverse, inverse

    nrm[rows_at(s, TOK), :] = normed_of()[1].astype(BF)
    dya[rows_at(s, TOK), :] = dy_ref[...]

    def pair(one, two):
        return jnp.where(iota((8, 128), 1) < 64, one, two)

    small = jnp.concatenate([sp_ref[...].astype(F32), jnp.zeros((1, 128 - PER), F32)], axis=1)
    ssend[...] = jnp.broadcast_to(small, (16, 128)).astype(BF)
    wide_q = wq_ref[...].astype(F32)
    wide_u = wu_ref[...].astype(F32)
    for k in range(SEQ):
        at = slice(k // 2 * 128, k // 2 * 128 + 128)
        q, kk, v = (wide_q[:, n * D : n * D + D][:, at] for n in range(3))
        turned = [pltpu.roll(part_of, 64, 1) for part_of in (q, kk, v)]
        q, kk, v = (q, turned[1], v) if k % 2 == 0 else (turned[0], kk, turned[2])
        low = jnp.concatenate([pair(q, kk), pair(v, jnp.zeros_like(v))], axis=1)
        block = jnp.concatenate([wide_u[:, k * HID : k * HID + HID], low], axis=0)
        wsend[k * 16 : k * 16 + 16, :] = block.astype(BF)

    wst[rows_at(s, 16), :] = wsend[rows_at(s, 16), :]
    sgot[rows_at(s, 16), :] = ssend[...]
    wos[...] = wo_ref[...].astype(F32)
    wd2[rows_at(b, 32), :] = wd_ref[...]
    wo2[rows_at(b, 8), :] = wos[...]

    pl.semaphore_wait(barrier, SEQ - 1 + BATCH - 1)

    def seq_copy(j, k, src, dst):
        return remote(src, dst, sq_ss.at[k], sq_rs.at[k], (lax.rem(s + j, SEQ), b))

    def seq_all(k, ref, count):
        ref = ref.at[pl.ds(0, (SEQ - 1) * count)]
        return seq_copy(1, k, ref, ref)

    def column_copy(j, k, src, dst):
        return remote(src, dst, bt_ss.at[k], bt_rs.at[k], (s, lax.rem(y + j, 4) * 2 + w))

    def column_start(k, send, recv, count):
        @pl.loop(1, 4)
        def _(j):
            peer = lax.rem(y + j, 4)
            column_copy(j, k, send.at[rows_at(peer, 2 * count)], recv.at[rows_at(y, 2 * count)]).start()

    def column_all(k, ref, count):
        ref = ref.at[pl.ds(0, 6 * count)]
        return column_copy(1, k, ref, ref)

    def pair_copy(k, pair, land, count):
        src = pair.at[rows_at(wo_, count)]
        return remote(src, land, bt_ss.at[k], bt_rs.at[k], (s, y * 2 + wo_))

    def column_sums(k, recv, pair, land, count):
        column_all(k, recv, count).wait_recv()
        total = recv[0 : 2 * count, :].astype(F32)
        for n in range(1, 4):
            total = total + recv[2 * n * count : 2 * (n + 1) * count, :].astype(F32)
        pair[...] = total.astype(pair.dtype)
        pair_copy(k + 5, pair, land, count).start()

    def pair_sum(k, pair, land, count):
        pair_copy(k + 5, pair, land, count).wait_recv()
        return pair[rows_at(w, count), :].astype(F32) + land[...].astype(F32)

    def batch_all(k, ref, count):
        ref = ref.at[pl.ds(0, (BATCH - 1) * count)]
        return batch_copy(1, k, ref, ref)

    def batch_copy(j, k, src, dst):
        return remote(src, dst, bt_ss.at[k], bt_rs.at[k], (s, lax.rem(b + j, BATCH)))

    @pl.loop(1, SEQ)
    def _(j):
        peer = lax.rem(s + j, SEQ)
        seq_copy(j, 0, wsend.at[rows_at(peer, 16)], wst.at[rows_at(s, 16)]).start()

    class Gather:
        def __init__(self, buf, k, size, slots, right, left, across, sibling=None):
            self.buf, self.k, self.size = buf, k, size
            own, far, of_left, of_right, far_left, far_right, opposite, far_opposite = slots[0]
            half = size // 2
            self.sends = {
                0: (own, right, 0, size), 1: (own, left, 0, size), 2: (own, across, 0, size),
                4: (far, right, 0, size), 5: (far, left, 0, size),
                7: (of_left, right, 0, half), 8: (of_right, left, half, half),
                11: (far_left, right, 0, half), 12: (far_right, left, half, half),
            }
            self.receives = {
                0: (of_left, 0, size), 1: (of_right, 0, size), 2: (far, 0, size),
                4: (far_left, 0, size), 5: (far_right, 0, size),
                7: (opposite, 0, half), 8: (opposite, half, half),
                11: (far_opposite, 0, half), 12: (far_opposite, half, half),
            }
            if sibling is not None:
                for e, n in ((3, 0), (6, 1), (9, 2), (10, 3), (13, 4), (14, 5), (15, 6), (16, 7)):
                    self.sends[e] = (slots[0][n], sibling, 0, size)
                    self.receives[e] = (slots[1][n], 0, size)

        def copy(self, e, index, device, low, count):
            at = self.buf.at[pl.ds(pl.multiple_of(index * self.size + low, self.size // 2), count)]
            return remote(at, at, ag_ss.at[self.k], ag_rs.at[self.k, e], device)

        def start(self, *events):
            for e in events:
                if e in self.sends:
                    self.copy(e, self.sends[e][0], *self.sends[e][1:]).start()

        def wait(self, *events):
            for e in events:
                if e in self.receives:
                    index, low, count = self.receives[e]
                    self.copy(e, index, self.sends[e][1], low, count).wait_recv()

        def step(self, n):
            if n == 0:
                self.start(0, 1, 2, 3)
            elif n == 1:
                self.wait(0)
                self.start(7)
                self.wait(1)
                self.start(8)
                self.wait(2)
                self.start(4, 5, 6, 9, 10)
            elif n == 2:
                self.wait(4)
                self.start(11, 13)
                self.wait(5)
                self.start(12, 14)
            elif n == 3:
                self.wait(7, 8)
                self.start(15)
                self.wait(11, 12)
                self.start(16)
            else:
                self.wait(3, 6, 9, 10, 13, 14, 15, 16)

        def drain(self):
            sent = self.buf.at[pl.ds(0, sum(what[3] for what in self.sends.values()))]
            remote(sent, sent, ag_ss.at[self.k], ag_rs.at[self.k, 0], right).wait_send()

    def row_slots(core):
        return [slot(p, q, core) for p, q in ((z, x), (zo, x), (z, xl), (z, xr), (zo, xl), (zo, xr), (z, xo), (zo, xo))]

    rows_slots = [q * 2 + p for p, q in ((w, y), (wo_, y), (w, yl), (w, yr), (wo_, yl), (wo_, yr), (w, yo), (wo_, yo))]

    normed_gather = Gather(nrm, 0, TOK, (row_slots(c), row_slots(co)), right, left, across, sibling)
    dy_gather = Gather(dya, 1, TOK, (row_slots(c), row_slots(co)), right, left, across, sibling)
    weight_gather = Gather(
        wbuf, 2, 256, (rows_slots,), (s, yr * 2 + w), (s, yl * 2 + w), (s, y * 2 + wo_)
    )
    normed_gather.step(0)

    @pl.loop(0, 32)
    def _(i):
        place = jnp.int32(0)
        for j in range(32):
            place = place + jnp.where(order_ref[j] == i, j, 0)
        inv_ref[i] = jnp.minimum(place, 31)

    @pl.loop(1, SEQ)
    def _(j):
        seq_copy(j, 4, ssend, sgot.at[rows_at(s, 16)]).start()

    outputs = (
        (mixed_ref, mixed_out), (gtok_ref, gtok_out), (gufin, gu_out), (gqfin, gq_out),
        (gd_ref, gd_out), (go_ref, go_out), (small_ref, small_out),
    )

    def output(n):
        return pltpu.make_async_copy(*outputs[n], out_ss.at[n])

    ends = [len_ref[0, 0]]
    for k in range(1, 4):
        ends.append(ends[-1] + len_ref[0, k])

    def begin_of(where):
        begin = jnp.zeros_like(where)
        for end in ends:
            begin = jnp.maximum(begin, jnp.where(where >= end, end, 0))
        return begin

    def doc_of(where):
        doc = jnp.zeros_like(where)
        for end in ends:
            doc = doc + jnp.where(where >= end, 1, 0)
        return doc

    def partner_of(part):
        lane = lax.rem(iota(part.shape, 1), 64)
        return jnp.where(lane < ROT // 2, pltpu.roll(part, 120, 1), pltpu.roll(part, 8, 1))

    rate = jnp.zeros((1, 128), F32)
    for k in range(ROT // 2):
        value = float(np.float32(10000.0) ** np.float32(-2.0 * k / ROT))
        rate = jnp.where(lax.rem(iota((1, 128), 1), 8) == k, value, rate)

    @pl.loop(0, 8, unroll=2)
    def _(i):
        where = i * QB + iota((QB, 128), 0)
        angle = (where - begin_of(where)).astype(F32) * rate
        lane = lax.rem(iota((QB, 128), 1), 64)
        sine = jnp.sin(angle)
        tabc[rows_at(i, QB), :] = jnp.where(lane < ROT, jnp.cos(angle), 1.0)
        sine = jnp.where(lane < ROT // 2, -sine, sine)
        tabs[rows_at(i, QB), :] = jnp.where(lane < ROT, sine, 0.0)

    normed_gather.step(1)
    seq_all(0, wst, 16).wait_recv()
    seq_all(4, sgot, 16).wait_recv()

    wbuf[rows_at(b, 256), :] = wst[...]
    weight_gather.step(0)
    lines = [sgot[k * 16 : k * 16 + 16, :].astype(F32)[0:1, :] for k in range(SEQ)]
    sall[rows_at(b, 16), :] = jnp.concatenate(lines, axis=0).astype(BF)

    @pl.loop(1, BATCH)
    def _(j):
        batch_copy(j, 0, sall.at[rows_at(b, 16)], sall.at[rows_at(b, 16)]).start()

    weight_gather.step(1)
    dy_gather.start(2)

    batch_all(0, sall, 16).wait_recv()

    def hot_of(line, number):
        low = (lax.rem(line, 16) * BATCH + line // 16) * PER
        return ((low <= number) & (number < low + PER)).astype(F32).astype(BF)

    def place_of(number):
        owner = jnp.floor((number.astype(F32) + 0.5) * (1.0 / PER)).astype(jnp.int32)
        return number - PER * owner

    for k in range(4):
        number = k * D + iota((D, 1), 0)
        found = dot(hot_of(iota((1, 128), 1), number), sall[...])
        found = jnp.where(iota((D, 128), 1) == place_of(number), found, 0.0)
        cols[:, k : k + 1] = jnp.sum(found, axis=1, keepdims=True)

    def small_row(number):
        found = dot_tn(sall[...], hot_of(iota((128, 1), 0), number))
        found = jnp.where(iota((128, number.shape[1]), 0) == place_of(number), found, 0.0)
        return jnp.sum(found, axis=0, keepdims=True)

    lane = iota((1, 256), 1)
    number_q = 4 * D + (lane // 64) * D + s * 64 + lax.rem(lane, 64)
    bias_q = small_row(jnp.where(lane < 192, number_q, -1000))
    bias_u = small_row(8 * D + s * HID + lane)
    wide = iota((1, D), 1)
    drow[...] = small_row(7 * D + wide) + small_row(12 * D + wide)

    normed_gather.step(2)
    weight_gather.step(2)
    dy_gather.start(0, 1)
    weight_gather.step(3)

    @pl.loop(0, SEQ)
    def _(i):
        for j in range(BATCH):
            block = wbuf[pl.ds(pl.multiple_of(j * 256 + i * 16, 16), 16), :].astype(F32)
            at = pl.ds(pl.multiple_of(i * 64 + j * 8, 8), 8)
            rawu[at, :] = block[0:8, :]
            rawq[at, :] = block[8:16, :]

    row_q, row_u = bias_q, bias_u
    for i in range(8):
        at = slice(i * 128, i * 128 + 128)
        wq, wu = rawq[at, :], rawu[at, :]
        wcat[at, 0:256] = (wq * cols[at, 0:1]).astype(BF)
        wcat[at, 256:512] = (wu * cols[at, 2:3]).astype(BF)
        row_q = row_q + jnp.sum(wq * cols[at, 1:2], axis=0, keepdims=True)
        row_u = row_u + jnp.sum(wu * cols[at, 3:4], axis=0, keepdims=True)
    brow[:, 0:256] = row_q
    brow[:, 256:512] = row_u

    normed_gather.step(3)
    dy_gather.wait(2)
    dy_gather.start(4, 5, 3, 6)
    normed_gather.step(4)

    @pl.loop(0, 4, unroll=4)
    def _(i):
        out = dot(nrm[rows_at(i, 512), :], wcat[:, 0:256]) + brow[:, 0:256]
        prj[pl.ds(i * 8, 8)] = out.reshape(8, 64, 256)

    @pl.loop(1, BATCH)
    def _(j):
        batch_copy(j, 1, wd_ref, wd2.at[rows_at(b, 32)]).start()
        batch_copy(j, 2, wos, wo2.at[rows_at(b, 8)]).start()

    def pieces_of(value):
        high = value.astype(BF).astype(F32)
        mid = (value - high).astype(BF).astype(F32)
        return high, mid, value - high - mid

    def with_lanes(base, first, values):
        lane = iota(base.shape, 1)
        for k, value in enumerate(values):
            base = jnp.where(lane == first + k, value, base)
        return base

    def blocks_of(ref, order, i):
        return jnp.concatenate([ref[order[i * 4 + k]] for k in range(4)], axis=0)

    @pl.loop(0, 8, unroll=4)
    def _(i):
        at = rows_at(i, QB)
        come = blocks_of(prj, inv_ref, i)
        both = come[:, 0:128]
        both = both * tabc[at, :] + partner_of(both) * tabs[at, :]
        lane = iota((QB, 128), 1)
        own = doc_of(i * QB + iota((QB, 128), 0)) == lane - 64
        front = lane < 64
        query = jnp.where(front, both * 0.125, jnp.where(own | (lane >= 68), 0.0, NEG)).astype(BF)
        tail = jnp.where(lane < 68, own.astype(F32), (lane < 71).astype(F32))
        key = jnp.where(front, pltpu.roll(both, 64, 1), tail).astype(BF)
        value = jnp.where(front, come[:, 128:256], (lane < 67).astype(F32)).astype(BF)
        qa[at, :], ka[at, :], va[at, :] = query, key, value
        qat[:, at] = query.T[0:64, :]
        kat[:, at] = key.T
        vat[:, at] = value.T

    dy_gather.wait(0)
    dy_gather.start(7)
    dy_gather.wait(1)
    dy_gather.start(8)

    lower = iota((AB, AB), 1) <= iota((AB, AB), 0)

    def attend(i):
        at = rows_at(i, AB)

        def step(j, carry, masked):
            top, total = carry
            k_at = rows_at(j, AB)
            scores = dot(qa[at, :], kat[:, k_at])
            if masked:
                scores = jnp.where(lower, scores, NEG)
            peak = jnp.maximum(top, jnp.max(scores, axis=1, keepdims=True))
            expos = jnp.exp(scores - peak).astype(BF)
            return peak, total * jnp.exp(top - peak) + dot(expos, va[k_at, :])

        carry = (jnp.full((AB, 1), NEG, F32), jnp.zeros((AB, 128), F32))
        for j in range(i + 1):
            carry = step(j, carry, j == i)
        top, total = carry
        norm = total[:, 64:65]
        osort[pl.ds(i * (AB // 64), AB // 64)] = (total / norm)[:, 0:64].reshape(AB // 64, 64, HD)
        qa[at, :] = with_lanes(qa[at, :].astype(F32), 68, pieces_of(-(top + jnp.log(norm)))).astype(BF)

    for i in range(3):
        attend(i)
    dy_gather.wait(4)
    dy_gather.start(11)
    dy_gather.wait(5)
    dy_gather.start(12, 9, 10, 13, 14)
    attend(3)

    @pl.loop(0, 4, unroll=4)
    def _(i):
        at = rows_at(i, 512)
        hidden = dot(nrm[at, :], wcat[:, 256:512]) + brow[:, 256:512]
        share = 0.5 * (1.0 + lax.erf(hidden * (2.0**-0.5)))
        act[at, :] = (hidden * share).astype(BF)
        dge[at, :] = share + hidden * jnp.exp(-0.5 * hidden * hidden) * ((2.0 * np.pi) ** -0.5)

    dy_gather.wait(7, 8)
    dy_gather.start(15)

    @pl.loop(0, 8)
    def _(j):
        ost[rows_at(j, QB), :] = blocks_of(osort, order_ref, j).astype(BF)

    batch_all(1, wd2, 32).wait_recv()
    batch_all(2, wo2, 8).wait_recv()

    wob[...] = wo2[...].astype(BF)

    class Scatter:
        def __init__(self, part, land, k):
            self.part, self.land, self.k = part, land, k
            self.order = [(zo, xo), (zo, xr), (zo, xl), (zo, x), (z, xo), (z, xr), (z, xl), (z, x)]
            table = [(n, co, 0, TOK, sibling, None) for n in range(8)]
            for g in (0, 4):
                table += [
                    (g, c, 0, 64, left, g + 2), (g, c, 64, 64, right, g + 1),
                    (g + 1, c, 0, 64, right, g + 3), (g + 2, c, 64, 64, left, g + 3),
                    (g + 1, c, 64, 64, right, g + 3), (g + 2, c, 0, 64, left, g + 3),
                ]
            table += [(3, c, 0, TOK, across, 7)]
            self.table, self.begin, at = table, [], 0
            for entry in table:
                self.begin.append(at)
                at += entry[3]

        def at(self, n, core, low, count):
            zz, xx = self.order[n]
            return pl.ds(pl.multiple_of(slot(zz, xx, core) * TOK + low, 16), count)

        def copy(self, e, src, dst, device):
            return remote(src, dst, rs_ss.at[self.k], rs_rs.at[self.k, e], device)

        def out(self, e):
            n, core, low, count, device, _ = self.table[e]
            return self.part.at[self.at(n, core, low, count)], self.land.at[pl.ds(self.begin[e], count)], device

        def start(self, *events):
            for e in events:
                self.copy(e, *self.out(e)).start()

        def wait(self, e):
            src, dst, device = self.out(e)
            self.copy(e, dst, dst, device).wait_recv()

        def landed(self, e):
            self.wait(e)
            return self.land[self.begin[e] : self.begin[e] + self.table[e][3], :].astype(F32)

        def add(self, *events):
            for e in events:
                n, core, low, count, _, to = self.table[e]
                to = e if e < 8 else to
                at = self.at(to, c, low, count)
                self.part[at, :] = (self.part[at, :].astype(F32) + self.landed(e)).astype(BF)

        def step(self, n):
            if n == 0 or n == 1:
                self.add(4 * n)
                self.start(8 + 6 * n, 9 + 6 * n)
            elif n == 2 or n == 3:
                g = n - 2
                self.add(4 * g + 1, 4 * g + 2)
                self.start(10 + 6 * g, 11 + 6 * g)
                self.add(4 * g + 3)
            elif n == 4 or n == 5:
                g = n - 4
                self.add(8 + 6 * g, 9 + 6 * g)
                self.start(12 + 6 * g, 13 + 6 * g)
            else:
                self.add(10, 11, 12, 13)
                self.start(20)

        def result(self):
            total = self.part[self.at(7, c, 0, TOK), :].astype(F32)
            low = total[0:64, :] + self.landed(16) + self.landed(19)
            high = total[64:TOK, :] + self.landed(17) + self.landed(18)
            return jnp.concatenate([low, high], axis=0) + self.landed(20)

        def drain(self):
            sent = self.part.at[pl.ds(0, sum(entry[3] for entry in self.table))]
            self.copy(0, sent, sent, sibling).wait_send()

    mixed_sum = Scatter(part_m, land_m, 0)
    dn_sum = Scatter(part_d, land_d, 1)

    def halves_of(which):
        return [(which, xo // 2), (which, 1 - xo // 2)]

    for k, (which, side) in enumerate(halves_of(zo) + halves_of(z)):
        at = rows_at(which * 2 + side, 512)
        part_m[at, :] = (dot(act[at, :], wd2[...]) + dot(ost[at, :], wob[...])).astype(BF)
        if k == 0:
            mixed_sum.start(0)
        elif k == 1:
            mixed_sum.start(1, 2, 3)
            dy_gather.wait(11, 12)
            dy_gather.start(16)
    mixed_sum.step(0)
    mixed_sum.start(4, 5, 6, 7)

    dy_gather.step(4)

    @pl.loop(0, 4, unroll=4)
    def _(i):
        at = rows_at(i, 512)
        dy = dya[at, :]
        dcat[at, 256:512] = (dot_nt(dy, wd2[...]) * dge[at, :]).astype(BF)
        dost[pl.ds(i * 8, 8)] = dot_nt(dy, wob[...]).astype(BF).reshape(8, 64, HD)

    mixed_sum.step(2)

    gdacc[...] = jnp.zeros_like(gdacc)

    @pl.loop(0, 2, unroll=2)
    def _(i):
        at = rows_at(i, 1024)
        gdacc[0:256, :] += dot_tn(act[at, :], dya[at, :])
        gdacc[256:320, :] += dot_tn(ost[at, :], dya[at, :])

    gdsend[...] = gdacc[0:256, :].astype(BF)
    gosend[...] = gdacc[256:320, :]
    gdrecv[rows_at(y, 64), :] = gdsend[rows_at(y, 64), :]
    gorecv[rows_at(y, 16), :] = gosend[rows_at(y, 16), :]
    column_start(3, gdsend, gdrecv, 32)
    column_start(4, gosend, gorecv, 8)

    mixed_sum.step(4)
    mixed_sum.step(1)
    mixed_sum.step(3)

    def column_sum(low):
        def add(i, total):
            return total + jnp.sum(dcat[rows_at(i, QB), low : low + 256].astype(F32), axis=0, keepdims=True)

        return lax.fori_loop(0, 8, add, jnp.zeros((1, 256), F32))

    def to_flat(line, values):
        for k in range(values.shape[1] // 128):
            flat[line + k : line + k + 1, :] = values[:, k * 128 : k * 128 + 128]

    def hand_out(gt, kept, sums, k, send):
        for i in range(4):
            at = slice(i * 256, i * 256 + 256)
            grad = gt[0:256, at].T
            kept[at, :] = grad
            grad = grad * cols[at, k : k + 1] + cols[at, k + 1 : k + 2] * sums
            for m in range(8):
                for h in range(2):
                    place = m * 128 + i * 32 + h * 16
                    first, second = (h * 2) * 64 + m * 8, (h * 2 + 1) * 64 + m * 8
                    send[place : place + 16, :] = jnp.concatenate(
                        [grad[first : first + 8, :], grad[second : second + 8, :]], axis=0
                    ).astype(BF)

    def small_sums(kept, raw, sums, k):
        for i in range(4):
            at = slice(i * 256, i * 256 + 256)
            gain = jnp.sum(kept[at, :] * raw[at, :], axis=1, keepdims=True)
            shift = jnp.sum(sums * raw[at, :], axis=1, keepdims=True)
            lane = iota((256, 128), 1)
            spread = jnp.where(lane == 0, gain, jnp.where(lane == 1, shift, 0.0)).T
            to_flat(k * 8 + i * 2, spread[0:1, :])
            to_flat(k * 8 + 8 + i * 2, spread[1:2, :])

    def to_owners(total, total_ref, final, k):
        total_ref[...] = total
        final[rows_at(s, 8), :] = total_ref[rows_at(s, 8), :]

        @pl.loop(1, SEQ)
        def _(j):
            peer = lax.rem(s + j, SEQ)
            seq_copy(j, k, total_ref.at[rows_at(peer, 8)], final.at[rows_at(s, 8)]).start()

    gtu[...] = jnp.zeros_like(gtu)

    @pl.loop(0, 2, unroll=2)
    def _(i):
        at = rows_at(i, 1024)
        gtu[...] += dot_tn(dcat[at, 256:512], nrm[at, :])

    sum_u = column_sum(256)
    hand_out(gtu, keptu, sum_u, 2, gusend)
    gurecv[rows_at(y, 256), :] = gusend[rows_at(y, 256), :]
    column_start(5, gusend, gurecv, 128)


    @pl.loop(0, 8, unroll=4)
    def _(i):
        at = rows_at(i, QB)
        grads = blocks_of(dost, inv_ref, i).astype(F32)
        past = osort[pl.ds(i * 4, 4)].reshape(QB, HD)
        delta = jnp.sum(grads * past, axis=1, keepdims=True)
        wide = jnp.concatenate([grads, jnp.zeros((QB, 64), F32)], axis=1)
        wide = with_lanes(wide, 64, pieces_of(-delta)).astype(BF)
        doa[at, :] = wide
        doat[:, at] = wide.T[0:64, :]

    dkt[...] = jnp.zeros_like(dkt)
    dvt[...] = jnp.zeros_like(dvt)

    def attend_back(q_at, k_at, masked):
        probs = jnp.exp(dot(qa[q_at, :], kat[:, k_at]))
        if masked:
            probs = jnp.where(lower, probs, 0.0)
        grads = (probs * dot(doa[q_at, :], vat[:, k_at])).astype(BF)
        dkt[:, k_at] += dot(qat[:, q_at], grads)
        dvt[:, k_at] += dot(doat[:, q_at], probs.astype(BF))
        dqs[q_at, :] += dot(grads, ka[k_at, :])

    dqs[...] = jnp.zeros_like(dqs)
    for i in range(ROW // AB):
        attend_back(slice(i * AB, i * AB + AB), slice(i * AB, i * AB + AB), True)
        if i < ROW // AB - 1:
            for k in range(i * AB, i * AB + AB, 256):
                attend_back(slice(i * AB + AB, ROW), slice(k, k + 256), False)

    mixed_sum.step(6)
    mixed_sum.step(5)

    @pl.loop(0, 8, unroll=4)
    def _(i):
        at = rows_at(i, QB)
        both = jnp.concatenate([dqs[at, 0:64] * 0.125, dkt[:, at].T], axis=1)
        both = both * tabc[at, :] - partner_of(both) * tabs[at, :]
        last = jnp.concatenate([dvt[:, at].T, jnp.zeros((QB, 64), F32)], axis=1)
        whole = jnp.concatenate([both, last], axis=1).astype(BF)
        dsort[pl.ds(i * 4, 4)] = whole.reshape(4, 64, 256)

    @pl.loop(0, 8)
    def _(j):
        dcat[rows_at(j, QB), 0:256] = blocks_of(dsort, order_ref, j)

    def dn_part(which, side):
        at = rows_at(which * 2 + side, 512)
        part_d[at, :] = dot_nt(dcat[at, :], wcat[...]).astype(BF)

    dn_part(*halves_of(zo)[0])
    dn_sum.start(0)
    dn_part(*halves_of(zo)[1])
    dn_sum.start(1, 2, 3)
    dn_sum.step(0)
    gtq[...] = jnp.zeros_like(gtq)

    @pl.loop(0, 2, unroll=2)
    def _(i):
        at = rows_at(i, 1024)
        gtq[...] += dot_tn(dcat[at, 0:256], nrm[at, :])

    dn_sum.step(2)
    sum_q = column_sum(0)
    hand_out(gtq, keptq, sum_q, 0, gqsend)
    gqrecv[rows_at(b, 128), :] = gqsend[rows_at(b, 128), :]

    @pl.loop(1, BATCH)
    def _(j):
        peer = lax.rem(b + j, BATCH)
        batch_copy(j, 6, gqsend.at[rows_at(peer, 128)], gqrecv.at[rows_at(b, 128)]).start()

    column_sums(5, gurecv, gupair, guland, 128)
    dn_sum.step(4)
    for which, side in halves_of(z):
        dn_part(which, side)
    dn_sum.start(4, 5, 6, 7)
    small_sums(keptu, rawu, sum_u, 2)
    small_sums(keptq, rawq, sum_q, 0)

    def low_half(part_of):
        return jnp.concatenate([part_of[:, 0:64], jnp.zeros((1, 64), F32)], axis=1)

    flat[32:56, :] = jnp.zeros((24, 128), F32)
    flat[64:96, :] = jnp.zeros((32, 128), F32)
    flat[104:112, :] = jnp.zeros((8, 128), F32)
    upper = lax.rem(s, 2) == 1
    spans = (sum_q[:, 0:128], pltpu.roll(sum_q[:, 0:128], 64, 1), sum_q[:, 128:256])
    for k in range(3):
        mine = low_half(spans[k])
        mine = jnp.where(upper, pltpu.roll(mine, 64, 1), mine)
        flat[pl.ds(32 + k * 8 + s // 2, 1), :] = mine
    flat[pl.ds(64 + 2 * s, 1), :] = sum_u[:, 0:128]
    flat[pl.ds(65 + 2 * s, 1), :] = sum_u[:, 128:256]
    dy_total = jnp.sum(dy_ref[...].astype(F32), axis=0, keepdims=True)
    to_flat(56, dy_total)
    to_flat(96, dy_total)
    for k in range(SEQ):
        fsend[k * 8 : k * 8 + 8, :] = flat[13 * k // 2 : 13 * k // 2 + 8, :]
    frecv[rows_at(s, 8), :] = fsend[rows_at(s, 8), :]

    @pl.loop(1, SEQ)
    def _(j):
        peer = lax.rem(s + j, SEQ)
        seq_copy(j, 3, fsend.at[rows_at(peer, 8)], frecv.at[rows_at(s, 8)]).start()

    column_sums(3, gdrecv, gdpair, gdland, 32)
    column_sums(4, gorecv, gopair, goland, 8)
    dn_sum.step(1)
    dn_sum.step(6)
    dn_sum.step(3)
    to_owners(pair_sum(5, gupair, guland, 128), gusum, gufin, 1)
    batch_all(6, gqrecv, 128).wait_recv()
    total = gqrecv[0:128, :].astype(F32)
    for k in range(1, BATCH):
        total = total + gqrecv[k * 128 : k * 128 + 128, :].astype(F32)
    to_owners(total, gqsum, gqfin, 2)
    dn_sum.step(5)
    mixed_ref[...] = (mixed_sum.result() + x_ref[...].astype(F32) + drow[...]).astype(BF)
    output(0).start()

    seq_all(3, frecv, 8).wait_recv()

    total = frecv[0:8, :]
    for k in range(1, SEQ):
        total = total + frecv[k * 8 : k * 8 + 8, :]
    fsum[...] = total
    fall[rows_at(b, 8), :] = total

    @pl.loop(1, BATCH)
    def _(j):
        batch_copy(j, 7, fsum, fall.at[rows_at(b, 8)]).start()

    gd_ref[...] = pair_sum(3, gdpair, gdland, 32)
    go_ref[...] = pair_sum(4, gopair, goland, 8)
    output(4).start()
    output(5).start()

    merged = dn_sum.result()
    _, normed, inverse = normed_of()
    grad_norm = inverse * (
        merged
        - jnp.mean(merged, axis=-1, keepdims=True)
        - normed * jnp.mean(merged * normed, axis=-1, keepdims=True)
    )
    gtok_ref[...] = (dy_ref[...].astype(F32) + grad_norm).astype(BF)
    output(1).start()

    seq_all(1, gufin, 8).wait_recv()
    seq_all(2, gqfin, 8).wait_recv()

    batch_all(7, fall, 8).wait_recv()

    output(2).start()
    output(3).start()
    total = fall[0:8, :]
    for k in range(1, BATCH):
        total = total + fall[k * 8 : k * 8 + 8, :]
    small_ref[...] = total
    output(6).start()

    normed_gather.drain()
    dy_gather.drain()
    weight_gather.drain()
    mixed_sum.drain()
    dn_sum.drain()

    for k, ref, count in ((0, wst, 16), (1, gufin, 8), (2, gqfin, 8), (3, frecv, 8), (4, sgot, 16)):
        seq_all(k, ref, count).wait_send()
    for k, ref, count in (
        (0, sall, 16), (1, wd2, 32), (2, wo2, 8), (6, gqrecv, 128), (7, fall, 8),
    ):
        batch_all(k, ref, count).wait_send()
    for k, ref, pair, land, count in (
        (3, gdrecv, gdpair, gdland, 32), (4, gorecv, gopair, goland, 8), (5, gurecv, gupair, guland, 128),
    ):
        column_all(k, ref, count).wait_send()
        pair_copy(k + 5, pair, land, count).wait_send()

    for n in range(7):
        output(n).wait()


def finish(
    mixed_ref, gtok_ref, gu_ref, gq_ref, gd_ref, go_ref, small_ref,
    mixed_out, gtok_out, small_out, qkv_out, out_out, up_out, down_out,
):
    s = lax.axis_index("seq")
    b = lax.axis_index("batch")
    mixed_out[...] = mixed_ref[...]
    gtok_out[...] = gtok_ref[...]
    out_out[...] = go_ref[...]
    down_out[...] = gd_ref[...]
    low = iota((8, 128), 1) < 64
    for k in range(SEQ):
        up_out[:, k * HID : k * HID + HID] = gu_ref[k * 8 : k * 8 + 8, :]
    for k in range(0, SEQ, 2):
        one, two = (gq_ref[n * 8 : n * 8 + 8, 0:128] for n in (k, k + 1))
        one_v, two_v = (gq_ref[n * 8 : n * 8 + 8, 128:256] for n in (k, k + 1))
        at = k * HD
        qkv_out[:, at : at + 128] = jnp.where(low, one, pltpu.roll(two, 64, 1))
        qkv_out[:, D + at : D + at + 128] = jnp.where(low, pltpu.roll(one, 64, 1), two)
        qkv_out[:, 2 * D + at : 2 * D + at + 128] = jnp.where(low, one_v, pltpu.roll(two_v, 64, 1))
    begin = b * PER + lax.rem(s, 2) * 64
    line = begin // 128
    both = jnp.concatenate([small_ref[pl.ds(line, 1), :], small_ref[pl.ds(line + 1, 1), :]], axis=1)
    both = pltpu.roll(jnp.broadcast_to(both, (8, 256)), 256 - lax.rem(begin, 128), 1)
    small_out[...] = both[0:1, 0:PER]


def layer(x, dy, wq, wo, wu, wd, sp, order, lengths):
    vmem = pl.BlockSpec(memory_space=pltpu.VMEM)
    smem = pl.BlockSpec(memory_space=pltpu.SMEM)
    scratch = [
        ((TOK, D), BF), ((TOK, D), BF), ((32, D), F32), ((8, D), F32), ((8, 128), F32),
        ((ROW, D), BF), ((ROW, D), BF), ((16, 128), BF), ((256, 128), BF), ((128, 128), BF),
        ((256, 256), BF), ((256, 256), BF), ((2048, 256), BF),
        ((256, D), BF), ((8, D), F32), ((64, D), F32), ((64, D), BF),
        ((D, 256), F32), ((D, 256), F32), ((D, 128), F32), ((D, 512), BF),
        ((1, 512), F32), ((1, D), F32),
        ((32, 64, 256), F32), ((ROW, HID), BF), ((ROW, HID), F32),
        ((ROW, 128), F32), ((ROW, 128), F32),
        ((ROW, 128), BF), ((ROW, 128), BF), ((ROW, 128), BF),
        ((128, ROW), BF), ((128, ROW), BF), ((64, ROW), BF), ((ROW, 128), BF), ((64, ROW), BF),
        ((32, 64, HD), BF), ((32, 64, HD), F32), ((ROW, HD), BF),
        ((ROW, 512), BF), ((HD, ROW), F32), ((HD, ROW), F32),
        ((32, 64, 256), BF), ((ROW, 128), F32),
        ((ROW, D), BF), ((ROW, D), BF),
        ((1920, D), BF), ((1920, D), BF), ((64, D), BF), ((32, D), BF), ((16, D), F32), ((8, D), F32),
        ((256, 256), BF), ((128, 256), BF), ((D, 256), F32), ((D, 256), F32),
        ((320, D), F32), ((256, D), F32), ((256, D), F32),
        ((256, D), BF), ((64, D), F32), ((256, D), BF), ((64, D), F32),
        ((D, 256), BF), ((D, 256), BF), ((128, 256), F32), ((128, 256), F32),
        ((D, 256), BF), ((D, 256), BF), ((128, 256), F32), ((128, 256), F32),
        ((112, 128), F32), ((128, 128), F32), ((128, 128), F32), ((8, 128), F32), ((64, 128), F32),
    ]
    shapes = [pltpu.VMEM(shape, dtype) for shape, dtype in scratch]
    shapes += [
        pltpu.SMEM((32,), jnp.int32),
        pltpu.SemaphoreType.DMA((7,)),
        pltpu.SemaphoreType.DMA((3,)), pltpu.SemaphoreType.DMA((3, 17)),
        pltpu.SemaphoreType.DMA((2,)), pltpu.SemaphoreType.DMA((2, 21)),
        pltpu.SemaphoreType.DMA((5,)), pltpu.SemaphoreType.DMA((5,)),
        pltpu.SemaphoreType.DMA((11,)), pltpu.SemaphoreType.DMA((11,)),
    ]
    parts = pl.pallas_call(
        kernel,
        out_shape=(
            jax.ShapeDtypeStruct((TOK, D), BF),
            jax.ShapeDtypeStruct((TOK, D), BF),
            jax.ShapeDtypeStruct((128, 256), F32),
            jax.ShapeDtypeStruct((128, 256), F32),
            jax.ShapeDtypeStruct((32, D), F32),
            jax.ShapeDtypeStruct((8, D), F32),
            jax.ShapeDtypeStruct((8, 128), F32),
        ),
        in_specs=[vmem] * 7 + [smem] * 2,
        out_specs=(pl.BlockSpec(memory_space=pl.ANY),) * 7,
        scratch_shapes=shapes,
        compiler_params=pltpu.CompilerParams(
            collective_id=0, has_side_effects=True, vmem_limit_bytes=62 * 2**20
        ),
    )(x, dy, wq, wo, wu, wd, sp, order, lengths)
    return pl.pallas_call(
        finish,
        out_shape=(
            jax.ShapeDtypeStruct((TOK, D), BF),
            jax.ShapeDtypeStruct((TOK, D), BF),
            jax.ShapeDtypeStruct((1, PER), F32),
            jax.ShapeDtypeStruct((8, 3 * D), F32),
            jax.ShapeDtypeStruct((8, D), F32),
            jax.ShapeDtypeStruct((8, SEQ * HID), F32),
            jax.ShapeDtypeStruct((32, D), F32),
        ),
        in_specs=[vmem] * 7,
        out_specs=(vmem,) * 7,
    )(*parts)


def local(tokens, doc_lengths, block_order, small_params, w_qkv, w_out, w_up, w_down, cotangent):
    mixed, grad_tokens, grad_small, grad_qkv, grad_out, grad_up, grad_down = layer(
        tokens[0], cotangent[0], w_qkv, w_out, w_up, w_down,
        small_params.reshape(1, PER), block_order, doc_lengths,
    )
    return (
        mixed[None], grad_tokens[None], grad_small.reshape(PER), grad_qkv, grad_out, grad_up, grad_down,
    )


def solution(mesh):
    placed = (
        P("batch", "seq", None),
        P("batch", None),
        P(),
        P(("seq", "batch")),
        P(("seq", "batch"), None),
        P(("seq", "batch"), None),
        P(("seq", "batch"), None),
        P(("seq", "batch"), None),
        P("batch", "seq", None),
    )
    return jax.shard_map(
        local,
        mesh=mesh,
        in_specs=placed,
        out_specs=(
            P("batch", "seq", None),
            P("batch", "seq", None),
            P(("seq", "batch")),
            P(("seq", "batch"), None),
            P(("seq", "batch"), None),
            P(("seq", "batch"), None),
            P(("seq", "batch"), None),
        ),
        check_vma=False,
    )
```

```python
import jax
import jax.numpy as jnp
import numpy as np
from jax import lax
from jax.experimental import pallas as pl
from jax.experimental.pallas import tpu as pltpu
from jax.sharding import PartitionSpec as P

HD = 64
ROT = 16
EPS = 1e-05
NEG = -1e30
MESH = pl.DeviceIdType.MESH
BF = jnp.bfloat16
F32 = jnp.float32

SEQ = 16
BATCH = 8
TOK = 128
ROW = SEQ * TOK
D = 1024
HID = 256
PER = 104
QB = 256
AB = 512


def dot(a, b):
    return lax.dot_general(a, b, (((1,), (0,)), ((), ())), preferred_element_type=F32)


def dot_nt(a, b):
    return lax.dot_general(a, b, (((1,), (1,)), ((), ())), preferred_element_type=F32)


def dot_tn(a, b):
    return lax.dot_general(a, b, (((0,), (0,)), ((), ())), preferred_element_type=F32)


def iota(shape, dim):
    return lax.broadcasted_iota(jnp.int32, shape, dim)


def slot(z, x, c):
    return z * 8 + x * 2 + c


def rows_at(index, count):
    return pl.ds(pl.multiple_of(index * count, count), count)


def kernel(
    x_ref, dy_ref, wq_ref, wo_ref, wu_ref, wd_ref, sp_ref, order_ref, len_ref,
    mixed_out, gtok_out, gu_out, gq_out, gd_out, go_out, small_out,
    mixed_ref, gtok_ref, gd_ref, go_ref, small_ref, nrm, dya, ssend, sgot, sall, wsend, wst, wbuf, wd2, wos, wo2, wob, rawq, rawu, cols, wcat, brow, drow,
    prj, act, dge, tabc, tabs, qa, ka, va, kat, vat, qat, doa, doat, dost, osort, ost,
    dcat, dkt, dvt, dsort, dqs,
    part_m, part_d, land_m, land_d, gdpair, gdland, gopair, goland, gupair, guland, keptu, keptq,
    gdacc, gtq, gtu, gdsend, gosend, gdrecv, gorecv,
    gusend, gurecv, gusum, gufin, gqsend, gqrecv, gqsum, gqfin,
    flat, fsend, frecv, fsum, fall,
    inv_ref, out_ss, ag_ss, ag_rs, rs_ss, rs_rs, sq_ss, sq_rs, bt_ss, bt_rs,
):
    s = lax.axis_index("seq")
    b = lax.axis_index("batch")
    z, x, c = s // 8, lax.rem(s // 2, 4), lax.rem(s, 2)
    xr, xl, xo = lax.rem(x + 1, 4), lax.rem(x + 3, 4), lax.rem(x + 2, 4)
    zo, co = 1 - z, 1 - c
    y, w = b // 2, lax.rem(b, 2)
    yr, yl, yo, wo_ = lax.rem(y + 1, 4), lax.rem(y + 3, 4), lax.rem(y + 2, 4), 1 - w
    right, left = (slot(z, xr, c), b), (slot(z, xl, c), b)
    across, sibling = (slot(zo, x, c), b), (slot(z, x, co), b)

    def remote(src, dst, send, recv, device):
        return pltpu.make_async_remote_copy(
            src_ref=src, dst_ref=dst, send_sem=send, recv_sem=recv,
            device_id=device, device_id_type=MESH,
        )

    barrier = pltpu.get_barrier_semaphore()

    @pl.loop(1, SEQ)
    def _(j):
        pl.semaphore_signal(barrier, inc=1, device_id=(lax.rem(s + j, SEQ), b), device_id_type=MESH)

    @pl.loop(1, BATCH)
    def _(j):
        pl.semaphore_signal(barrier, inc=1, device_id=(s, lax.rem(b + j, BATCH)), device_id_type=MESH)

    def normed_of():
        inputs = x_ref[...].astype(F32)
        centred = inputs - jnp.mean(inputs, axis=-1, keepdims=True)
        inverse = lax.rsqrt(jnp.mean(centred * centred, axis=-1, keepdims=True) + EPS)
        return inputs, centred * inverse, inverse

    nrm[rows_at(s, TOK), :] = normed_of()[1].astype(BF)
    dya[rows_at(s, TOK), :] = dy_ref[...]

    def pair(one, two):
        return jnp.where(iota((8, 128), 1) < 64, one, two)

    small = jnp.concatenate([sp_ref[...].astype(F32), jnp.zeros((1, 128 - PER), F32)], axis=1)
    ssend[...] = jnp.broadcast_to(small, (16, 128)).astype(BF)
    wide_q = wq_ref[...].astype(F32)
    wide_u = wu_ref[...].astype(F32)
    for k in range(SEQ):
        at = slice(k // 2 * 128, k // 2 * 128 + 128)
        q, kk, v = (wide_q[:, n * D : n * D + D][:, at] for n in range(3))
        turned = [pltpu.roll(part_of, 64, 1) for part_of in (q, kk, v)]
        q, kk, v = (q, turned[1], v) if k % 2 == 0 else (turned[0], kk, turned[2])
        low = jnp.concatenate([pair(q, kk), pair(v, jnp.zeros_like(v))], axis=1)
        block = jnp.concatenate([wide_u[:, k * HID : k * HID + HID], low], axis=0)
        wsend[k * 16 : k * 16 + 16, :] = block.astype(BF)

    wst[rows_at(s, 16), :] = wsend[rows_at(s, 16), :]
    sgot[rows_at(s, 16), :] = ssend[...]
    wos[...] = wo_ref[...].astype(F32)
    wd2[rows_at(b, 32), :] = wd_ref[...]
    wo2[rows_at(b, 8), :] = wos[...]

    pl.semaphore_wait(barrier, SEQ - 1 + BATCH - 1)

    def seq_copy(j, k, src, dst):
        return remote(src, dst, sq_ss.at[k], sq_rs.at[k], (lax.rem(s + j, SEQ), b))

    def seq_all(k, ref, count):
        ref = ref.at[pl.ds(0, (SEQ - 1) * count)]
        return seq_copy(1, k, ref, ref)

    def column_copy(j, k, src, dst):
        return remote(src, dst, bt_ss.at[k], bt_rs.at[k], (s, lax.rem(y + j, 4) * 2 + w))

    def column_start(k, send, recv, count):
        @pl.loop(1, 4)
        def _(j):
            peer = lax.rem(y + j, 4)
            column_copy(j, k, send.at[rows_at(peer, 2 * count)], recv.at[rows_at(y, 2 * count)]).start()

    def column_all(k, ref, count):
        ref = ref.at[pl.ds(0, 6 * count)]
        return column_copy(1, k, ref, ref)

    def pair_copy(k, pair, land, count):
        src = pair.at[rows_at(wo_, count)]
        return remote(src, land, bt_ss.at[k], bt_rs.at[k], (s, y * 2 + wo_))

    def column_sums(k, recv, pair, land, count):
        column_all(k, recv, count).wait_recv()
        total = recv[0 : 2 * count, :].astype(F32)
        for n in range(1, 4):
            total = total + recv[2 * n * count : 2 * (n + 1) * count, :].astype(F32)
        pair[...] = total.astype(pair.dtype)
        pair_copy(k + 5, pair, land, count).start()

    def pair_sum(k, pair, land, count):
        pair_copy(k + 5, pair, land, count).wait_recv()
        return pair[rows_at(w, count), :].astype(F32) + land[...].astype(F32)

    def batch_all(k, ref, count):
        ref = ref.at[pl.ds(0, (BATCH - 1) * count)]
        return batch_copy(1, k, ref, ref)

    def batch_copy(j, k, src, dst):
        return remote(src, dst, bt_ss.at[k], bt_rs.at[k], (s, lax.rem(b + j, BATCH)))

    @pl.loop(1, SEQ)
    def _(j):
        peer = lax.rem(s + j, SEQ)
        seq_copy(j, 0, wsend.at[rows_at(peer, 16)], wst.at[rows_at(s, 16)]).start()

    class Gather:
        def __init__(self, buf, k, size, slots, right, left, across, sibling=None):
            self.buf, self.k, self.size = buf, k, size
            own, far, of_left, of_right, far_left, far_right, opposite, far_opposite = slots[0]
            half = size // 2
            self.sends = {
                0: (own, right, 0, size), 1: (own, left, 0, size), 2: (own, across, 0, size),
                4: (far, right, 0, size), 5: (far, left, 0, size),
                7: (of_left, right, 0, half), 8: (of_right, left, half, half),
                11: (far_left, right, 0, half), 12: (far_right, left, half, half),
            }
            self.receives = {
                0: (of_left, 0, size), 1: (of_right, 0, size), 2: (far, 0, size),
                4: (far_left, 0, size), 5: (far_right, 0, size),
                7: (opposite, 0, half), 8: (opposite, half, half),
                11: (far_opposite, 0, half), 12: (far_opposite, half, half),
            }
            if sibling is not None:
                for e, n in ((3, 0), (6, 1), (9, 2), (10, 3), (13, 4), (14, 5), (15, 6), (16, 7)):
                    self.sends[e] = (slots[0][n], sibling, 0, size)
                    self.receives[e] = (slots[1][n], 0, size)

        def copy(self, e, index, device, low, count):
            at = self.buf.at[pl.ds(pl.multiple_of(index * self.size + low, self.size // 2), count)]
            return remote(at, at, ag_ss.at[self.k], ag_rs.at[self.k, e], device)

        def start(self, *events):
            for e in events:
                if e in self.sends:
                    self.copy(e, self.sends[e][0], *self.sends[e][1:]).start()

        def wait(self, *events):
            for e in events:
                if e in self.receives:
                    index, low, count = self.receives[e]
                    self.copy(e, index, self.sends[e][1], low, count).wait_recv()

        def step(self, n):
            if n == 0:
                self.start(0, 1, 2, 3)
            elif n == 1:
                self.wait(0)
                self.start(7)
                self.wait(1)
                self.start(8)
                self.wait(2)
                self.start(4, 5, 6, 9, 10)
            elif n == 2:
                self.wait(4)
                self.start(11, 13)
                self.wait(5)
                self.start(12, 14)
            elif n == 3:
                self.wait(7, 8)
                self.start(15)
                self.wait(11, 12)
                self.start(16)
            else:
                self.wait(3, 6, 9, 10, 13, 14, 15, 16)

        def drain(self):
            sent = self.buf.at[pl.ds(0, sum(what[3] for what in self.sends.values()))]
            remote(sent, sent, ag_ss.at[self.k], ag_rs.at[self.k, 0], right).wait_send()

    def row_slots(core):
        return [slot(p, q, core) for p, q in ((z, x), (zo, x), (z, xl), (z, xr), (zo, xl), (zo, xr), (z, xo), (zo, xo))]

    rows_slots = [q * 2 + p for p, q in ((w, y), (wo_, y), (w, yl), (w, yr), (wo_, yl), (wo_, yr), (w, yo), (wo_, yo))]

    normed_gather = Gather(nrm, 0, TOK, (row_slots(c), row_slots(co)), right, left, across, sibling)
    dy_gather = Gather(dya, 1, TOK, (row_slots(c), row_slots(co)), right, left, across, sibling)
    weight_gather = Gather(
        wbuf, 2, 256, (rows_slots,), (s, yr * 2 + w), (s, yl * 2 + w), (s, y * 2 + wo_)
    )
    normed_gather.step(0)

    @pl.loop(0, 32)
    def _(i):
        place = jnp.int32(0)
        for j in range(32):
            place = place + jnp.where(order_ref[j] == i, j, 0)
        inv_ref[i] = jnp.minimum(place, 31)

    @pl.loop(1, SEQ)
    def _(j):
        seq_copy(j, 4, ssend, sgot.at[rows_at(s, 16)]).start()

    outputs = (
        (mixed_ref, mixed_out), (gtok_ref, gtok_out), (gufin, gu_out), (gqfin, gq_out),
        (gd_ref, gd_out), (go_ref, go_out), (small_ref, small_out),
    )

    def output(n):
        return pltpu.make_async_copy(*outputs[n], out_ss.at[n])

    ends = [len_ref[0, 0]]
    for k in range(1, 4):
        ends.append(ends[-1] + len_ref[0, k])

    def begin_of(where):
        begin = jnp.zeros_like(where)
        for end in ends:
            begin = jnp.maximum(begin, jnp.where(where >= end, end, 0))
        return begin

    def doc_of(where):
        doc = jnp.zeros_like(where)
        for end in ends:
            doc = doc + jnp.where(where >= end, 1, 0)
        return doc

    def partner_of(part):
        lane = lax.rem(iota(part.shape, 1), 64)
        return jnp.where(lane < ROT // 2, pltpu.roll(part, 120, 1), pltpu.roll(part, 8, 1))

    rate = jnp.zeros((1, 128), F32)
    for k in range(ROT // 2):
        value = float(np.float32(10000.0) ** np.float32(-2.0 * k / ROT))
        rate = jnp.where(lax.rem(iota((1, 128), 1), 8) == k, value, rate)

    @pl.loop(0, 8, unroll=2)
    def _(i):
        where = i * QB + iota((QB, 128), 0)
        angle = (where - begin_of(where)).astype(F32) * rate
        lane = lax.rem(iota((QB, 128), 1), 64)
        sine = jnp.sin(angle)
        tabc[rows_at(i, QB), :] = jnp.where(lane < ROT, jnp.cos(angle), 1.0)
        sine = jnp.where(lane < ROT // 2, -sine, sine)
        tabs[rows_at(i, QB), :] = jnp.where(lane < ROT, sine, 0.0)

    normed_gather.step(1)
    seq_all(0, wst, 16).wait_recv()
    seq_all(4, sgot, 16).wait_recv()

    wbuf[rows_at(b, 256), :] = wst[...]
    weight_gather.step(0)
    lines = [sgot[k * 16 : k * 16 + 16, :].astype(F32)[0:1, :] for k in range(SEQ)]
    sall[rows_at(b, 16), :] = jnp.concatenate(lines, axis=0).astype(BF)

    @pl.loop(1, BATCH)
    def _(j):
        batch_copy(j, 0, sall.at[rows_at(b, 16)], sall.at[rows_at(b, 16)]).start()

    weight_gather.step(1)
    dy_gather.start(2)

    batch_all(0, sall, 16).wait_recv()

    def hot_of(line, number):
        low = (lax.rem(line, 16) * BATCH + line // 16) * PER
        return ((low <= number) & (number < low + PER)).astype(F32).astype(BF)

    def place_of(number):
        owner = jnp.floor((number.astype(F32) + 0.5) * (1.0 / PER)).astype(jnp.int32)
        return number - PER * owner

    for k in range(4):
        number = k * D + iota((D, 1), 0)
        found = dot(hot_of(iota((1, 128), 1), number), sall[...])
        found = jnp.where(iota((D, 128), 1) == place_of(number), found, 0.0)
        cols[:, k : k + 1] = jnp.sum(found, axis=1, keepdims=True)

    def small_row(number):
        found = dot_tn(sall[...], hot_of(iota((128, 1), 0), number))
        found = jnp.where(iota((128, number.shape[1]), 0) == place_of(number), found, 0.0)
        return jnp.sum(found, axis=0, keepdims=True)

    lane = iota((1, 256), 1)
    number_q = 4 * D + (lane // 64) * D + s * 64 + lax.rem(lane, 64)
    bias_q = small_row(jnp.where(lane < 192, number_q, -1000))
    bias_u = small_row(8 * D + s * HID + lane)
    wide = iota((1, D), 1)
    drow[...] = small_row(7 * D + wide) + small_row(12 * D + wide)

    normed_gather.step(2)
    weight_gather.step(2)
    dy_gather.start(0, 1)
    normed_gather.wait(7, 8)
    normed_gather.start(15)
    weight_gather.step(3)
    normed_gather.wait(11, 12)
    normed_gather.start(16)

    @pl.loop(0, SEQ)
    def _(i):
        for j in range(BATCH):
            block = wbuf[pl.ds(pl.multiple_of(j * 256 + i * 16, 16), 16), :].astype(F32)
            at = pl.ds(pl.multiple_of(i * 64 + j * 8, 8), 8)
            rawu[at, :] = block[0:8, :]
            rawq[at, :] = block[8:16, :]

    row_q, row_u = bias_q, bias_u
    for i in range(8):
        at = slice(i * 128, i * 128 + 128)
        wq, wu = rawq[at, :], rawu[at, :]
        wcat[at, 0:256] = (wq * cols[at, 0:1]).astype(BF)
        wcat[at, 256:512] = (wu * cols[at, 2:3]).astype(BF)
        row_q = row_q + jnp.sum(wq * cols[at, 1:2], axis=0, keepdims=True)
        row_u = row_u + jnp.sum(wu * cols[at, 3:4], axis=0, keepdims=True)
    brow[:, 0:256] = row_q
    brow[:, 256:512] = row_u

    dy_gather.wait(2)
    dy_gather.start(4, 5, 3, 6)
    normed_gather.step(4)

    @pl.loop(0, 4, unroll=4)
    def _(i):
        out = dot(nrm[rows_at(i, 512), :], wcat[:, 0:256]) + brow[:, 0:256]
        prj[pl.ds(i * 8, 8)] = out.reshape(8, 64, 256)

    @pl.loop(1, BATCH)
    def _(j):
        batch_copy(j, 1, wd_ref, wd2.at[rows_at(b, 32)]).start()
        batch_copy(j, 2, wos, wo2.at[rows_at(b, 8)]).start()

    def pieces_of(value):
        high = value.astype(BF).astype(F32)
        mid = (value - high).astype(BF).astype(F32)
        return high, mid, value - high - mid

    def with_lanes(base, first, values):
        lane = iota(base.shape, 1)
        for k, value in enumerate(values):
            base = jnp.where(lane == first + k, value, base)
        return base

    def blocks_of(ref, order, i):
        return jnp.concatenate([ref[order[i * 4 + k]] for k in range(4)], axis=0)

    @pl.loop(0, 8, unroll=4)
    def _(i):
        at = rows_at(i, QB)
        come = blocks_of(prj, inv_ref, i)
        both = come[:, 0:128]
        both = both * tabc[at, :] + partner_of(both) * tabs[at, :]
        lane = iota((QB, 128), 1)
        own = doc_of(i * QB + iota((QB, 128), 0)) == lane - 64
        front = lane < 64
        query = jnp.where(front, both * 0.125, jnp.where(own | (lane >= 68), 0.0, NEG)).astype(BF)
        tail = jnp.where(lane < 68, own.astype(F32), (lane < 71).astype(F32))
        key = jnp.where(front, pltpu.roll(both, 64, 1), tail).astype(BF)
        value = jnp.where(front, come[:, 128:256], (lane < 67).astype(F32)).astype(BF)
        qa[at, :], ka[at, :], va[at, :] = query, key, value
        qat[:, at] = query.T[0:64, :]
        kat[:, at] = key.T
        vat[:, at] = value.T

    dy_gather.wait(0)
    dy_gather.start(7)
    dy_gather.wait(1)
    dy_gather.start(8)

    lower = iota((AB, AB), 1) <= iota((AB, AB), 0)

    def attend(i):
        at = rows_at(i, AB)

        def step(j, carry, masked):
            top, total = carry
            k_at = rows_at(j, AB)
            scores = dot(qa[at, :], kat[:, k_at])
            if masked:
                scores = jnp.where(lower, scores, NEG)
            peak = jnp.maximum(top, jnp.max(scores, axis=1, keepdims=True))
            expos = jnp.exp(scores - peak).astype(BF)
            return peak, total * jnp.exp(top - peak) + dot(expos, va[k_at, :])

        carry = (jnp.full((AB, 1), NEG, F32), jnp.zeros((AB, 128), F32))
        for j in range(i + 1):
            carry = step(j, carry, j == i)
        top, total = carry
        norm = total[:, 64:65]
        osort[pl.ds(i * (AB // 64), AB // 64)] = (total / norm)[:, 0:64].reshape(AB // 64, 64, HD)
        qa[at, :] = with_lanes(qa[at, :].astype(F32), 68, pieces_of(-(top + jnp.log(norm)))).astype(BF)

    for i in range(3):
        attend(i)
    dy_gather.wait(4)
    dy_gather.start(11)
    dy_gather.wait(5)
    dy_gather.start(12, 9, 10, 13, 14)
    attend(3)

    @pl.loop(0, 4, unroll=4)
    def _(i):
        at = rows_at(i, 512)
        hidden = dot(nrm[at, :], wcat[:, 256:512]) + brow[:, 256:512]
        share = 0.5 * (1.0 + lax.erf(hidden * (2.0**-0.5)))
        act[at, :] = (hidden * share).astype(BF)
        dge[at, :] = share + hidden * jnp.exp(-0.5 * hidden * hidden) * ((2.0 * np.pi) ** -0.5)

    dy_gather.wait(7, 8)
    dy_gather.start(15)

    @pl.loop(0, 8)
    def _(j):
        ost[rows_at(j, QB), :] = blocks_of(osort, order_ref, j).astype(BF)

    batch_all(1, wd2, 32).wait_recv()
    batch_all(2, wo2, 8).wait_recv()

    wob[...] = wo2[...].astype(BF)

    class Scatter:
        def __init__(self, part, land, k):
            self.part, self.land, self.k = part, land, k
            self.order = [(zo, xo), (zo, xr), (zo, xl), (zo, x), (z, xo), (z, xr), (z, xl), (z, x)]
            table = [(n, co, 0, TOK, sibling, None) for n in range(8)]
            for g in (0, 4):
                table += [
                    (g, c, 0, 64, left, g + 2), (g, c, 64, 64, right, g + 1),
                    (g + 1, c, 0, 64, right, g + 3), (g + 2, c, 64, 64, left, g + 3),
                    (g + 1, c, 64, 64, right, g + 3), (g + 2, c, 0, 64, left, g + 3),
                ]
            table += [(3, c, 0, TOK, across, 7)]
            self.table, self.begin, at = table, [], 0
            for entry in table:
                self.begin.append(at)
                at += entry[3]

        def at(self, n, core, low, count):
            zz, xx = self.order[n]
            return pl.ds(pl.multiple_of(slot(zz, xx, core) * TOK + low, 16), count)

        def copy(self, e, src, dst, device):
            return remote(src, dst, rs_ss.at[self.k], rs_rs.at[self.k, e], device)

        def out(self, e):
            n, core, low, count, device, _ = self.table[e]
            return self.part.at[self.at(n, core, low, count)], self.land.at[pl.ds(self.begin[e], count)], device

        def start(self, *events):
            for e in events:
                self.copy(e, *self.out(e)).start()

        def wait(self, e):
            src, dst, device = self.out(e)
            self.copy(e, dst, dst, device).wait_recv()

        def landed(self, e):
            self.wait(e)
            return self.land[self.begin[e] : self.begin[e] + self.table[e][3], :].astype(F32)

        def add(self, *events):
            for e in events:
                n, core, low, count, _, to = self.table[e]
                to = e if e < 8 else to
                at = self.at(to, c, low, count)
                self.part[at, :] = (self.part[at, :].astype(F32) + self.landed(e)).astype(BF)

        def step(self, n):
            if n == 0 or n == 1:
                self.add(4 * n)
                self.start(8 + 6 * n, 9 + 6 * n)
            elif n == 2 or n == 3:
                g = n - 2
                self.add(4 * g + 1, 4 * g + 2)
                self.start(10 + 6 * g, 11 + 6 * g)
                self.add(4 * g + 3)
            elif n == 4 or n == 5:
                g = n - 4
                self.add(8 + 6 * g, 9 + 6 * g)
                self.start(12 + 6 * g, 13 + 6 * g)
            else:
                self.add(10, 11, 12, 13)
                self.start(20)

        def result(self):
            total = self.part[self.at(7, c, 0, TOK), :].astype(F32)
            low = total[0:64, :] + self.landed(16) + self.landed(19)
            high = total[64:TOK, :] + self.landed(17) + self.landed(18)
            return jnp.concatenate([low, high], axis=0) + self.landed(20)

        def drain(self):
            sent = self.part.at[pl.ds(0, sum(entry[3] for entry in self.table))]
            self.copy(0, sent, sent, sibling).wait_send()

    mixed_sum = Scatter(part_m, land_m, 0)
    dn_sum = Scatter(part_d, land_d, 1)

    def halves_of(which):
        return [(which, xo // 2), (which, 1 - xo // 2)]

    for k, (which, side) in enumerate(halves_of(zo) + halves_of(z)):
        at = rows_at(which * 2 + side, 512)
        part_m[at, :] = (dot(act[at, :], wd2[...]) + dot(ost[at, :], wob[...])).astype(BF)
        if k == 0:
            mixed_sum.start(0)
        elif k == 1:
            mixed_sum.start(1, 2, 3)
            dy_gather.wait(11, 12)
            dy_gather.start(16)
    mixed_sum.step(0)
    mixed_sum.start(4, 5, 6, 7)

    dy_gather.step(4)

    @pl.loop(0, 4, unroll=4)
    def _(i):
        at = rows_at(i, 512)
        dy = dya[at, :]
        dcat[at, 256:512] = (dot_nt(dy, wd2[...]) * dge[at, :]).astype(BF)
        dost[pl.ds(i * 8, 8)] = dot_nt(dy, wob[...]).astype(BF).reshape(8, 64, HD)

    mixed_sum.step(2)

    gdacc[...] = jnp.zeros_like(gdacc)

    @pl.loop(0, 2, unroll=2)
    def _(i):
        at = rows_at(i, 1024)
        gdacc[0:256, :] += dot_tn(act[at, :], dya[at, :])
        gdacc[256:320, :] += dot_tn(ost[at, :], dya[at, :])

    gdsend[...] = gdacc[0:256, :].astype(BF)
    gosend[...] = gdacc[256:320, :]
    gdrecv[rows_at(y, 64), :] = gdsend[rows_at(y, 64), :]
    gorecv[rows_at(y, 16), :] = gosend[rows_at(y, 16), :]
    column_start(3, gdsend, gdrecv, 32)
    column_start(4, gosend, gorecv, 8)

    mixed_sum.step(4)
    mixed_sum.step(1)
    mixed_sum.step(3)

    def column_sum(low):
        def add(i, total):
            return total + jnp.sum(dcat[rows_at(i, QB), low : low + 256].astype(F32), axis=0, keepdims=True)

        return lax.fori_loop(0, 8, add, jnp.zeros((1, 256), F32))

    def to_flat(line, values):
        for k in range(values.shape[1] // 128):
            flat[line + k : line + k + 1, :] = values[:, k * 128 : k * 128 + 128]

    def hand_out(gt, kept, sums, k, send):
        for i in range(4):
            at = slice(i * 256, i * 256 + 256)
            grad = gt[0:256, at].T
            kept[at, :] = grad
            grad = grad * cols[at, k : k + 1] + cols[at, k + 1 : k + 2] * sums
            for m in range(8):
                for h in range(2):
                    place = m * 128 + i * 32 + h * 16
                    first, second = (h * 2) * 64 + m * 8, (h * 2 + 1) * 64 + m * 8
                    send[place : place + 16, :] = jnp.concatenate(
                        [grad[first : first + 8, :], grad[second : second + 8, :]], axis=0
                    ).astype(BF)

    def small_sums(kept, raw, sums, k):
        for i in range(4):
            at = slice(i * 256, i * 256 + 256)
            gain = jnp.sum(kept[at, :] * raw[at, :], axis=1, keepdims=True)
            shift = jnp.sum(sums * raw[at, :], axis=1, keepdims=True)
            lane = iota((256, 128), 1)
            spread = jnp.where(lane == 0, gain, jnp.where(lane == 1, shift, 0.0)).T
            to_flat(k * 8 + i * 2, spread[0:1, :])
            to_flat(k * 8 + 8 + i * 2, spread[1:2, :])

    def to_owners(total, total_ref, final, k):
        total_ref[...] = total
        final[rows_at(s, 8), :] = total_ref[rows_at(s, 8), :]

        @pl.loop(1, SEQ)
        def _(j):
            peer = lax.rem(s + j, SEQ)
            seq_copy(j, k, total_ref.at[rows_at(peer, 8)], final.at[rows_at(s, 8)]).start()

    gtu[...] = jnp.zeros_like(gtu)

    @pl.loop(0, 2, unroll=2)
    def _(i):
        at = rows_at(i, 1024)
        gtu[...] += dot_tn(dcat[at, 256:512], nrm[at, :])

    sum_u = column_sum(256)
    hand_out(gtu, keptu, sum_u, 2, gusend)
    gurecv[rows_at(y, 256), :] = gusend[rows_at(y, 256), :]
    column_start(5, gusend, gurecv, 128)


    @pl.loop(0, 8, unroll=4)
    def _(i):
        at = rows_at(i, QB)
        grads = blocks_of(dost, inv_ref, i).astype(F32)
        past = osort[pl.ds(i * 4, 4)].reshape(QB, HD)
        delta = jnp.sum(grads * past, axis=1, keepdims=True)
        wide = jnp.concatenate([grads, jnp.zeros((QB, 64), F32)], axis=1)
        wide = with_lanes(wide, 64, pieces_of(-delta)).astype(BF)
        doa[at, :] = wide
        doat[:, at] = wide.T[0:64, :]

    dkt[...] = jnp.zeros_like(dkt)
    dvt[...] = jnp.zeros_like(dvt)

    def attend_back(q_at, k_at, masked):
        probs = jnp.exp(dot(qa[q_at, :], kat[:, k_at]))
        if masked:
            probs = jnp.where(lower, probs, 0.0)
        grads = (probs * dot(doa[q_at, :], vat[:, k_at])).astype(BF)
        dkt[:, k_at] += dot(qat[:, q_at], grads)
        dvt[:, k_at] += dot(doat[:, q_at], probs.astype(BF))
        dqs[q_at, :] += dot(grads, ka[k_at, :])

    dqs[...] = jnp.zeros_like(dqs)
    for i in range(ROW // AB):
        attend_back(slice(i * AB, i * AB + AB), slice(i * AB, i * AB + AB), True)
        if i < ROW // AB - 1:
            for k in range(i * AB, i * AB + AB, 256):
                attend_back(slice(i * AB + AB, ROW), slice(k, k + 256), False)

    mixed_sum.step(6)
    mixed_sum.step(5)

    @pl.loop(0, 8, unroll=4)
    def _(i):
        at = rows_at(i, QB)
        both = jnp.concatenate([dqs[at, 0:64] * 0.125, dkt[:, at].T], axis=1)
        both = both * tabc[at, :] - partner_of(both) * tabs[at, :]
        last = jnp.concatenate([dvt[:, at].T, jnp.zeros((QB, 64), F32)], axis=1)
        whole = jnp.concatenate([both, last], axis=1).astype(BF)
        dsort[pl.ds(i * 4, 4)] = whole.reshape(4, 64, 256)

    @pl.loop(0, 8)
    def _(j):
        dcat[rows_at(j, QB), 0:256] = blocks_of(dsort, order_ref, j)

    def dn_part(which, side):
        at = rows_at(which * 2 + side, 512)
        part_d[at, :] = dot_nt(dcat[at, :], wcat[...]).astype(BF)

    dn_part(*halves_of(zo)[0])
    dn_sum.start(0)
    dn_part(*halves_of(zo)[1])
    dn_sum.start(1, 2, 3)
    dn_sum.step(0)
    gtq[...] = jnp.zeros_like(gtq)

    @pl.loop(0, 2, unroll=2)
    def _(i):
        at = rows_at(i, 1024)
        gtq[...] += dot_tn(dcat[at, 0:256], nrm[at, :])

    dn_sum.step(2)
    sum_q = column_sum(0)
    hand_out(gtq, keptq, sum_q, 0, gqsend)
    gqrecv[rows_at(b, 128), :] = gqsend[rows_at(b, 128), :]

    @pl.loop(1, BATCH)
    def _(j):
        peer = lax.rem(b + j, BATCH)
        batch_copy(j, 6, gqsend.at[rows_at(peer, 128)], gqrecv.at[rows_at(b, 128)]).start()

    column_sums(5, gurecv, gupair, guland, 128)
    dn_sum.step(4)
    for which, side in halves_of(z):
        dn_part(which, side)
    dn_sum.start(4, 5, 6, 7)
    small_sums(keptu, rawu, sum_u, 2)
    small_sums(keptq, rawq, sum_q, 0)

    def low_half(part_of):
        return jnp.concatenate([part_of[:, 0:64], jnp.zeros((1, 64), F32)], axis=1)

    flat[32:56, :] = jnp.zeros((24, 128), F32)
    flat[64:96, :] = jnp.zeros((32, 128), F32)
    flat[104:112, :] = jnp.zeros((8, 128), F32)
    upper = lax.rem(s, 2) == 1
    spans = (sum_q[:, 0:128], pltpu.roll(sum_q[:, 0:128], 64, 1), sum_q[:, 128:256])
    for k in range(3):
        mine = low_half(spans[k])
        mine = jnp.where(upper, pltpu.roll(mine, 64, 1), mine)
        flat[pl.ds(32 + k * 8 + s // 2, 1), :] = mine
    flat[pl.ds(64 + 2 * s, 1), :] = sum_u[:, 0:128]
    flat[pl.ds(65 + 2 * s, 1), :] = sum_u[:, 128:256]
    dy_total = jnp.sum(dy_ref[...].astype(F32), axis=0, keepdims=True)
    to_flat(56, dy_total)
    to_flat(96, dy_total)
    for k in range(SEQ):
        fsend[k * 8 : k * 8 + 8, :] = flat[13 * k // 2 : 13 * k // 2 + 8, :]
    frecv[rows_at(s, 8), :] = fsend[rows_at(s, 8), :]

    @pl.loop(1, SEQ)
    def _(j):
        peer = lax.rem(s + j, SEQ)
        seq_copy(j, 3, fsend.at[rows_at(peer, 8)], frecv.at[rows_at(s, 8)]).start()

    column_sums(3, gdrecv, gdpair, gdland, 32)
    column_sums(4, gorecv, gopair, goland, 8)
    dn_sum.step(1)
    dn_sum.step(6)
    dn_sum.step(3)
    to_owners(pair_sum(5, gupair, guland, 128), gusum, gufin, 1)
    batch_all(6, gqrecv, 128).wait_recv()
    total = gqrecv[0:128, :].astype(F32)
    for k in range(1, BATCH):
        total = total + gqrecv[k * 128 : k * 128 + 128, :].astype(F32)
    to_owners(total, gqsum, gqfin, 2)
    dn_sum.step(5)
    mixed_ref[...] = (mixed_sum.result() + x_ref[...].astype(F32) + drow[...]).astype(BF)
    output(0).start()

    seq_all(3, frecv, 8).wait_recv()

    total = frecv[0:8, :]
    for k in range(1, SEQ):
        total = total + frecv[k * 8 : k * 8 + 8, :]
    fsum[...] = total
    fall[rows_at(b, 8), :] = total

    @pl.loop(1, BATCH)
    def _(j):
        batch_copy(j, 7, fsum, fall.at[rows_at(b, 8)]).start()

    gd_ref[...] = pair_sum(3, gdpair, gdland, 32)
    go_ref[...] = pair_sum(4, gopair, goland, 8)
    output(4).start()
    output(5).start()

    merged = dn_sum.result()
    _, normed, inverse = normed_of()
    grad_norm = inverse * (
        merged
        - jnp.mean(merged, axis=-1, keepdims=True)
        - normed * jnp.mean(merged * normed, axis=-1, keepdims=True)
    )
    gtok_ref[...] = (dy_ref[...].astype(F32) + grad_norm).astype(BF)
    output(1).start()

    seq_all(1, gufin, 8).wait_recv()
    seq_all(2, gqfin, 8).wait_recv()

    batch_all(7, fall, 8).wait_recv()

    output(2).start()
    output(3).start()
    total = fall[0:8, :]
    for k in range(1, BATCH):
        total = total + fall[k * 8 : k * 8 + 8, :]
    small_ref[...] = total
    output(6).start()

    normed_gather.drain()
    dy_gather.drain()
    weight_gather.drain()
    mixed_sum.drain()
    dn_sum.drain()

    for k, ref, count in ((0, wst, 16), (1, gufin, 8), (2, gqfin, 8), (3, frecv, 8), (4, sgot, 16)):
        seq_all(k, ref, count).wait_send()
    for k, ref, count in (
        (0, sall, 16), (1, wd2, 32), (2, wo2, 8), (6, gqrecv, 128), (7, fall, 8),
    ):
        batch_all(k, ref, count).wait_send()
    for k, ref, pair, land, count in (
        (3, gdrecv, gdpair, gdland, 32), (4, gorecv, gopair, goland, 8), (5, gurecv, gupair, guland, 128),
    ):
        column_all(k, ref, count).wait_send()
        pair_copy(k + 5, pair, land, count).wait_send()

    for n in range(7):
        output(n).wait()


def finish(
    mixed_ref, gtok_ref, gu_ref, gq_ref, gd_ref, go_ref, small_ref,
    mixed_out, gtok_out, small_out, qkv_out, out_out, up_out, down_out,
):
    s = lax.axis_index("seq")
    b = lax.axis_index("batch")
    mixed_out[...] = mixed_ref[...]
    gtok_out[...] = gtok_ref[...]
    out_out[...] = go_ref[...]
    down_out[...] = gd_ref[...]
    low = iota((8, 128), 1) < 64
    for k in range(SEQ):
        up_out[:, k * HID : k * HID + HID] = gu_ref[k * 8 : k * 8 + 8, :]
    for k in range(0, SEQ, 2):
        one, two = (gq_ref[n * 8 : n * 8 + 8, 0:128] for n in (k, k + 1))
        one_v, two_v = (gq_ref[n * 8 : n * 8 + 8, 128:256] for n in (k, k + 1))
        at = k * HD
        qkv_out[:, at : at + 128] = jnp.where(low, one, pltpu.roll(two, 64, 1))
        qkv_out[:, D + at : D + at + 128] = jnp.where(low, pltpu.roll(one, 64, 1), two)
        qkv_out[:, 2 * D + at : 2 * D + at + 128] = jnp.where(low, one_v, pltpu.roll(two_v, 64, 1))
    begin = b * PER + lax.rem(s, 2) * 64
    line = begin // 128
    both = jnp.concatenate([small_ref[pl.ds(line, 1), :], small_ref[pl.ds(line + 1, 1), :]], axis=1)
    both = pltpu.roll(jnp.broadcast_to(both, (8, 256)), 256 - lax.rem(begin, 128), 1)
    small_out[...] = both[0:1, 0:PER]


def layer(x, dy, wq, wo, wu, wd, sp, order, lengths):
    vmem = pl.BlockSpec(memory_space=pltpu.VMEM)
    smem = pl.BlockSpec(memory_space=pltpu.SMEM)
    scratch = [
        ((TOK, D), BF), ((TOK, D), BF), ((32, D), F32), ((8, D), F32), ((8, 128), F32),
        ((ROW, D), BF), ((ROW, D), BF), ((16, 128), BF), ((256, 128), BF), ((128, 128), BF),
        ((256, 256), BF), ((256, 256), BF), ((2048, 256), BF),
        ((256, D), BF), ((8, D), F32), ((64, D), F32), ((64, D), BF),
        ((D, 256), F32), ((D, 256), F32), ((D, 128), F32), ((D, 512), BF),
        ((1, 512), F32), ((1, D), F32),
        ((32, 64, 256), F32), ((ROW, HID), BF), ((ROW, HID), F32),
        ((ROW, 128), F32), ((ROW, 128), F32),
        ((ROW, 128), BF), ((ROW, 128), BF), ((ROW, 128), BF),
        ((128, ROW), BF), ((128, ROW), BF), ((64, ROW), BF), ((ROW, 128), BF), ((64, ROW), BF),
        ((32, 64, HD), BF), ((32, 64, HD), F32), ((ROW, HD), BF),
        ((ROW, 512), BF), ((HD, ROW), F32), ((HD, ROW), F32),
        ((32, 64, 256), BF), ((ROW, 128), F32),
        ((ROW, D), BF), ((ROW, D), BF),
        ((1920, D), BF), ((1920, D), BF), ((64, D), BF), ((32, D), BF), ((16, D), F32), ((8, D), F32),
        ((256, 256), BF), ((128, 256), BF), ((D, 256), F32), ((D, 256), F32),
        ((320, D), F32), ((256, D), F32), ((256, D), F32),
        ((256, D), BF), ((64, D), F32), ((256, D), BF), ((64, D), F32),
        ((D, 256), BF), ((D, 256), BF), ((128, 256), F32), ((128, 256), F32),
        ((D, 256), BF), ((D, 256), BF), ((128, 256), F32), ((128, 256), F32),
        ((112, 128), F32), ((128, 128), F32), ((128, 128), F32), ((8, 128), F32), ((64, 128), F32),
    ]
    shapes = [pltpu.VMEM(shape, dtype) for shape, dtype in scratch]
    shapes += [
        pltpu.SMEM((32,), jnp.int32),
        pltpu.SemaphoreType.DMA((7,)),
        pltpu.SemaphoreType.DMA((3,)), pltpu.SemaphoreType.DMA((3, 17)),
        pltpu.SemaphoreType.DMA((2,)), pltpu.SemaphoreType.DMA((2, 21)),
        pltpu.SemaphoreType.DMA((5,)), pltpu.SemaphoreType.DMA((5,)),
        pltpu.SemaphoreType.DMA((11,)), pltpu.SemaphoreType.DMA((11,)),
    ]
    parts = pl.pallas_call(
        kernel,
        out_shape=(
            jax.ShapeDtypeStruct((TOK, D), BF),
            jax.ShapeDtypeStruct((TOK, D), BF),
            jax.ShapeDtypeStruct((128, 256), F32),
            jax.ShapeDtypeStruct((128, 256), F32),
            jax.ShapeDtypeStruct((32, D), F32),
            jax.ShapeDtypeStruct((8, D), F32),
            jax.ShapeDtypeStruct((8, 128), F32),
        ),
        in_specs=[vmem] * 7 + [smem] * 2,
        out_specs=(pl.BlockSpec(memory_space=pl.ANY),) * 7,
        scratch_shapes=shapes,
        compiler_params=pltpu.CompilerParams(
            collective_id=0, has_side_effects=True, vmem_limit_bytes=62 * 2**20
        ),
    )(x, dy, wq, wo, wu, wd, sp, order, lengths)
    return pl.pallas_call(
        finish,
        out_shape=(
            jax.ShapeDtypeStruct((TOK, D), BF),
            jax.ShapeDtypeStruct((TOK, D), BF),
            jax.ShapeDtypeStruct((1, PER), F32),
            jax.ShapeDtypeStruct((8, 3 * D), F32),
            jax.ShapeDtypeStruct((8, D), F32),
            jax.ShapeDtypeStruct((8, SEQ * HID), F32),
            jax.ShapeDtypeStruct((32, D), F32),
        ),
        in_specs=[vmem] * 7,
        out_specs=(vmem,) * 7,
    )(*parts)


def local(tokens, doc_lengths, block_order, small_params, w_qkv, w_out, w_up, w_down, cotangent):
    mixed, grad_tokens, grad_small, grad_qkv, grad_out, grad_up, grad_down = layer(
        tokens[0], cotangent[0], w_qkv, w_out, w_up, w_down,
        small_params.reshape(1, PER), block_order, doc_lengths,
    )
    return (
        mixed[None], grad_tokens[None], grad_small.reshape(PER), grad_qkv, grad_out, grad_up, grad_down,
    )


def solution(mesh):
    placed = (
        P("batch", "seq", None),
        P("batch", None),
        P(),
        P(("seq", "batch")),
        P(("seq", "batch"), None),
        P(("seq", "batch"), None),
        P(("seq", "batch"), None),
        P(("seq", "batch"), None),
        P("batch", "seq", None),
    )
    return jax.shard_map(
        local,
        mesh=mesh,
        in_specs=placed,
        out_specs=(
            P("batch", "seq", None),
            P("batch", "seq", None),
            P(("seq", "batch")),
            P(("seq", "batch"), None),
            P(("seq", "batch"), None),
            P(("seq", "batch"), None),
            P(("seq", "batch"), None),
        ),
        check_vma=False,
    )
```
